512 devices in a mesh: ctx: 64 (over y, x, core), tp: 8 (over z).
Axes of the slice: x: 4, y: 8, z: 8, core: 2. Of those that a mesh axis runs over, the one named last changes fastest.
Arguments:
- queries: bfloat16 [4096, 4096], P('ctx', 'tp'), may hold values from -256 to 256
- key_vectors: bfloat16 [4096, 1024], P('ctx', 'tp'), may hold values from -6 to 6
- value_vectors: bfloat16 [4096, 1024], P('ctx', 'tp'), may hold values from -6 to 6
- out_weight: bfloat16 [4096, 4096], P('tp'), may hold values from -0.09375 to 0.09375
- router_logit: float32 [4096], P('ctx'), may hold values from -8 to 8
- chosen_index: int32 [4096], P('ctx'), may hold values from 0 to 511, as said below
- chosen_count: int32 [64], P('ctx'), may hold values from 1 to 64, as said below
- out_cotangent: bfloat16 [4096, 4096], P('ctx', 'tp'), may hold values from -6 to 6
- hidden_state: bfloat16 [32768, 4096], P('ctx', 'tp'), may hold values from -4 to 4
Outputs:
- update: bfloat16 [4096, 4096], P('ctx', 'tp')
- grad_queries: bfloat16 [4096, 4096], P('ctx', 'tp')
- grad_keys: bfloat16 [4096, 1024], P('ctx', 'tp')
- grad_values: bfloat16 [4096, 1024], P('ctx', 'tp')
- grad_logit: float32 [4096], P('ctx')
- hidden_after: bfloat16 [32768, 4096], P('ctx', 'tp')
The draws below stay inside these ranges and needn't reach their ends.
Inputs may be any that keep to these rules, and one draw needn't show every extreme that they name: `chosen_index`: in each shard's block of 64 slots, the first chosen_count entries are strictly increasing token indices; the remaining entries are 511. `chosen_count`: some shard has all 64 slots filled.
All inputs are finite; a program needn't handle non-finite values.
Results may differ from the reference program's by a relative error of at most 0.015.
Values may be sent and summed in bfloat16 or wider, within the bound.
No kernel may reach another device: no remote copies, remote signals or barrier semaphores. Data moves between devices by JAX's collectives and lax.ppermute only.
A program may use at most 128 MiB of HBM per device.

```python
import math
import jax
import jax.numpy as jnp
from jax import lax

D = 4096
HEADS = 32
KV_HEADS = 8
HD = 128
TOK_DEV = 512
CAP = 64
SLOTS = 4096
TOKENS = 32768
N_CTX = 64


def shard_counts(key):
    count_key = jax.random.fold_in(key, 101)
    shard_total = SLOTS // CAP
    first_key, second_key, pick_key = jax.random.split(count_key, 3)
    first_draw = jax.random.randint(first_key, (shard_total,), 1, CAP + 1)
    second_draw = jax.random.randint(second_key, (shard_total,), 1, CAP + 1)
    fullest = jax.random.randint(pick_key, (), 0, shard_total)
    counted = jnp.maximum(first_draw, second_draw)
    return jnp.where(jnp.arange(shard_total) == fullest, CAP, counted).astype(jnp.int32)


def shared_keys(key):
    key_draw = jax.random.fold_in(key, 202)
    normal_key = jax.random.fold_in(key_draw, 0)
    normal_part = jax.random.truncated_normal(normal_key, -6.0, 6.0, (SLOTS, KV_HEADS * HD), jnp.float32)
    return normal_part


def draw_chosen_count(key, part):
    return shard_counts(key)


def draw_chosen_index(key, part):
    counted = shard_counts(key)
    key = jax.random.fold_in(key, 3)
    shard_total = SLOTS // CAP
    shard_keys = jax.random.split(key, shard_total)
    orders = jax.vmap(lambda single_key: jax.random.permutation(single_key, TOK_DEV))(shard_keys)[:, :CAP]
    slot_ids = jnp.arange(CAP)
    live_slot = slot_ids[None, :] < counted[:, None]
    masked = jnp.where(live_slot, orders, 2 * TOK_DEV)
    ordered = jnp.sort(masked, axis=1)
    filled = jnp.where(live_slot, ordered, TOK_DEV - 1)
    return filled.reshape(SLOTS).astype(jnp.int32)


def draw_key_vectors(key, part):
    return shared_keys(key).astype(jnp.bfloat16)


def draw_queries(key, part):
    key = jax.random.fold_in(key, 11)
    drawn = 2.0 * jax.random.truncated_normal(key, -6.0, 6.0, (SLOTS, HEADS * HD), jnp.float32)
    return drawn.astype(jnp.bfloat16)


def levels(key, dims, cuts, smallest, high):
    def one(axis_at, shards_of):
        heights = jax.random.uniform(jax.random.fold_in(jax.random.fold_in(key, 6), axis_at), (shards_of,), jnp.float32, smallest / len(cuts), high / len(cuts))
        return jnp.repeat(jnp.exp(heights), dims[axis_at] // shards_of).reshape((-1,) + (1,) * (len(dims) - axis_at - 1))

    factor_of = one(*cuts[0])
    for cut in cuts[1:]:
        factor_of = factor_of * one(*cut)
    return factor_of


def noise(stream_key, dims, scale, reach, cuts=(), kind=jnp.bfloat16):
    result = scale * jax.random.normal(stream_key, dims, jnp.float32)
    if cuts:
        result = result * levels(stream_key, dims, cuts, -0.22, 0.18)
    return jnp.clip(result, -reach, reach).astype(kind)


def setup_inputs(seed: int = 0) -> dict:
    splits = jax.random.split(jax.random.key(seed), 10)
    queries = draw_queries(jax.random.fold_in(splits[9], 71), 0)
    key_vectors = draw_key_vectors(jax.random.fold_in(splits[9], 71), 0)
    value_vectors = noise(splits[2], (SLOTS, KV_HEADS * HD), 1.0, 6.0, ((0, 64), (1, 8)))
    out_weight = noise(splits[3], (HEADS * HD, D), (HEADS * HD) ** -0.5, 0.09375, ((0, 8),))
    router_logit = noise(splits[4], (SLOTS,), 2.0, 8.0, ((0, 64),), jnp.float32)
    chosen_index = draw_chosen_index(jax.random.fold_in(splits[9], 71), 0)
    chosen_count = draw_chosen_count(jax.random.fold_in(splits[9], 71), 0)
    out_cotangent = noise(splits[7], (SLOTS, D), 1.0, 6.0, ((0, 64), (1, 8)))
    hidden_state = noise(splits[8], (TOKENS, D), 0.25, 4.0, ((0, 64), (1, 8)))
    return {"queries": queries, "key_vectors": key_vectors, "value_vectors": value_vectors, "out_weight": out_weight, "router_logit": router_logit, "chosen_index": chosen_index, "chosen_count": chosen_count, "out_cotangent": out_cotangent, "hidden_state": hidden_state}


ROTARY_BASE = 500000.0

def to_bf16(values_in):
    return lax.optimization_barrier(values_in.astype(jnp.bfloat16))

def rotate(field_in, position, sign_value):
    row_count = field_in.shape[0]
    row_width = field_in.shape[1]
    head_count = row_width // HD
    half_width = HD // 2
    frequency = ROTARY_BASE ** (-(jnp.arange(half_width, dtype=jnp.float32) * 2.0 / HD))
    angles = position.astype(jnp.float32)[:, None] * frequency[None, :]
    cos_part = jnp.cos(angles)[:, None, :]
    sin_part = sign_value * jnp.sin(angles)[:, None, :]
    shaped = field_in.astype(jnp.float32).reshape(row_count, head_count, HD)
    first_half = shaped[:, :, :half_width]
    second_half = shaped[:, :, half_width:]
    turned = jnp.concatenate([first_half * cos_part - second_half * sin_part, second_half * cos_part + first_half * sin_part], axis=2)
    return turned.reshape(row_count, row_width)

def reference(queries, key_vectors, value_vectors, out_weight, router_logit, chosen_index, chosen_count, out_cotangent, hidden_state):
    slot_count = queries.shape[0]
    slot_ids = jnp.arange(slot_count, dtype=jnp.int32)
    shard_ids = slot_ids // CAP
    position = (shard_ids * TOK_DEV + chosen_index).astype(jnp.int32)
    live_slot = slot_ids % CAP < chosen_count[shard_ids]
    key_position = jnp.where(live_slot, position, TOK_DEV * N_CTX).astype(jnp.int32)
    score_scale = 1.0 / math.sqrt(HD)
    group_size = HEADS // KV_HEADS
    turned_queries = to_bf16(rotate(queries, position, 1.0))
    turned_keys = to_bf16(rotate(key_vectors, position, 1.0))
    allowed = key_position[None, :] <= position[:, None]
    head_ids = jnp.arange(HEADS, dtype=jnp.int32)

    def head_scores(head_index):
        query_head = lax.dynamic_slice_in_dim(turned_queries, head_index * HD, HD, 1).astype(jnp.float32)
        key_head = lax.dynamic_slice_in_dim(turned_keys, head_index // group_size * HD, HD, 1).astype(jnp.float32)
        value_head = lax.dynamic_slice_in_dim(value_vectors, head_index // group_size * HD, HD, 1).astype(jnp.float32)
        scores = jnp.dot(query_head, key_head.T, preferred_element_type=jnp.float32) * score_scale
        return (jnp.where(allowed, scores, -jnp.inf), query_head, key_head, value_head)

    def forward_head(head_index):
        scores, query_head, key_head, value_head = head_scores(head_index)
        row_max = lax.optimization_barrier(jnp.max(scores, axis=1))
        weights = jnp.exp(scores - row_max[:, None])
        row_total = lax.optimization_barrier(jnp.sum(weights, axis=1))
        head_out = jnp.dot(to_bf16(weights).astype(jnp.float32), value_head, preferred_element_type=jnp.float32) / row_total[:, None]
        return (head_out.astype(jnp.bfloat16), row_max + jnp.log(row_total))
    attention_heads, log_total = lax.map(forward_head, head_ids)
    attention = jnp.transpose(attention_heads, (1, 0, 2)).reshape(slot_count, HEADS * HD)
    projection = jnp.dot(attention.astype(jnp.float32), out_weight.astype(jnp.float32), preferred_element_type=jnp.float32)
    gate_value = jax.nn.sigmoid(router_logit)
    kept_gate = jnp.where(live_slot, gate_value, 0.0)
    update = (kept_gate[:, None] * projection).astype(jnp.bfloat16)
    hidden_after = hidden_state.astype(jnp.float32).at[position].add(update.astype(jnp.float32)).astype(jnp.bfloat16)
    cotangent = out_cotangent.astype(jnp.float32)
    grad_logit = jnp.where(live_slot, gate_value * (1.0 - gate_value), 0.0) * lax.optimization_barrier(jnp.sum(cotangent * projection, axis=1))
    scaled = to_bf16(kept_gate[:, None] * cotangent)
    grad_attention = to_bf16(jnp.dot(scaled.astype(jnp.float32), out_weight.astype(jnp.float32).T, preferred_element_type=jnp.float32))
    grad_heads = jnp.transpose(grad_attention.reshape(slot_count, HEADS, HD), (1, 0, 2))

    def backward_head(inputs):
        head_index, head_log_total, head_out, head_grad = inputs
        scores, query_head, key_head, value_head = head_scores(head_index)
        out_values = head_out.astype(jnp.float32)
        grad_values_in = head_grad.astype(jnp.float32)
        row_delta = lax.optimization_barrier(jnp.sum(out_values * grad_values_in, axis=1))
        probability = jnp.exp(scores - head_log_total[:, None])
        rounded_prob = to_bf16(probability).astype(jnp.float32)
        value_grad = jnp.dot(rounded_prob.T, grad_values_in, preferred_element_type=jnp.float32)
        grad_probs = jnp.dot(grad_values_in, value_head.T, preferred_element_type=jnp.float32)
        grad_score = to_bf16(probability * (grad_probs - row_delta[:, None]) * score_scale).astype(jnp.float32)
        query_grad = jnp.dot(grad_score, key_head, preferred_element_type=jnp.float32)
        key_grad = jnp.dot(grad_score.T, query_head, preferred_element_type=jnp.float32)
        return (query_grad, key_grad, value_grad)
    query_grads, key_grads, value_grads = lax.map(backward_head, (head_ids, log_total, attention_heads, grad_heads))
    grad_turned_queries = jnp.transpose(query_grads, (1, 0, 2)).reshape(slot_count, HEADS * HD)
    key_sum = lax.optimization_barrier(jnp.sum(key_grads.reshape(KV_HEADS, group_size, slot_count, HD), axis=1))
    value_sum = lax.optimization_barrier(jnp.sum(value_grads.reshape(KV_HEADS, group_size, slot_count, HD), axis=1))
    grad_turned_keys = jnp.transpose(key_sum, (1, 0, 2)).reshape(slot_count, KV_HEADS * HD)
    grad_values = jnp.transpose(value_sum, (1, 0, 2)).reshape(slot_count, KV_HEADS * HD).astype(jnp.bfloat16)
    grad_queries = rotate(grad_turned_queries, position, -1.0).astype(jnp.bfloat16)
    grad_keys = rotate(grad_turned_keys, position, -1.0).astype(jnp.bfloat16)
    return (update, grad_queries, grad_keys, grad_values, grad_logit, hidden_after)
```

```python
import functools
import math

import jax
import jax.numpy as jnp
from jax import lax
from jax.experimental import pallas as pl
from jax.experimental.pallas import tpu as pltpu
from jax.sharding import PartitionSpec as P

HD = 128
TOK_DEV = 512
ROTARY_BASE = 500000.0
LOWEST = -1e30
DEAD_MARK = 1024.0
DEAD_LIMIT = 512.0
F32 = jnp.float32
BF16 = jnp.bfloat16

VMEM = pl.BlockSpec(memory_space=pltpu.VMEM)
SMEM = pl.BlockSpec(memory_space=pltpu.SMEM)


def call(kernel, out_shape, in_specs, scratch=(), limit=32):
    return pl.pallas_call(
        kernel,
        out_shape=out_shape,
        in_specs=in_specs,
        out_specs=jax.tree.map(lambda _: VMEM, out_shape),
        scratch_shapes=list(scratch),
        compiler_params=pltpu.CompilerParams(vmem_limit_bytes=limit * 1024 * 1024),
    )


def turn(rows, cos_full, sin_signed):
    return rows * cos_full + pltpu.roll(rows, HD // 2, 1) * sin_signed


def matmul(a, b, dims):
    return lax.dot_general(a, b, (dims, ((), ())), preferred_element_type=F32)


def payload_kernel(key_ref, value_ref, cos_ref, sin_ref, count_ref, pay_ref):
    rows = key_ref.shape[0]
    turned = turn(key_ref[...].astype(F32), cos_ref[...], sin_ref[...])
    pay_ref[0:rows, :] = turned.astype(BF16)
    row_ids = lax.broadcasted_iota(jnp.int32, (rows, HD), 0)
    col_ids = lax.broadcasted_iota(jnp.int32, (rows, HD), 1)
    marked = (row_ids >= count_ref[0]) & (col_ids == 0)
    value = jnp.where(marked, DEAD_MARK, value_ref[...].astype(F32))
    pay_ref[rows : 2 * rows, :] = value.astype(BF16)


def cotangent_kernel(weight_ref, gate_ref, cot_ref, grad_ref):
    width = cot_ref.shape[2]
    total = None
    for step in range(cot_ref.shape[0]):
        part = matmul(cot_ref[step], weight_ref[:, step * width : (step + 1) * width], ((1,), (1,)))
        total = part if total is None else total + part
    grad_ref[...] = (total * gate_ref[...]).astype(BF16)


def attention_kernel(
    dims,
    place_ref,
    query_ref,
    cos_ref,
    sin_ref,
    col_ref,
    row_ref,
    grad_ref,
    own_ref,
    same_ref,
    other_ref,
    att_ref,
    dq_ref,
    delta_ref,
    own_out,
    same_out,
    other_out,
    score_ref,
    weight_ref,
):
    ny, nx, nc = dims
    slots = query_ref.shape[0]
    heads = query_ref.shape[1] // HD
    rows = slots * heads
    keys = ny * slots
    scale = 1.0 / math.sqrt(HD)
    cos_full, sin_signed = cos_ref[...], sin_ref[...]

    me = place_ref[0]
    my_core = lax.rem(me, nc)
    groups = [(ref, out, flip, x) for flip, (ref, out) in enumerate(((same_ref, same_out), (other_ref, other_out))) for x in range(nx)]

    turned = [
        turn(query_ref[:, h * HD : (h + 1) * HD].astype(F32), cos_full, sin_signed).astype(BF16)
        for h in range(heads)
    ]
    query_t = jnp.concatenate(turned, axis=0).astype(F32).T
    query_tb = query_t.astype(BF16)
    grads = [grad_ref[:, h * HD : (h + 1) * HD].astype(F32) for h in range(heads)]
    grad_t = jnp.concatenate(grads, axis=0).T
    grad_tb = grad_t.astype(BF16)
    own_keys, own_values = own_ref[0:slots, :], own_ref[slots : 2 * slots, :]

    def keys_of(group):
        return group[0][group[3], :, 0:slots, :].reshape(keys, HD)

    def values_of(group):
        return group[0][group[3], :, slots : 2 * slots, :].reshape(keys, HD)

    own_scores = matmul(own_keys, query_tb, ((1,), (0,)))
    dead = own_values[:, 0:1].astype(F32) > DEAD_LIMIT
    own_scores = jnp.where(col_ref[...] <= row_ref[...], own_scores, LOWEST)
    own_scores = own_scores + jnp.where(dead, LOWEST, 0.0)
    peak = jnp.max(own_scores, axis=0, keepdims=True)
    for number, group in enumerate(groups):
        core = my_core if group[2] == 0 else (nc - 1) - my_core
        scores = matmul(keys_of(group), query_tb, ((1,), (0,)))
        for y in range(ny):
            shard = (y * nx + group[3]) * nc + core
            reach = jnp.where(shard < me, 0.0, LOWEST)
            first = group[0][group[3], y, slots : 2 * slots, 0:1].astype(F32)
            bias = jnp.where(first > DEAD_LIMIT, LOWEST, reach)
            block = scores[y * slots : (y + 1) * slots, :] + bias
            score_ref[number, y * slots : (y + 1) * slots, :] = block
            peak = jnp.maximum(peak, jnp.max(block, axis=0, keepdims=True))

    factor = scale * math.log2(math.e)
    own_weights = jnp.exp2((own_scores - peak) * factor)
    total = jnp.sum(own_weights, axis=0, keepdims=True)
    own_weights = own_weights.astype(BF16)
    summed = matmul(own_values, own_weights, ((0,), (0,)))
    for number, group in enumerate(groups):
        weights = jnp.exp2((score_ref[number] - peak) * factor)
        total = total + jnp.sum(weights, axis=0, keepdims=True)
        weights = weights.astype(BF16)
        weight_ref[number] = weights
        summed = summed + matmul(values_of(group), weights, ((0,), (0,)))

    inverse = 1.0 / total
    att_t = (summed * inverse).astype(BF16).astype(F32)
    att = att_t.T.astype(BF16)
    for h in range(heads):
        att_ref[:, h * HD : (h + 1) * HD] = att[h * slots : (h + 1) * slots, :]
    delta = jnp.sum(att_t * grad_t, axis=0, keepdims=True)
    delta_ref[...] = jnp.broadcast_to(delta, delta_ref.shape)

    query_scaled = (query_t * (inverse * scale)).astype(BF16)
    grad_scaled = (grad_t * inverse).astype(BF16)

    def backward(weights, keys_in, values_in):
        grad_probs = matmul(values_in, grad_tb, ((1,), (0,)))
        grad_score = (weights.astype(F32) * (grad_probs - delta)).astype(BF16)
        key_part = matmul(grad_score, query_scaled, ((1,), (1,)))
        value_part = matmul(weights, grad_scaled, ((1,), (1,)))
        return key_part, value_part, matmul(keys_in, grad_score, ((0,), (0,)))

    key_part, value_part, dq_t = backward(own_weights, own_keys, own_values)
    own_out[0:slots, :] = key_part
    own_out[slots : 2 * slots, :] = value_part
    for number, group in enumerate(groups):
        key_part, value_part, dq_part = backward(weight_ref[number], keys_of(group), values_of(group))
        out, x = group[1], group[3]
        out[x, :, 0:slots, :] = key_part.astype(BF16).reshape(ny, slots, HD)
        out[x, :, slots : 2 * slots, :] = value_part.astype(BF16).reshape(ny, slots, HD)
        dq_t = dq_t + dq_part
    dq = (dq_t * (inverse * scale)).T
    for h in range(heads):
        back = turn(dq[h * slots : (h + 1) * slots, :], cos_full, -sin_signed)
        dq_ref[:, h * HD : (h + 1) * HD] = back.astype(BF16)


def projection_kernel(weight_ref, att_ref, delta_ref, part_ref):
    slots = att_ref.shape[0]
    width = part_ref.shape[2]
    rows = delta_ref.shape[1]
    delta = delta_ref[...]
    row_sum = delta[:, 0:slots]
    for h in range(1, rows // slots):
        row_sum = row_sum + delta[:, h * slots : (h + 1) * slots]
    high = row_sum.astype(BF16).astype(F32)
    low = row_sum - high
    extra_ids = lax.broadcasted_iota(jnp.int32, (16, slots), 0)
    high = jnp.concatenate([high, high], axis=0)
    low = jnp.concatenate([low, low], axis=0)
    extra = jnp.where(extra_ids == 0, high, jnp.where(extra_ids == 1, low, 0.0))
    extra = jnp.concatenate([extra, jnp.zeros((16, width - slots), F32)], axis=1).astype(BF16)
    att = att_ref[...]
    for step in range(part_ref.shape[0]):
        part = matmul(att, weight_ref[:, step * width : (step + 1) * width], ((1,), (0,)))
        part_ref[step, 0:slots, :] = part.astype(BF16)
        part_ref[step, slots : slots + 16, :] = extra


def added_up(stack_ref):
    total = stack_ref[0].astype(F32)
    for step in range(1, stack_ref.shape[0]):
        total = total + stack_ref[step].astype(F32)
    return total


def update_kernel(shares_ref, gate_ref, index_ref, gate_row_ref, hidden_ref, update_ref, after_ref, logit_ref):
    slots = update_ref.shape[0]
    tokens = hidden_ref.shape[0]
    total = added_up(shares_ref)
    update = (total[0:slots, :] * gate_ref[...]).astype(BF16)
    update_ref[...] = update
    token_ids = lax.broadcasted_iota(jnp.int32, (tokens, slots), 0)
    chosen = jnp.where(token_ids == index_ref[...], 1.0, 0.0).astype(BF16)
    added = matmul(chosen, update, ((1,), (0,)))
    after_ref[...] = (hidden_ref[...].astype(F32) + added).astype(BF16)
    sums = total[slots : slots + 1, 0:slots] + total[slots + 1 : slots + 2, 0:slots]
    logit_ref[...] = sums * gate_row_ref[...]


def finish_kernel(cos_ref, sin_ref, own_ref, landed_ref, dk_ref, dv_ref):
    slots = dk_ref.shape[0]
    total = own_ref[...] + added_up(landed_ref)
    dk_ref[...] = turn(total[0:slots, :], cos_ref[...], -sin_ref[...]).astype(BF16)
    dv_ref[...] = total[slots : 2 * slots, :].astype(BF16)


def on_device(
    dims,
    tp_count,
    queries,
    key_vectors,
    value_vectors,
    out_weight,
    router_logit,
    chosen_index,
    chosen_count,
    out_cotangent,
    hidden_state,
):
    ny, nx, nc = dims
    slots, width = queries.shape
    heads = width // HD

    def at(y, x, c):
        return (y * nx + x) * nc + c

    y_groups = [[at(y, x, c) for y in range(ny)] for x in range(nx) for c in range(nc)]
    x_groups = [[at(y, x, c) for x in range(nx)] for y in range(ny) for c in range(nc)]
    flips = [(i, i + 1 if i % nc == 0 else i - 1) for i in range(ny * nx * nc)]

    def exchange(array, axis, groups=None):
        return lax.all_to_all(array, axis, 0, 0, axis_index_groups=groups, tiled=True)

    def copies(array, count):
        return jnp.broadcast_to(array[None], (count,) + array.shape)

    my_shard = lax.axis_index("ctx").astype(jnp.int32)
    my_part = lax.axis_index("tp").astype(jnp.int32)
    place = jnp.stack([my_shard, my_part])
    position = my_shard * TOK_DEV + chosen_index
    half = jnp.arange(HD // 2, dtype=F32)
    frequency = ROTARY_BASE ** (-(half * 2.0 / HD))
    angles = position.astype(F32)[:, None] * jnp.concatenate([frequency, frequency])[None, :]
    sign = jnp.concatenate([jnp.full((HD // 2,), -1.0, F32), jnp.ones((HD // 2,), F32)])
    cos_full = jnp.cos(angles)
    sin_signed = jnp.sin(angles) * sign[None, :]

    cot = exchange(copies(out_cotangent, tp_count), "tp")

    payload = call(
        payload_kernel, jax.ShapeDtypeStruct((2 * slots, HD), BF16), [VMEM] * 4 + [SMEM]
    )(key_vectors, value_vectors, cos_full, sin_signed, chosen_count)

    column = exchange(copies(payload, ny), "ctx", y_groups)
    same = exchange(copies(column, nx), "ctx", x_groups)
    other = lax.ppermute(same, "ctx", flips)

    gate_value = jax.nn.sigmoid(router_logit)
    live_slot = jnp.arange(slots, dtype=jnp.int32) < chosen_count[0]
    kept_gate = jnp.where(live_slot, gate_value, 0.0)
    rest_gate = jnp.where(live_slot, 1.0 - gate_value, 0.0)

    grad_attention = call(
        cotangent_kernel, jax.ShapeDtypeStruct((slots, width), BF16), [VMEM] * 3
    )(out_weight, kept_gate[:, None], cot)

    rows = slots * heads
    half_shape = (nx, ny, 2 * slots, HD)
    attention, grad_queries, delta, own_part, same_part, other_part = call(
        functools.partial(attention_kernel, dims),
        [
            jax.ShapeDtypeStruct((slots, width), BF16),
            jax.ShapeDtypeStruct((slots, width), BF16),
            jax.ShapeDtypeStruct((8, rows), F32),
            jax.ShapeDtypeStruct((2 * slots, HD), F32),
            jax.ShapeDtypeStruct(half_shape, BF16),
            jax.ShapeDtypeStruct(half_shape, BF16),
        ],
        [SMEM] + [VMEM] * 9,
        [
            pltpu.VMEM((nx * nc, ny * slots, rows), F32),
            pltpu.VMEM((nx * nc, ny * slots, rows), BF16),
        ],
        limit=48,
    )(
        place,
        queries,
        cos_full,
        sin_signed,
        chosen_index[:, None],
        jnp.tile(chosen_index, heads)[None, :],
        grad_attention,
        payload,
        same,
        other,
    )

    paired = (same_part.astype(F32) + lax.ppermute(other_part, "ctx", flips).astype(F32)).astype(BF16)
    crossed = exchange(paired, "ctx", x_groups)
    stacked = jnp.sum(crossed.astype(F32), axis=0).astype(BF16)

    shares = call(
        projection_kernel,
        jax.ShapeDtypeStruct((tp_count, slots + 16, width), BF16),
        [VMEM] * 3,
    )(out_weight, attention, delta)
    arrived = exchange(shares, "tp")
    update, hidden_after, logit_row = call(
        update_kernel,
        [
            jax.ShapeDtypeStruct((slots, width), BF16),
            jax.ShapeDtypeStruct(hidden_state.shape, BF16),
            jax.ShapeDtypeStruct((1, slots), F32),
        ],
        [VMEM] * 5,
    )(arrived, kept_gate[:, None], chosen_index[None, :], rest_gate[None, :], hidden_state)

    landed = exchange(stacked, "ctx", y_groups)
    grad_keys, grad_values = call(
        finish_kernel, [jax.ShapeDtypeStruct((slots, HD), BF16)] * 2, [VMEM] * 4
    )(cos_full, sin_signed, own_part, landed)
    return (update, grad_queries, grad_keys, grad_values, logit_row[0], hidden_after)


def solution(mesh):
    shards, tp_count = mesh.shape["ctx"], mesh.shape["tp"]
    nc = 2
    nx = 4 if shards >= 64 else 2
    dims = (shards // (nx * nc), nx, nc)
    placed = (
        P("ctx", "tp"),
        P("ctx", "tp"),
        P("ctx", "tp"),
        P("tp", None),
        P("ctx"),
        P("ctx"),
        P("ctx"),
        P("ctx", "tp"),
        P("ctx", "tp"),
    )
    return jax.shard_map(
        functools.partial(on_device, dims, tp_count),
        mesh=mesh,
        in_specs=placed,
        out_specs=(
            P("ctx", "tp"),
            P("ctx", "tp"),
            P("ctx", "tp"),
            P("ctx", "tp"),
            P("ctx"),
            P("ctx", "tp"),
        ),
        check_vma=False,
    )
```

```python
import functools
import math

import jax
import jax.numpy as jnp
from jax import lax
from jax.experimental import pallas as pl
from jax.experimental.pallas import tpu as pltpu
from jax.sharding import PartitionSpec as P

HD = 128
TOK_DEV = 512
ROTARY_BASE = 500000.0
LOWEST = -1e30
DEAD_MARK = 1024.0
DEAD_LIMIT = 512.0
SCALE = 1.0 / math.sqrt(HD)
FACTOR = SCALE * math.log2(math.e)
F32 = jnp.float32
BF16 = jnp.bfloat16

VMEM = pl.BlockSpec(memory_space=pltpu.VMEM)
SMEM = pl.BlockSpec(memory_space=pltpu.SMEM)
HBM = pl.BlockSpec(memory_space=pltpu.HBM)


def call(kernel, out_shape, in_specs, scratch=(), limit=32, out_specs=None):
    return pl.pallas_call(
        kernel,
        out_shape=out_shape,
        in_specs=in_specs,
        out_specs=out_specs or jax.tree.map(lambda _: VMEM, out_shape),
        scratch_shapes=list(scratch),
        compiler_params=pltpu.CompilerParams(vmem_limit_bytes=limit * 1024 * 1024),
    )


def turn(rows, cos_full, sin_signed):
    return rows * cos_full + pltpu.roll(rows, HD // 2, 1) * sin_signed


def matmul(a, b, dims):
    return lax.dot_general(a, b, (dims, ((), ())), preferred_element_type=F32)


def as_column(row):
    count = row.shape[1]
    down = lax.broadcasted_iota(jnp.int32, (count, count), 0)
    across = lax.broadcasted_iota(jnp.int32, (count, count), 1)
    return jnp.sum(jnp.where(down == across, row, 0.0), axis=1, keepdims=True)


def live_row(count_ref, slots):
    return lax.broadcasted_iota(jnp.int32, (1, slots), 1) < count_ref[0]


def stacked_heads(field):
    heads = field.shape[1] // HD
    return jnp.concatenate([field[:, h * HD : (h + 1) * HD].astype(F32) for h in range(heads)], axis=0)


def payload_kernel(count_ref, pair_ref, position_ref, frequency_ref, pay_ref, copies_ref, cos_ref, sin_ref):
    slots = cos_ref.shape[0]
    angles = as_column(position_ref[...]) * frequency_ref[...]
    col_ids = lax.broadcasted_iota(jnp.int32, (slots, HD), 1)
    row_ids = lax.broadcasted_iota(jnp.int32, (slots, HD), 0)
    cos_full = jnp.cos(angles)
    sin_signed = jnp.where(col_ids < HD // 2, -1.0, 1.0) * jnp.sin(angles)
    cos_ref[...] = cos_full
    sin_ref[...] = sin_signed
    turned = turn(pair_ref[0:slots, :].astype(F32), cos_full, sin_signed).astype(BF16)
    marked = (row_ids >= count_ref[0]) & (col_ids == 0)
    value = jnp.where(marked, DEAD_MARK, pair_ref[slots : 2 * slots, :].astype(F32)).astype(BF16)
    pay_ref[0:slots, :] = turned
    pay_ref[slots : 2 * slots, :] = value
    for i in range(copies_ref.shape[0]):
        copies_ref[i, 0:slots, :] = turned
        copies_ref[i, slots : 2 * slots, :] = value


def copies_kernel(in_ref, out_ref, sems):
    copies = [pltpu.make_async_copy(in_ref, out_ref.at[i], sems.at[i]) for i in range(out_ref.shape[0])]
    for copy in copies:
        copy.start()
    for copy in copies:
        copy.wait()


def weight_kernel(place_ref, weight_ref, held_ref, sems):
    parts, _, width = held_ref.shape
    way = 1 - 2 * lax.rem(place_ref[0], 2)
    copies = []
    for at, step in enumerate(doubling_order(parts)):
        owner = lax.rem(place_ref[1] - step * way + parts, parts)
        columns = pl.ds(pl.multiple_of(owner * width, width), width)
        copies.append(pltpu.make_async_copy(weight_ref.at[:, columns], held_ref.at[at], sems.at[at]))
    for copy in copies:
        copy.start()
    for copy in copies:
        copy.wait()


def query_kernel(query_ref, cos_ref, sin_ref, out_ref):
    cos_full, sin_signed = cos_ref[...], sin_ref[...]
    for h in range(query_ref.shape[1] // HD):
        part = query_ref[:, h * HD : (h + 1) * HD].astype(F32)
        out_ref[:, h * HD : (h + 1) * HD] = turn(part, cos_full, sin_signed).astype(BF16)


def cotangent_kernel(count_ref, held_ref, logit_ref, cot_ref, part_ref, grad_ref, bundle_ref):
    slots = grad_ref.shape[0]
    bundle_ref[0 : HD + 8, :] = part_ref[...]
    gate = jnp.where(live_row(count_ref, slots), 1.0 / (1.0 + jnp.exp(-logit_ref[...])), 0.0)
    total = None
    for step in range(held_ref.shape[0]):
        part = matmul(cot_ref[step], held_ref[step], ((1,), (1,)))
        total = part if total is None else total + part
    grad = (total * as_column(gate)).astype(BF16)
    grad_ref[...] = grad
    bundle_ref[HD + 8 : HD + 8 + slots, :] = grad.astype(F32)


def forward_kernel(dims, place_ref, index_ref, own_ref, sibling_ref, pay_ref, piece_ref, part_ref, weight_ref, score_ref):
    ny, nx, nc = dims
    slots = own_ref.shape[0]
    rows = part_ref.shape[1]
    keys = ny * slots
    me = place_ref[0]
    my_core = lax.rem(me, nc)
    my_x = lax.rem(lax.div(me, nc), nx)
    my_y = lax.div(me, nc * nx)

    query = jnp.concatenate([stacked_heads(own_ref[...]), stacked_heads(sibling_ref[...])], axis=0)
    query_t = query.T.astype(BF16)
    index_row = index_ref[...].astype(F32)
    index_col = as_column(index_row)
    beyond = jnp.where(my_core == 0, 2.0 * TOK_DEV, -1.0)
    sibling_row = jnp.full((1, rows // 2), 1.0, F32) * beyond
    own_rows = rows // 2 // slots
    limit_row = jnp.concatenate([index_row] * own_rows + [sibling_row], axis=1)

    peak = jnp.full((1, rows), LOWEST, F32)
    for x in range(nx):
        scores = matmul(piece_ref[x, :, 0:slots, :].reshape(keys, HD), query_t, ((1,), (0,)))
        for y in range(ny):
            shard = (y * nx + x) * nc + my_core
            reach = jnp.where(shard < me, 0.0, LOWEST)
            first = piece_ref[x, y, slots : 2 * slots, 0:1].astype(F32)
            bias = jnp.where(first > DEAD_LIMIT, LOWEST, reach)
            block = scores[y * slots : (y + 1) * slots, :] + bias
            score_ref[x, y * slots : (y + 1) * slots, :] = block
            peak = jnp.maximum(peak, jnp.max(block, axis=0, keepdims=True))

    own_keys, own_values = pay_ref[0:slots, :], pay_ref[slots : 2 * slots, :]
    own_scores = matmul(own_keys, query_t, ((1,), (0,)))
    own_scores = jnp.where(index_col <= limit_row, own_scores, LOWEST)
    own_scores = own_scores + jnp.where(own_values[:, 0:1].astype(F32) > DEAD_LIMIT, LOWEST, 0.0)
    own_at = pl.ds(pl.multiple_of(my_y * slots, slots), slots)
    score_ref[pl.ds(my_x, 1), own_at, :] = own_scores[None]
    peak = jnp.maximum(peak, jnp.max(own_scores, axis=0, keepdims=True))

    total = jnp.zeros((1, rows), F32)
    summed = jnp.zeros((HD, rows), F32)
    for x in range(nx):
        weights = jnp.exp2((score_ref[x] - peak) * FACTOR)
        total = total + jnp.sum(weights, axis=0, keepdims=True)
        weights = weights.astype(BF16)
        weight_ref[x] = weights
        values = piece_ref[x, :, slots : 2 * slots, :].reshape(keys, HD)
        summed = summed + matmul(values, weights, ((0,), (0,)))
    part_ref[0:HD, :] = summed
    row_ids = lax.broadcasted_iota(jnp.int32, (8, rows), 0)
    part_ref[HD : HD + 8, :] = jnp.where(row_ids == 0, peak, total)


def backward_kernel(
    dims, own_part, sibling_part, own_ref, sibling_ref, grad_ref, weight_ref, piece_ref, att_ref, delta_ref, dq_ref, dq_sibling_ref, out_ref, stage, sems
):
    ny, nx, nc = dims
    slots = own_ref.shape[0]
    rows = own_part.shape[1]
    half = rows // 2
    heads = half // slots
    keys = ny * slots

    def swapped(at):
        return jnp.concatenate([sibling_part[at, half:rows], sibling_part[at, 0:half]], axis=1)

    stats = pl.ds(HD, 8)
    mine, theirs = own_part[stats, :], swapped(stats)
    peak = jnp.maximum(mine[0:1], theirs[0:1])
    mine_factor = jnp.exp2((mine[0:1] - peak) * FACTOR)
    their_factor = jnp.exp2((theirs[0:1] - peak) * FACTOR)
    inverse = 1.0 / (mine[1:2] * mine_factor + theirs[1:2] * their_factor)
    body = pl.ds(0, HD)
    mine_factor, their_factor = mine_factor * inverse, their_factor * inverse
    att_t = own_part[body, :] * mine_factor + swapped(body) * their_factor
    att_t = att_t.astype(BF16).astype(F32)
    att = att_t[:, 0:half].T.astype(BF16)
    for h in range(heads):
        att_ref[:, h * HD : (h + 1) * HD] = att[h * slots : (h + 1) * slots, :]

    query_t = jnp.concatenate([stacked_heads(own_ref[...]), stacked_heads(sibling_ref[...])], axis=0).T
    sibling_grad = sibling_part[HD + 8 : HD + 8 + slots, :]
    grad_t = jnp.concatenate([stacked_heads(grad_ref[...]), stacked_heads(sibling_grad)], axis=0).T
    grad_tb = grad_t.astype(BF16)
    delta = jnp.sum(att_t * grad_t, axis=0, keepdims=True)
    delta_ref[...] = jnp.broadcast_to(delta[:, 0:half], delta_ref.shape)

    query_scaled = (query_t * (mine_factor * SCALE)).astype(BF16)
    grad_scaled = (grad_t * mine_factor).astype(BF16)
    dq_t = jnp.zeros((HD, rows), F32)
    copies = []
    for x in range(nx):
        weights = weight_ref[x]
        values = piece_ref[x, :, slots : 2 * slots, :].reshape(keys, HD)
        grad_probs = matmul(values, grad_tb, ((1,), (0,)))
        grad_score = (weights.astype(F32) * (grad_probs - delta)).astype(BF16)
        key_part = matmul(grad_score, query_scaled, ((1,), (1,)))
        value_part = matmul(weights, grad_scaled, ((1,), (1,)))
        stage[x, :, 0:slots, :] = key_part.astype(BF16).reshape(ny, slots, HD)
        stage[x, :, slots : 2 * slots, :] = value_part.astype(BF16).reshape(ny, slots, HD)
        copies.append(pltpu.make_async_copy(stage.at[x], out_ref.at[x], sems.at[x]))
        copies[-1].start()
        dq_t = dq_t + matmul(piece_ref[x, :, 0:slots, :].reshape(keys, HD), grad_score, ((0,), (0,)))
    dq = (dq_t * (mine_factor * SCALE)).T
    dq_ref[...] = dq[0:half, :]
    dq_sibling_ref[...] = dq[half:rows, :].astype(BF16)
    for copy in copies:
        copy.wait()


def projection_kernel(held_ref, att_ref, delta_ref, near_ref, far_ref):
    slots = att_ref.shape[0]
    half, _, width = near_ref.shape
    rows = delta_ref.shape[1]
    delta = delta_ref[...]
    row_sum = delta[:, 0:slots]
    for h in range(1, rows // slots):
        row_sum = row_sum + delta[:, h * slots : (h + 1) * slots]
    extra = jnp.concatenate([row_sum, jnp.zeros((8, width - slots), F32)], axis=1)
    extra = jnp.concatenate([extra, extra], axis=0).astype(BF16)
    att = att_ref[...]
    for step in range(held_ref.shape[0]):
        part_ref, at = (near_ref, step) if step < half else (far_ref, step - half)
        part_ref[at, 0:slots, :] = matmul(att, held_ref[step], ((1,), (0,))).astype(BF16)
        part_ref[at, slots : slots + 16, :] = extra


def added_up(stack_ref):
    total = stack_ref[0].astype(F32)
    for step in range(1, stack_ref.shape[0]):
        total = total + stack_ref[step].astype(F32)
    return total


def sum_kernel(stack_ref, out_ref):
    out_ref[...] = added_up(stack_ref).astype(BF16)


def update_kernel(count_ref, own_ref, landed_ref, logit_ref, index_ref, hidden_ref, update_ref, after_ref, grad_ref):
    slots = update_ref.shape[0]
    tokens = hidden_ref.shape[0]
    live = live_row(count_ref, slots)
    gate = 1.0 / (1.0 + jnp.exp(-logit_ref[...]))
    total = own_ref[0].astype(F32) + landed_ref[0].astype(F32)
    update = (total[0:slots, :] * as_column(jnp.where(live, gate, 0.0))).astype(BF16)
    update_ref[...] = update
    token_ids = lax.broadcasted_iota(jnp.int32, (tokens, slots), 0)
    chosen = jnp.where(token_ids == index_ref[...], 1.0, 0.0).astype(BF16)
    added = matmul(chosen, update, ((1,), (0,)))
    after_ref[...] = (hidden_ref[...].astype(F32) + added).astype(BF16)
    grad_ref[...] = jnp.where(live, total[slots : slots + 1, 0:slots] * (1.0 - gate), 0.0)


def query_grad_kernel(cos_ref, sin_ref, own_ref, arrived_ref, dq_ref):
    slots = dq_ref.shape[0]
    total = own_ref[...] + arrived_ref[...].astype(F32)
    for h in range(dq_ref.shape[1] // HD):
        back = turn(total[h * slots : (h + 1) * slots, :], cos_ref[...], -sin_ref[...])
        dq_ref[:, h * HD : (h + 1) * HD] = back.astype(BF16)


def finish_kernel(cos_ref, sin_ref, landed_ref, dk_ref, dv_ref):
    slots = dk_ref.shape[0]
    total = added_up(landed_ref)
    dk_ref[...] = turn(total[0:slots, :], cos_ref[...], -sin_ref[...]).astype(BF16)
    dv_ref[...] = total[slots : 2 * slots, :].astype(BF16)


def doubling_steps(count):
    steps = []
    step = count // 2
    while step:
        steps.append(step)
        step //= 2
    return steps


def doubling_order(count):
    order = [0]
    for step in doubling_steps(count):
        order = order + [place + step for place in order]
    return order


def on_device(
    dims,
    tp_count,
    queries,
    key_vectors,
    value_vectors,
    out_weight,
    router_logit,
    chosen_index,
    chosen_count,
    out_cotangent,
    hidden_state,
):
    ny, nx, nc = dims
    slots, width = queries.shape
    heads = width // HD
    rows = nc * heads * slots
    keys = ny * slots

    def at(y, x, c):
        return (y * nx + x) * nc + c

    y_groups = [[at(y, x, c) for y in range(ny)] for x in range(nx) for c in range(nc)]
    x_groups = [[at(y, x, c) for x in range(nx)] for y in range(ny) for c in range(nc)]

    def exchange(array, groups):
        return lax.all_to_all(array, "ctx", 0, 0, axis_index_groups=groups, tiled=True)

    def to_sibling(array):
        return lax.ppermute(array, "ctx", [(i, i ^ 1) for i in range(ny * nx * nc)])

    def tp_send(array, shift):
        pairs = []
        for shard in range(ny * nx * nc):
            for part in range(tp_count):
                to = (part + shift * (1 - 2 * (shard % nc))) % tp_count
                pairs.append((shard * tp_count + part, shard * tp_count + to))
        return lax.ppermute(array, ("ctx", "tp"), pairs)

    def summed(first, second):
        return (first.astype(F32) + second.astype(F32)).astype(BF16)

    my_shard = lax.axis_index("ctx").astype(jnp.int32)
    place = jnp.stack([my_shard, lax.axis_index("tp").astype(jnp.int32)])
    index_row = chosen_index[None, :]
    logit_row = router_logit[None, :]
    half = jnp.arange(HD // 2, dtype=F32)
    frequency = ROTARY_BASE ** (-(half * 2.0 / HD))
    frequency = jnp.concatenate([frequency, frequency])[None, :]

    payload, payloads, cos_full, sin_signed = call(
        payload_kernel,
        [
            jax.ShapeDtypeStruct((2 * slots, HD), BF16),
            jax.ShapeDtypeStruct((ny, 2 * slots, HD), BF16),
            jax.ShapeDtypeStruct((slots, HD), F32),
            jax.ShapeDtypeStruct((slots, HD), F32),
        ],
        [SMEM] + [VMEM] * 3,
    )(
        chosen_count,
        jnp.concatenate([key_vectors, value_vectors], axis=0),
        (my_shard * TOK_DEV + chosen_index).astype(F32)[None, :],
        frequency,
    )
    column = exchange(payloads, y_groups)

    own_queries = call(
        query_kernel, jax.ShapeDtypeStruct((slots, width), BF16), [VMEM] * 3
    )(queries, cos_full, sin_signed)
    sibling_queries = to_sibling(own_queries)
    column, sibling_queries = lax.optimization_barrier((column, sibling_queries))
    columns = call(
        copies_kernel,
        jax.ShapeDtypeStruct((nx,) + column.shape, BF16),
        [VMEM],
        [pltpu.SemaphoreType.DMA((nx,))],
        out_specs=HBM,
    )(column)
    pieces = exchange(columns, x_groups)

    held = call(
        weight_kernel,
        jax.ShapeDtypeStruct((tp_count, width, width), BF16),
        [SMEM, HBM],
        [pltpu.SemaphoreType.DMA((tp_count,))],
    )(place, out_weight)

    cot = out_cotangent[None]
    for step in doubling_steps(tp_count):
        if step == 1:
            cot, held = lax.optimization_barrier((cot, held))
        cot = jnp.concatenate([cot, tp_send(cot, step)], axis=0)

    part, weights = call(
        functools.partial(forward_kernel, dims),
        [
            jax.ShapeDtypeStruct((HD + 8, rows), F32),
            jax.ShapeDtypeStruct((nx, keys, rows), BF16),
        ],
        [SMEM] + [VMEM] * 5,
        [pltpu.VMEM((nx, keys, rows), F32)],
    )(place, index_row, own_queries, sibling_queries, payload, pieces)
    grad_attention, bundle = call(
        cotangent_kernel,
        [
            jax.ShapeDtypeStruct((slots, width), BF16),
            jax.ShapeDtypeStruct((HD + 8 + slots, rows), F32),
        ],
        [SMEM] + [VMEM] * 4,
    )(chosen_count, held, logit_row, cot, part)
    sibling_bundle = to_sibling(bundle)
    attention, delta, dq_own, dq_sibling, outs = call(
        functools.partial(backward_kernel, dims),
        [
            jax.ShapeDtypeStruct((slots, width), BF16),
            jax.ShapeDtypeStruct((8, rows // 2), F32),
            jax.ShapeDtypeStruct((rows // 2, HD), F32),
            jax.ShapeDtypeStruct((rows // 2, HD), BF16),
            jax.ShapeDtypeStruct((nx, ny, 2 * slots, HD), BF16),
        ],
        [VMEM] * 7,
        [pltpu.VMEM((nx, ny, 2 * slots, HD), BF16), pltpu.SemaphoreType.DMA((nx,))],
        out_specs=[VMEM] * 4 + [HBM],
    )(part, sibling_bundle, own_queries, sibling_queries, grad_attention, weights, pieces)

    crossed = exchange(outs, x_groups)
    near, far = call(
        projection_kernel,
        [jax.ShapeDtypeStruct((tp_count // 2, slots + 16, width), BF16)] * 2,
        [VMEM] * 3,
    )(held, attention, delta)
    dq_arrived = to_sibling(dq_sibling)
    grad_queries = call(
        query_grad_kernel, jax.ShapeDtypeStruct((slots, width), BF16), [VMEM] * 4
    )(cos_full, sin_signed, dq_own, dq_arrived)

    for step in reversed(doubling_steps(tp_count)):
        arrived = tp_send(far, -step)
        if step == 1:
            arrived, grad_queries = lax.optimization_barrier((arrived, grad_queries))
        if near.shape[0] > 1:
            count = near.shape[0] // 2
            far = summed(near[count:], arrived[count:])
            near = summed(near[:count], arrived[:count])
    stacked = call(sum_kernel, jax.ShapeDtypeStruct((ny, 2 * slots, HD), BF16), [VMEM])(crossed)
    landed = exchange(stacked, y_groups)
    grad_keys, grad_values = call(
        finish_kernel, [jax.ShapeDtypeStruct((slots, HD), BF16)] * 2, [VMEM] * 3
    )(cos_full, sin_signed, landed)

    update, hidden_after, grad_row = call(
        update_kernel,
        [
            jax.ShapeDtypeStruct((slots, width), BF16),
            jax.ShapeDtypeStruct(hidden_state.shape, BF16),
            jax.ShapeDtypeStruct((1, slots), F32),
        ],
        [SMEM] + [VMEM] * 5,
    )(chosen_count, near, arrived, logit_row, index_row, hidden_state)
    return (update, grad_queries, grad_keys, grad_values, grad_row[0], hidden_after)


def layout(shards):
    nx = 4 if shards >= 16 else 2
    return (shards // (nx * 2), nx, 2)


def solution(mesh):
    shards, tp_count = mesh.shape["ctx"], mesh.shape["tp"]
    placed = (
        P("ctx", "tp"),
        P("ctx", "tp"),
        P("ctx", "tp"),
        P("tp", None),
        P("ctx"),
        P("ctx"),
        P("ctx"),
        P("ctx", "tp"),
        P("ctx", "tp"),
    )
    return jax.shard_map(
        functools.partial(on_device, layout(shards), tp_count),
        mesh=mesh,
        in_specs=placed,
        out_specs=(
            P("ctx", "tp"),
            P("ctx", "tp"),
            P("ctx", "tp"),
            P("ctx", "tp"),
            P("ctx"),
            P("ctx", "tp"),
        ),
        check_vma=False,
    )
```

```python
import functools
import math

import jax
import jax.numpy as jnp
from jax import lax
from jax.experimental import pallas as pl
from jax.experimental.pallas import tpu as pltpu
from jax.sharding import PartitionSpec as P

HD = 128
TOK_DEV = 512
ROTARY_BASE = 500000.0
LOWEST = -1e30
DEAD_MARK = 1024.0
DEAD_LIMIT = 512.0
SCALE = 1.0 / math.sqrt(HD)
FACTOR = SCALE * math.log2(math.e)
F32 = jnp.float32
BF16 = jnp.bfloat16

VMEM = pl.BlockSpec(memory_space=pltpu.VMEM)
SMEM = pl.BlockSpec(memory_space=pltpu.SMEM)
HBM = pl.BlockSpec(memory_space=pltpu.HBM)


def call(kernel, out_shape, in_specs, scratch=(), limit=32, out_specs=None):
    return pl.pallas_call(
        kernel,
        out_shape=out_shape,
        in_specs=in_specs,
        out_specs=out_specs or jax.tree.map(lambda _: VMEM, out_shape),
        scratch_shapes=list(scratch),
        compiler_params=pltpu.CompilerParams(vmem_limit_bytes=limit * 1024 * 1024),
    )


def turn(rows, cos_full, sin_signed):
    return rows * cos_full + pltpu.roll(rows, HD // 2, 1) * sin_signed


def matmul(a, b, dims):
    return lax.dot_general(a, b, (dims, ((), ())), preferred_element_type=F32)


def as_column(row):
    count = row.shape[1]
    down = lax.broadcasted_iota(jnp.int32, (count, count), 0)
    across = lax.broadcasted_iota(jnp.int32, (count, count), 1)
    return jnp.sum(jnp.where(down == across, row, 0.0), axis=1, keepdims=True)


def live_row(count_ref, slots):
    return lax.broadcasted_iota(jnp.int32, (1, slots), 1) < count_ref[0]


def stacked_heads(field):
    heads = field.shape[1] // HD
    return jnp.concatenate([field[:, h * HD : (h + 1) * HD].astype(F32) for h in range(heads)], axis=0)


def payload_kernel(count_ref, pair_ref, position_ref, frequency_ref, pay_ref, copies_ref, cos_ref, sin_ref, stage, sems):
    slots = cos_ref.shape[0]
    angles = as_column(position_ref[...]) * frequency_ref[...]
    col_ids = lax.broadcasted_iota(jnp.int32, (slots, HD), 1)
    row_ids = lax.broadcasted_iota(jnp.int32, (slots, HD), 0)
    cos_full = jnp.cos(angles)
    sin_signed = jnp.where(col_ids < HD // 2, -1.0, 1.0) * jnp.sin(angles)
    cos_ref[...] = cos_full
    sin_ref[...] = sin_signed
    turned = turn(pair_ref[0:slots, :].astype(F32), cos_full, sin_signed).astype(BF16)
    marked = (row_ids >= count_ref[0]) & (col_ids == 0)
    value = jnp.where(marked, DEAD_MARK, pair_ref[slots : 2 * slots, :].astype(F32)).astype(BF16)
    pay_ref[0:slots, :] = turned
    pay_ref[slots : 2 * slots, :] = value
    chunk = stage.shape[0]
    for i in range(chunk):
        stage[i, 0:slots, :] = turned
        stage[i, slots : 2 * slots, :] = value
    copies = [
        pltpu.make_async_copy(stage, copies_ref.at[pl.ds(i * chunk, chunk)], sems.at[i])
        for i in range(copies_ref.shape[0] // chunk)
    ]
    for copy in copies:
        copy.start()
    for copy in copies:
        copy.wait()


def column_block(place_ref, at, parts, width):
    way = 1 - 2 * lax.rem(place_ref[0], 2)
    owner = lax.rem(place_ref[1] - tp_order(parts)[at] * way + 2 * parts, parts)
    return pl.ds(pl.multiple_of(owner * width, width), width)


def query_kernel(query_ref, cos_ref, sin_ref, out_ref):
    cos_full, sin_signed = cos_ref[...], sin_ref[...]
    for h in range(query_ref.shape[1] // HD):
        part = query_ref[:, h * HD : (h + 1) * HD].astype(F32)
        out_ref[:, h * HD : (h + 1) * HD] = turn(part, cos_full, sin_signed).astype(BF16)


def cotangent_kernel(place_ref, count_ref, weight_ref, logit_ref, cot_ref, grad_ref):
    slots = grad_ref.shape[0]
    gate = jnp.where(live_row(count_ref, slots), 1.0 / (1.0 + jnp.exp(-logit_ref[...])), 0.0)
    total = None
    parts, _, width = cot_ref.shape
    for step in range(parts):
        columns = column_block(place_ref, step, parts, width)
        part = matmul(cot_ref[step], weight_ref[:, columns], ((1,), (1,)))
        total = part if total is None else total + part
    grad_ref[...] = (total * as_column(gate)).astype(BF16)


def forward_kernel(place_ref, index_ref, own_ref, sibling_ref, grad_ref, pay_ref, piece_ref, part_ref, weight_ref, score_ref):
    slots = own_ref.shape[0]
    groups, keys, rows = score_ref.shape
    chunk = keys // slots
    me = place_ref[0]
    my_core = lax.rem(me, 2)
    my_chip = lax.div(me, 2)

    query = jnp.concatenate([stacked_heads(own_ref[...]), stacked_heads(sibling_ref[...])], axis=0)
    query_t = query.T.astype(BF16)
    index_row = index_ref[...].astype(F32)
    index_col = as_column(index_row)
    beyond = jnp.where(my_core == 0, 2.0 * TOK_DEV, -1.0)
    sibling_row = jnp.full((1, rows // 2), 1.0, F32) * beyond
    own_rows = rows // 2 // slots
    limit_row = jnp.concatenate([index_row] * own_rows + [sibling_row], axis=1)

    peak = jnp.full((1, rows), LOWEST, F32)
    for group in range(groups):
        blocks = pl.ds(group * chunk, chunk)
        scores = matmul(piece_ref[blocks, 0:slots, :].reshape(keys, HD), query_t, ((1,), (0,)))
        for i in range(chunk):
            chip = group * chunk + i
            reach = jnp.where(chip < my_chip, 0.0, LOWEST)
            first = piece_ref[chip, slots : 2 * slots, 0:1].astype(F32)
            bias = jnp.where(first > DEAD_LIMIT, LOWEST, reach)
            block = scores[i * slots : (i + 1) * slots, :] + bias
            score_ref[group, i * slots : (i + 1) * slots, :] = block
            peak = jnp.maximum(peak, jnp.max(block, axis=0, keepdims=True))

    own_keys, own_values = pay_ref[0:slots, :], pay_ref[slots : 2 * slots, :]
    own_scores = matmul(own_keys, query_t, ((1,), (0,)))
    own_scores = jnp.where(index_col <= limit_row, own_scores, LOWEST)
    own_scores = own_scores + jnp.where(own_values[:, 0:1].astype(F32) > DEAD_LIMIT, LOWEST, 0.0)
    own_at = pl.ds(pl.multiple_of(lax.rem(my_chip, chunk) * slots, slots), slots)
    score_ref[pl.ds(lax.div(my_chip, chunk), 1), own_at, :] = own_scores[None]
    peak = jnp.maximum(peak, jnp.max(own_scores, axis=0, keepdims=True))

    total = jnp.zeros((1, rows), F32)
    summed = jnp.zeros((HD, rows), F32)
    for group in range(groups):
        weights = jnp.exp2((score_ref[group] - peak) * FACTOR)
        total = total + jnp.sum(weights, axis=0, keepdims=True)
        weights = weights.astype(BF16)
        weight_ref[group] = weights
        values = piece_ref[pl.ds(group * chunk, chunk), slots : 2 * slots, :].reshape(keys, HD)
        summed = summed + matmul(values, weights, ((0,), (0,)))
    part_ref[0:HD, :] = summed
    row_ids = lax.broadcasted_iota(jnp.int32, (8, rows), 0)
    part_ref[HD : HD + 8, :] = jnp.where(row_ids == 0, peak, total)
    part_ref[HD + 8 : HD + 8 + slots, :] = grad_ref[...].astype(F32)


def backward_kernel(
    own_part, sibling_part, own_ref, sibling_ref, grad_ref, weight_ref, piece_ref, att_ref, delta_ref, dq_ref, dq_sibling_ref, out_ref, stage, sems
):
    slots = own_ref.shape[0]
    groups, keys, rows = weight_ref.shape
    chunk = keys // slots
    half = rows // 2
    heads = half // slots

    def swapped(at):
        return jnp.concatenate([sibling_part[at, half:rows], sibling_part[at, 0:half]], axis=1)

    stats = pl.ds(HD, 8)
    mine, theirs = own_part[stats, :], swapped(stats)
    peak = jnp.maximum(mine[0:1], theirs[0:1])
    mine_factor = jnp.exp2((mine[0:1] - peak) * FACTOR)
    their_factor = jnp.exp2((theirs[0:1] - peak) * FACTOR)
    inverse = 1.0 / (mine[1:2] * mine_factor + theirs[1:2] * their_factor)
    body = pl.ds(0, HD)
    mine_factor, their_factor = mine_factor * inverse, their_factor * inverse
    att_t = own_part[body, :] * mine_factor + swapped(body) * their_factor
    att_t = att_t.astype(BF16).astype(F32)
    att = att_t[:, 0:half].T.astype(BF16)
    for h in range(heads):
        att_ref[:, h * HD : (h + 1) * HD] = att[h * slots : (h + 1) * slots, :]

    query_t = jnp.concatenate([stacked_heads(own_ref[...]), stacked_heads(sibling_ref[...])], axis=0).T
    sibling_grad = sibling_part[HD + 8 : HD + 8 + slots, :]
    grad_t = jnp.concatenate([stacked_heads(grad_ref[...]), stacked_heads(sibling_grad)], axis=0).T
    grad_tb = grad_t.astype(BF16)
    delta = jnp.sum(att_t * grad_t, axis=0, keepdims=True)
    delta_ref[...] = jnp.broadcast_to(delta[:, 0:half], delta_ref.shape)

    query_scaled = (query_t * (mine_factor * SCALE)).astype(BF16)
    grad_scaled = (grad_t * mine_factor).astype(BF16)
    dq_t = jnp.zeros((HD, rows), F32)
    copies = []
    for group in range(groups):
        blocks = pl.ds(group * chunk, chunk)
        weights = weight_ref[group]
        values = piece_ref[blocks, slots : 2 * slots, :].reshape(keys, HD)
        grad_probs = matmul(values, grad_tb, ((1,), (0,)))
        grad_score = (weights.astype(F32) * (grad_probs - delta)).astype(BF16)
        key_part = matmul(grad_score, query_scaled, ((1,), (1,)))
        value_part = matmul(weights, grad_scaled, ((1,), (1,)))
        stage[blocks, 0:slots, :] = key_part.astype(BF16).reshape(chunk, slots, HD)
        stage[blocks, slots : 2 * slots, :] = value_part.astype(BF16).reshape(chunk, slots, HD)
        copies.append(pltpu.make_async_copy(stage.at[blocks], out_ref.at[blocks], sems.at[group]))
        copies[-1].start()
        dq_t = dq_t + matmul(piece_ref[blocks, 0:slots, :].reshape(keys, HD), grad_score, ((0,), (0,)))
    dq = (dq_t * (mine_factor * SCALE)).T
    dq_ref[...] = dq[0:half, :]
    dq_sibling_ref[...] = dq[half:rows, :].astype(BF16)
    for copy in copies:
        copy.wait()


def projection_kernel(place_ref, weight_ref, att_ref, delta_ref, *part_refs):
    slots = att_ref.shape[0]
    pair, _, width = part_refs[0].shape
    parts = pair * len(part_refs)
    rows = delta_ref.shape[1]
    delta = delta_ref[...]
    row_sum = delta[:, 0:slots]
    for h in range(1, rows // slots):
        row_sum = row_sum + delta[:, h * slots : (h + 1) * slots]
    extra = jnp.concatenate([row_sum, jnp.zeros((8, width - slots), F32)], axis=1)
    extra = jnp.concatenate([extra, extra], axis=0).astype(BF16)
    att = att_ref[...]
    for at in range(parts):
        columns = column_block(place_ref, at, parts, width)
        part_ref = part_refs[at // pair]
        part_ref[at % pair, 0:slots, :] = matmul(att, weight_ref[:, columns], ((1,), (0,))).astype(BF16)
        part_ref[at % pair, slots : slots + 16, :] = extra


def added_up(stack_ref):
    total = stack_ref[0].astype(F32)
    for step in range(1, stack_ref.shape[0]):
        total = total + stack_ref[step].astype(F32)
    return total


def update_kernel(count_ref, own_ref, landed_ref, logit_ref, index_ref, hidden_ref, update_ref, after_ref, grad_ref):
    slots = update_ref.shape[0]
    tokens = hidden_ref.shape[0]
    live = live_row(count_ref, slots)
    gate = 1.0 / (1.0 + jnp.exp(-logit_ref[...]))
    total = own_ref[0].astype(F32) + landed_ref[0].astype(F32)
    update = (total[0:slots, :] * as_column(jnp.where(live, gate, 0.0))).astype(BF16)
    update_ref[...] = update
    token_ids = lax.broadcasted_iota(jnp.int32, (tokens, slots), 0)
    chosen = jnp.where(token_ids == index_ref[...], 1.0, 0.0).astype(BF16)
    added = matmul(chosen, update, ((1,), (0,)))
    after_ref[...] = (hidden_ref[...].astype(F32) + added).astype(BF16)
    grad_ref[...] = jnp.where(live, total[slots : slots + 1, 0:slots] * (1.0 - gate), 0.0)


def query_grad_kernel(cos_ref, sin_ref, own_ref, arrived_ref, dq_ref):
    slots = dq_ref.shape[0]
    total = own_ref[...] + arrived_ref[...].astype(F32)
    for h in range(dq_ref.shape[1] // HD):
        back = turn(total[h * slots : (h + 1) * slots, :], cos_ref[...], -sin_ref[...])
        dq_ref[:, h * HD : (h + 1) * HD] = back.astype(BF16)


def finish_kernel(cos_ref, sin_ref, landed_ref, dk_ref, dv_ref):
    slots = dk_ref.shape[0]
    total = added_up(landed_ref)
    dk_ref[...] = turn(total[0:slots, :], cos_ref[...], -sin_ref[...]).astype(BF16)
    dv_ref[...] = total[slots : 2 * slots, :].astype(BF16)


def tp_shifts(parts):
    half = parts // 2
    return [shift if 2 * shift <= half else shift - half for shift in range(1, half)]


def tp_order(parts):
    return [shift + step for shift in [0] + tp_shifts(parts) for step in (0, parts // 2)]


def on_device(
    dims,
    tp_count,
    queries,
    key_vectors,
    value_vectors,
    out_weight,
    router_logit,
    chosen_index,
    chosen_count,
    out_cotangent,
    hidden_state,
):
    ny, nx, nc = dims
    slots, width = queries.shape
    heads = width // HD
    rows = nc * heads * slots
    blocks = ny * nx
    chunk = min(8, blocks)

    def exchange(array):
        groups = [[chip * nc + core for chip in range(blocks)] for core in range(nc)]
        return lax.all_to_all(array, "ctx", 0, 0, axis_index_groups=groups, tiled=True)

    def to_sibling(array):
        return lax.ppermute(array, "ctx", [(i, i ^ 1) for i in range(ny * nx * nc)])

    def tp_send(array, shift):
        pairs = []
        for shard in range(ny * nx * nc):
            for part in range(tp_count):
                to = (part + shift * (1 - 2 * (shard % nc))) % tp_count
                pairs.append((shard * tp_count + part, shard * tp_count + to))
        return lax.ppermute(array, ("ctx", "tp"), pairs)

    def summed(first, second):
        return (first.astype(F32) + second.astype(F32)).astype(BF16)

    my_shard = lax.axis_index("ctx").astype(jnp.int32)
    place = jnp.stack([my_shard, lax.axis_index("tp").astype(jnp.int32)])
    index_row = chosen_index[None, :]
    logit_row = router_logit[None, :]
    half = jnp.arange(HD // 2, dtype=F32)
    frequency = ROTARY_BASE ** (-(half * 2.0 / HD))
    frequency = jnp.concatenate([frequency, frequency])[None, :]

    payload, payloads, cos_full, sin_signed = call(
        payload_kernel,
        [
            jax.ShapeDtypeStruct((2 * slots, HD), BF16),
            jax.ShapeDtypeStruct((blocks, 2 * slots, HD), BF16),
            jax.ShapeDtypeStruct((slots, HD), F32),
            jax.ShapeDtypeStruct((slots, HD), F32),
        ],
        [SMEM] + [VMEM] * 3,
        [pltpu.VMEM((chunk, 2 * slots, HD), BF16), pltpu.SemaphoreType.DMA((blocks // chunk,))],
        out_specs=[VMEM, HBM, VMEM, VMEM],
    )(
        chosen_count,
        jnp.concatenate([key_vectors, value_vectors], axis=0),
        (my_shard * TOK_DEV + chosen_index).astype(F32)[None, :],
        frequency,
    )
    pieces = exchange(payloads)

    own_queries = call(
        query_kernel, jax.ShapeDtypeStruct((slots, width), BF16), [VMEM] * 3
    )(queries, cos_full, sin_signed)
    sibling_queries = to_sibling(own_queries)
    pair = jnp.concatenate([out_cotangent[None], tp_send(out_cotangent[None], tp_count // 2)], axis=0)
    cot = jnp.concatenate([pair] + [tp_send(pair, shift) for shift in tp_shifts(tp_count)], axis=0)

    grad_attention = call(
        cotangent_kernel, jax.ShapeDtypeStruct((slots, width), BF16), [SMEM] * 2 + [VMEM] * 3
    )(place, chosen_count, out_weight, logit_row, cot)

    scored = (blocks // chunk, chunk * slots, rows)
    part, weights = call(
        forward_kernel,
        [
            jax.ShapeDtypeStruct((HD + 8 + slots, rows), F32),
            jax.ShapeDtypeStruct(scored, BF16),
        ],
        [SMEM] + [VMEM] * 6,
        [pltpu.VMEM(scored, F32)],
    )(place, index_row, own_queries, sibling_queries, grad_attention, payload, pieces)
    sibling_part = to_sibling(part)
    attention, delta, dq_own, dq_sibling, outs = call(
        backward_kernel,
        [
            jax.ShapeDtypeStruct((slots, width), BF16),
            jax.ShapeDtypeStruct((8, rows // 2), F32),
            jax.ShapeDtypeStruct((rows // 2, HD), F32),
            jax.ShapeDtypeStruct((rows // 2, HD), BF16),
            jax.ShapeDtypeStruct((blocks, 2 * slots, HD), BF16),
        ],
        [VMEM] * 7,
        [pltpu.VMEM((blocks, 2 * slots, HD), BF16), pltpu.SemaphoreType.DMA((blocks // chunk,))],
        out_specs=[VMEM] * 4 + [HBM],
    )(part, sibling_part, own_queries, sibling_queries, grad_attention, weights, pieces)
    landed = exchange(outs)

    shares = call(
        projection_kernel,
        [jax.ShapeDtypeStruct((2, slots + 16, width), BF16)] * (tp_count // 2),
        [SMEM] + [VMEM] * 3,
    )(place, out_weight, attention, delta)
    dq_arrived = to_sibling(dq_sibling)
    grad_queries = call(
        query_grad_kernel, jax.ShapeDtypeStruct((slots, width), BF16), [VMEM] * 4
    )(cos_full, sin_signed, dq_own, dq_arrived)
    arrived = [tp_send(share, -shift) for share, shift in zip(shares[1:], tp_shifts(tp_count))]
    arrived, grad_queries = lax.optimization_barrier((arrived, grad_queries))
    shares = functools.reduce(jnp.add, [part.astype(F32) for part in [shares[0]] + arrived]).astype(BF16)
    near = shares[:1]
    arrived = tp_send(shares[1:], -(tp_count // 2))

    grad_keys, grad_values = call(
        finish_kernel, [jax.ShapeDtypeStruct((slots, HD), BF16)] * 2, [VMEM] * 3
    )(cos_full, sin_signed, landed)

    update, hidden_after, grad_row = call(
        update_kernel,
        [
            jax.ShapeDtypeStruct((slots, width), BF16),
            jax.ShapeDtypeStruct(hidden_state.shape, BF16),
            jax.ShapeDtypeStruct((1, slots), F32),
        ],
        [SMEM] + [VMEM] * 5,
    )(chosen_count, near, arrived, logit_row, index_row, hidden_state)
    return (update, grad_queries, grad_keys, grad_values, grad_row[0], hidden_after)


def layout(shards):
    nx = 4 if shards >= 16 else 2
    return (shards // (nx * 2), nx, 2)


def solution(mesh):
    shards, tp_count = mesh.shape["ctx"], mesh.shape["tp"]
    placed = (
        P("ctx", "tp"),
        P("ctx", "tp"),
        P("ctx", "tp"),
        P("tp", None),
        P("ctx"),
        P("ctx"),
        P("ctx"),
        P("ctx", "tp"),
        P("ctx", "tp"),
    )
    return jax.shard_map(
        functools.partial(on_device, layout(shards), tp_count),
        mesh=mesh,
        in_specs=placed,
        out_specs=(
            P("ctx", "tp"),
            P("ctx", "tp"),
            P("ctx", "tp"),
            P("ctx", "tp"),
            P("ctx"),
            P("ctx", "tp"),
        ),
        check_vma=False,
    )
```

```python
import functools
import math

import jax
import jax.numpy as jnp
from jax import lax
from jax.experimental import pallas as pl
from jax.experimental.pallas import tpu as pltpu
from jax.sharding import PartitionSpec as P

HD = 128
TOK_DEV = 512
ROTARY_BASE = 500000.0
LOWEST = -1e30
DEAD_MARK = 1024.0
DEAD_LIMIT = 512.0
SCALE = 1.0 / math.sqrt(HD)
FACTOR = SCALE * math.log2(math.e)
F32 = jnp.float32
BF16 = jnp.bfloat16

VMEM = pl.BlockSpec(memory_space=pltpu.VMEM)
SMEM = pl.BlockSpec(memory_space=pltpu.SMEM)
HBM = pl.BlockSpec(memory_space=pltpu.HBM)


def call(kernel, out_shape, in_specs, scratch=(), limit=32, out_specs=None):
    return pl.pallas_call(
        kernel,
        out_shape=out_shape,
        in_specs=in_specs,
        out_specs=out_specs or jax.tree.map(lambda _: VMEM, out_shape),
        scratch_shapes=list(scratch),
        compiler_params=pltpu.CompilerParams(vmem_limit_bytes=limit * 1024 * 1024),
    )


def turn(rows, cos_full, sin_signed):
    return rows * cos_full + pltpu.roll(rows, HD // 2, 1) * sin_signed


def matmul(a, b, dims):
    return lax.dot_general(a, b, (dims, ((), ())), preferred_element_type=F32)


def as_column(row):
    count = row.shape[1]
    down = lax.broadcasted_iota(jnp.int32, (count, count), 0)
    across = lax.broadcasted_iota(jnp.int32, (count, count), 1)
    return jnp.sum(jnp.where(down == across, row, 0.0), axis=1, keepdims=True)


def live_row(count_ref, slots):
    return lax.broadcasted_iota(jnp.int32, (1, slots), 1) < count_ref[0]


def stacked_heads(field):
    heads = field.shape[1] // HD
    return jnp.concatenate([field[:, h * HD : (h + 1) * HD].astype(F32) for h in range(heads)], axis=0)


def payload_kernel(count_ref, pair_ref, position_ref, frequency_ref, pay_ref, copies_ref, cos_ref, sin_ref, stage, sems):
    slots = cos_ref.shape[0]
    angles = as_column(position_ref[...]) * frequency_ref[...]
    col_ids = lax.broadcasted_iota(jnp.int32, (slots, HD), 1)
    row_ids = lax.broadcasted_iota(jnp.int32, (slots, HD), 0)
    cos_full = jnp.cos(angles)
    sin_signed = jnp.where(col_ids < HD // 2, -1.0, 1.0) * jnp.sin(angles)
    cos_ref[...] = cos_full
    sin_ref[...] = sin_signed
    turned = turn(pair_ref[0:slots, :].astype(F32), cos_full, sin_signed).astype(BF16)
    marked = (row_ids >= count_ref[0]) & (col_ids == 0)
    value = jnp.where(marked, DEAD_MARK, pair_ref[slots : 2 * slots, :].astype(F32)).astype(BF16)
    pay_ref[0:slots, :] = turned
    pay_ref[slots : 2 * slots, :] = value
    chunk = stage.shape[0]
    for i in range(chunk):
        stage[i, 0:slots, :] = turned
        stage[i, slots : 2 * slots, :] = value
    copies = [
        pltpu.make_async_copy(stage, copies_ref.at[pl.ds(i * chunk, chunk)], sems.at[i])
        for i in range(copies_ref.shape[0] // chunk)
    ]
    for copy in copies:
        copy.start()
    for copy in copies:
        copy.wait()


def column_block(place_ref, shift, parts, width):
    way = 1 - 2 * lax.rem(place_ref[0], 2)
    owner = lax.rem(place_ref[1] - shift * way + 2 * parts, parts)
    return pl.ds(pl.multiple_of(owner * width, width), width)


def query_kernel(count_ref, query_ref, cos_ref, sin_ref, logit_ref, cot_ref, out_ref, gate_ref, cot_out):
    cos_full, sin_signed = cos_ref[...], sin_ref[...]
    for h in range(query_ref.shape[1] // HD):
        part = query_ref[:, h * HD : (h + 1) * HD].astype(F32)
        out_ref[:, h * HD : (h + 1) * HD] = turn(part, cos_full, sin_signed).astype(BF16)
    slots = query_ref.shape[0]
    gate = jnp.where(live_row(count_ref, slots), 1.0 / (1.0 + jnp.exp(-logit_ref[...])), 0.0)
    gate_ref[...] = jnp.broadcast_to(as_column(gate), gate_ref.shape)
    cot_out[...] = cot_ref[...]


def cotangent_kernel(place_ref, weight_ref, gate_ref, *refs):
    pieces, grad_ref = refs[:-1], refs[-1]
    parts = len(pieces)
    width = grad_ref.shape[1]
    total = None
    for piece, shift in zip(pieces, [0] + direct_shifts(parts)):
        columns = column_block(place_ref, shift, parts, width)
        part = matmul(piece[...], weight_ref[:, columns], ((1,), (1,)))
        total = part if total is None else total + part
    grad_ref[...] = (total * gate_ref[:, 0:1]).astype(BF16)


def forward_kernel(place_ref, index_ref, own_ref, sibling_ref, grad_ref, pay_ref, piece_ref, part_ref, weight_ref, score_ref):
    slots = own_ref.shape[0]
    groups, keys, rows = score_ref.shape
    chunk = keys // slots
    me = place_ref[0]
    my_core = lax.rem(me, 2)
    my_chip = lax.div(me, 2)

    query = jnp.concatenate([stacked_heads(own_ref[...]), stacked_heads(sibling_ref[...])], axis=0)
    query_t = query.T.astype(BF16)
    index_row = index_ref[...].astype(F32)
    index_col = as_column(index_row)
    beyond = jnp.where(my_core == 0, 2.0 * TOK_DEV, -1.0)
    sibling_row = jnp.full((1, rows // 2), 1.0, F32) * beyond
    own_rows = rows // 2 // slots
    limit_row = jnp.concatenate([index_row] * own_rows + [sibling_row], axis=1)

    peak = jnp.full((1, rows), LOWEST, F32)
    for group in range(groups):
        blocks = pl.ds(group * chunk, chunk)
        scores = matmul(piece_ref[blocks, 0:slots, :].reshape(keys, HD), query_t, ((1,), (0,)))
        for i in range(chunk):
            chip = group * chunk + i
            reach = jnp.where(chip < my_chip, 0.0, LOWEST)
            first = piece_ref[chip, slots : 2 * slots, 0:1].astype(F32)
            bias = jnp.where(first > DEAD_LIMIT, LOWEST, reach)
            block = scores[i * slots : (i + 1) * slots, :] + bias
            score_ref[group, i * slots : (i + 1) * slots, :] = block
            peak = jnp.maximum(peak, jnp.max(block, axis=0, keepdims=True))

    own_keys, own_values = pay_ref[0:slots, :], pay_ref[slots : 2 * slots, :]
    own_scores = matmul(own_keys, query_t, ((1,), (0,)))
    own_scores = jnp.where(index_col <= limit_row, own_scores, LOWEST)
    own_scores = own_scores + jnp.where(own_values[:, 0:1].astype(F32) > DEAD_LIMIT, LOWEST, 0.0)
    own_at = pl.ds(pl.multiple_of(lax.rem(my_chip, chunk) * slots, slots), slots)
    score_ref[pl.ds(lax.div(my_chip, chunk), 1), own_at, :] = own_scores[None]
    peak = jnp.maximum(peak, jnp.max(own_scores, axis=0, keepdims=True))

    total = jnp.zeros((1, rows), F32)
    summed = jnp.zeros((HD, rows), F32)
    for group in range(groups):
        weights = jnp.exp2((score_ref[group] - peak) * FACTOR)
        total = total + jnp.sum(weights, axis=0, keepdims=True)
        weights = weights.astype(BF16)
        weight_ref[group] = weights
        values = piece_ref[pl.ds(group * chunk, chunk), slots : 2 * slots, :].reshape(keys, HD)
        summed = summed + matmul(values, weights, ((0,), (0,)))
    part_ref[0:HD, :] = summed
    row_ids = lax.broadcasted_iota(jnp.int32, (8, rows), 0)
    part_ref[HD : HD + 8, :] = jnp.where(row_ids == 0, peak, total)
    part_ref[HD + 8 : HD + 8 + slots, :] = grad_ref[...].astype(F32)


def backward_kernel(
    own_part, sibling_part, own_ref, sibling_ref, grad_ref, weight_ref, piece_ref, att_ref, delta_ref, dq_ref, dq_sibling_ref, out_ref, stage, sems
):
    slots = own_ref.shape[0]
    groups, keys, rows = weight_ref.shape
    chunk = keys // slots
    half = rows // 2
    heads = half // slots

    def swapped(at):
        return jnp.concatenate([sibling_part[at, half:rows], sibling_part[at, 0:half]], axis=1)

    stats = pl.ds(HD, 8)
    mine, theirs = own_part[stats, :], swapped(stats)
    peak = jnp.maximum(mine[0:1], theirs[0:1])
    mine_factor = jnp.exp2((mine[0:1] - peak) * FACTOR)
    their_factor = jnp.exp2((theirs[0:1] - peak) * FACTOR)
    inverse = 1.0 / (mine[1:2] * mine_factor + theirs[1:2] * their_factor)
    body = pl.ds(0, HD)
    mine_factor, their_factor = mine_factor * inverse, their_factor * inverse
    att_t = own_part[body, :] * mine_factor + swapped(body) * their_factor
    att_t = att_t.astype(BF16).astype(F32)
    att = att_t[:, 0:half].T.astype(BF16)
    for h in range(heads):
        att_ref[:, h * HD : (h + 1) * HD] = att[h * slots : (h + 1) * slots, :]

    query_t = jnp.concatenate([stacked_heads(own_ref[...]), stacked_heads(sibling_ref[...])], axis=0).T
    sibling_grad = sibling_part[HD + 8 : HD + 8 + slots, :]
    grad_t = jnp.concatenate([stacked_heads(grad_ref[...]), stacked_heads(sibling_grad)], axis=0).T
    grad_tb = grad_t.astype(BF16)
    delta = jnp.sum(att_t * grad_t, axis=0, keepdims=True)
    delta_ref[...] = jnp.broadcast_to(delta[:, 0:half], delta_ref.shape)

    query_scaled = (query_t * (mine_factor * SCALE)).astype(BF16)
    grad_scaled = (grad_t * mine_factor).astype(BF16)
    dq_t = jnp.zeros((HD, rows), F32)
    copies = []
    for group in range(groups):
        blocks = pl.ds(group * chunk, chunk)
        weights = weight_ref[group]
        values = piece_ref[blocks, slots : 2 * slots, :].reshape(keys, HD)
        grad_probs = matmul(values, grad_tb, ((1,), (0,)))
        grad_score = (weights.astype(F32) * (grad_probs - delta)).astype(BF16)
        key_part = matmul(grad_score, query_scaled, ((1,), (1,)))
        value_part = matmul(weights, grad_scaled, ((1,), (1,)))
        stage[blocks, 0:slots, :] = key_part.astype(BF16).reshape(chunk, slots, HD)
        stage[blocks, slots : 2 * slots, :] = value_part.astype(BF16).reshape(chunk, slots, HD)
        copies.append(pltpu.make_async_copy(stage.at[blocks], out_ref.at[blocks], sems.at[group]))
        copies[-1].start()
        dq_t = dq_t + matmul(piece_ref[blocks, 0:slots, :].reshape(keys, HD), grad_score, ((0,), (0,)))
    dq = (dq_t * (mine_factor * SCALE)).T
    dq_ref[...] = dq[0:half, :]
    dq_sibling_ref[...] = dq[half:rows, :].astype(BF16)
    for copy in copies:
        copy.wait()


def projection_kernel(place_ref, weight_ref, att_ref, delta_ref, *part_refs):
    slots = att_ref.shape[0]
    pair, _, width = part_refs[0].shape
    parts = pair * len(part_refs)
    rows = delta_ref.shape[1]
    delta = delta_ref[...]
    row_sum = delta[:, 0:slots]
    for h in range(1, rows // slots):
        row_sum = row_sum + delta[:, h * slots : (h + 1) * slots]
    extra = jnp.concatenate([row_sum, jnp.zeros((8, width - slots), F32)], axis=1)
    extra = jnp.concatenate([extra, extra], axis=0).astype(BF16)
    att = att_ref[...]
    for at in range(parts):
        columns = column_block(place_ref, tp_order(parts)[at], parts, width)
        part_ref = part_refs[at // pair]
        part_ref[at % pair, 0:slots, :] = matmul(att, weight_ref[:, columns], ((1,), (0,))).astype(BF16)
        part_ref[at % pair, slots : slots + 16, :] = extra


def added_up(stack_ref):
    total = stack_ref[0].astype(F32)
    for step in range(1, stack_ref.shape[0]):
        total = total + stack_ref[step].astype(F32)
    return total


def update_kernel(count_ref, own_ref, landed_ref, logit_ref, index_ref, hidden_ref, update_ref, after_ref, grad_ref):
    slots = update_ref.shape[0]
    tokens = hidden_ref.shape[0]
    live = live_row(count_ref, slots)
    gate = 1.0 / (1.0 + jnp.exp(-logit_ref[...]))
    total = own_ref[0].astype(F32) + landed_ref[0].astype(F32)
    update = (total[0:slots, :] * as_column(jnp.where(live, gate, 0.0))).astype(BF16)
    update_ref[...] = update
    token_ids = lax.broadcasted_iota(jnp.int32, (tokens, slots), 0)
    chosen = jnp.where(token_ids == index_ref[...], 1.0, 0.0).astype(BF16)
    added = matmul(chosen, update, ((1,), (0,)))
    after_ref[...] = (hidden_ref[...].astype(F32) + added).astype(BF16)
    grad_ref[...] = jnp.where(live, total[slots : slots + 1, 0:slots] * (1.0 - gate), 0.0)


def query_grad_kernel(cos_ref, sin_ref, own_ref, arrived_ref, dq_ref):
    slots = dq_ref.shape[0]
    total = own_ref[...] + arrived_ref[...].astype(F32)
    for h in range(dq_ref.shape[1] // HD):
        back = turn(total[h * slots : (h + 1) * slots, :], cos_ref[...], -sin_ref[...])
        dq_ref[:, h * HD : (h + 1) * HD] = back.astype(BF16)


def finish_kernel(cos_ref, sin_ref, landed_ref, dk_ref, dv_ref):
    slots = dk_ref.shape[0]
    total = added_up(landed_ref)
    dk_ref[...] = turn(total[0:slots, :], cos_ref[...], -sin_ref[...]).astype(BF16)
    dv_ref[...] = total[slots : 2 * slots, :].astype(BF16)


def direct_shifts(parts):
    shifts = []
    for distance in range(parts // 2, 0, -1):
        shifts += [distance] if 2 * distance == parts else [distance, -distance]
    return shifts


def tp_shifts(parts):
    half = parts // 2
    return [shift if 2 * shift <= half else shift - half for shift in range(1, half)]


def tp_order(parts):
    return [shift + step for shift in [0] + tp_shifts(parts) for step in (0, parts // 2)]


def on_device(
    dims,
    tp_count,
    queries,
    key_vectors,
    value_vectors,
    out_weight,
    router_logit,
    chosen_index,
    chosen_count,
    out_cotangent,
    hidden_state,
):
    ny, nx, nc = dims
    slots, width = queries.shape
    heads = width // HD
    rows = nc * heads * slots
    blocks = ny * nx
    chunk = min(8, blocks)

    def exchange(array):
        groups = [[chip * nc + core for chip in range(blocks)] for core in range(nc)]
        return lax.all_to_all(array, "ctx", 0, 0, axis_index_groups=groups, tiled=True)

    def to_sibling(array):
        return lax.ppermute(array, "ctx", [(i, i ^ 1) for i in range(ny * nx * nc)])

    def tp_send(array, shift):
        pairs = []
        for shard in range(ny * nx * nc):
            for part in range(tp_count):
                to = (part + shift * (1 - 2 * (shard % nc))) % tp_count
                pairs.append((shard * tp_count + part, shard * tp_count + to))
        return lax.ppermute(array, ("ctx", "tp"), pairs)

    def summed(first, second):
        return (first.astype(F32) + second.astype(F32)).astype(BF16)

    my_shard = lax.axis_index("ctx").astype(jnp.int32)
    place = jnp.stack([my_shard, lax.axis_index("tp").astype(jnp.int32)])
    index_row = chosen_index[None, :]
    logit_row = router_logit[None, :]
    half = jnp.arange(HD // 2, dtype=F32)
    frequency = ROTARY_BASE ** (-(half * 2.0 / HD))
    frequency = jnp.concatenate([frequency, frequency])[None, :]

    payload, payloads, cos_full, sin_signed = call(
        payload_kernel,
        [
            jax.ShapeDtypeStruct((2 * slots, HD), BF16),
            jax.ShapeDtypeStruct((blocks, 2 * slots, HD), BF16),
            jax.ShapeDtypeStruct((slots, HD), F32),
            jax.ShapeDtypeStruct((slots, HD), F32),
        ],
        [SMEM] + [VMEM] * 3,
        [pltpu.VMEM((chunk, 2 * slots, HD), BF16), pltpu.SemaphoreType.DMA((blocks // chunk,))],
        out_specs=[VMEM, HBM, VMEM, VMEM],
    )(
        chosen_count,
        jnp.concatenate([key_vectors, value_vectors], axis=0),
        (my_shard * TOK_DEV + chosen_index).astype(F32)[None, :],
        frequency,
    )
    pieces = exchange(payloads)

    own_queries, gate, own_cot = call(
        query_kernel,
        [
            jax.ShapeDtypeStruct((slots, width), BF16),
            jax.ShapeDtypeStruct((slots, HD), F32),
            jax.ShapeDtypeStruct((slots, width), BF16),
        ],
        [SMEM] + [VMEM] * 5,
    )(chosen_count, queries, cos_full, sin_signed, logit_row, out_cotangent)
    sibling_queries = to_sibling(own_queries)

    cot = [own_cot] + [tp_send(out_cotangent, shift) for shift in direct_shifts(tp_count)]
    grad_attention = call(
        cotangent_kernel,
        jax.ShapeDtypeStruct((slots, width), BF16),
        [SMEM] + [VMEM] * (2 + tp_count),
    )(place, out_weight, gate, *cot)

    scored = (blocks // chunk, chunk * slots, rows)
    part, weights = call(
        forward_kernel,
        [
            jax.ShapeDtypeStruct((HD + 8 + slots, rows), F32),
            jax.ShapeDtypeStruct(scored, BF16),
        ],
        [SMEM] + [VMEM] * 6,
        [pltpu.VMEM(scored, F32)],
    )(place, index_row, own_queries, sibling_queries, grad_attention, payload, pieces)
    sibling_part = to_sibling(part)
    attention, delta, dq_own, dq_sibling, outs = call(
        backward_kernel,
        [
            jax.ShapeDtypeStruct((slots, width), BF16),
            jax.ShapeDtypeStruct((8, rows // 2), F32),
            jax.ShapeDtypeStruct((rows // 2, HD), F32),
            jax.ShapeDtypeStruct((rows // 2, HD), BF16),
            jax.ShapeDtypeStruct((blocks, 2 * slots, HD), BF16),
        ],
        [VMEM] * 7,
        [pltpu.VMEM((blocks, 2 * slots, HD), BF16), pltpu.SemaphoreType.DMA((blocks // chunk,))],
        out_specs=[VMEM] * 4 + [HBM],
    )(part, sibling_part, own_queries, sibling_queries, grad_attention, weights, pieces)
    landed = exchange(outs)

    shares = call(
        projection_kernel,
        [jax.ShapeDtypeStruct((2, slots + 16, width), BF16)] * (tp_count // 2),
        [SMEM] + [VMEM] * 3,
    )(place, out_weight, attention, delta)
    dq_arrived = to_sibling(dq_sibling)
    grad_queries = call(
        query_grad_kernel, jax.ShapeDtypeStruct((slots, width), BF16), [VMEM] * 4
    )(cos_full, sin_signed, dq_own, dq_arrived)
    arrived = [tp_send(share, -shift) for share, shift in zip(shares[1:], tp_shifts(tp_count))]
    shares = functools.reduce(jnp.add, [part.astype(F32) for part in [shares[0]] + arrived]).astype(BF16)
    near = shares[:1]
    arrived = tp_send(shares[1:], -(tp_count // 2))

    grad_keys, grad_values = call(
        finish_kernel, [jax.ShapeDtypeStruct((slots, HD), BF16)] * 2, [VMEM] * 3
    )(cos_full, sin_signed, landed)

    update, hidden_after, grad_row = call(
        update_kernel,
        [
            jax.ShapeDtypeStruct((slots, width), BF16),
            jax.ShapeDtypeStruct(hidden_state.shape, BF16),
            jax.ShapeDtypeStruct((1, slots), F32),
        ],
        [SMEM] + [VMEM] * 5,
    )(chosen_count, near, arrived, logit_row, index_row, hidden_state)
    return (update, grad_queries, grad_keys, grad_values, grad_row[0], hidden_after)


def layout(shards):
    nx = 4 if shards >= 16 else 2
    return (shards // (nx * 2), nx, 2)


def solution(mesh):
    shards, tp_count = mesh.shape["ctx"], mesh.shape["tp"]
    placed = (
        P("ctx", "tp"),
        P("ctx", "tp"),
        P("ctx", "tp"),
        P("tp", None),
        P("ctx"),
        P("ctx"),
        P("ctx"),
        P("ctx", "tp"),
        P("ctx", "tp"),
    )
    return jax.shard_map(
        functools.partial(on_device, layout(shards), tp_count),
        mesh=mesh,
        in_specs=placed,
        out_specs=(
            P("ctx", "tp"),
            P("ctx", "tp"),
            P("ctx", "tp"),
            P("ctx", "tp"),
            P("ctx"),
            P("ctx", "tp"),
        ),
        check_vma=False,
    )
```

```python
import functools
import math

import jax
import jax.numpy as jnp
from jax import lax
from jax.experimental import pallas as pl
from jax.experimental.pallas import tpu as pltpu
from jax.sharding import PartitionSpec as P

HD = 128
TOK_DEV = 512
ROTARY_BASE = 500000.0
LOWEST = -1e30
DEAD_MARK = 1024.0
DEAD_LIMIT = 512.0
SCALE = 1.0 / math.sqrt(HD)
FACTOR = SCALE * math.log2(math.e)
F32 = jnp.float32
BF16 = jnp.bfloat16

VMEM = pl.BlockSpec(memory_space=pltpu.VMEM)
SMEM = pl.BlockSpec(memory_space=pltpu.SMEM)
HBM = pl.BlockSpec(memory_space=pltpu.HBM)


def call(kernel, out_shape, in_specs, scratch=(), limit=32, out_specs=None):
    return pl.pallas_call(
        kernel,
        out_shape=out_shape,
        in_specs=in_specs,
        out_specs=out_specs or jax.tree.map(lambda _: VMEM, out_shape),
        scratch_shapes=list(scratch),
        compiler_params=pltpu.CompilerParams(vmem_limit_bytes=limit * 1024 * 1024),
    )


def turn(rows, cos_full, sin_signed):
    return rows * cos_full + pltpu.roll(rows, HD // 2, 1) * sin_signed


def matmul(a, b, dims):
    return lax.dot_general(a, b, (dims, ((), ())), preferred_element_type=F32)


def as_column(row):
    count = row.shape[1]
    down = lax.broadcasted_iota(jnp.int32, (count, count), 0)
    across = lax.broadcasted_iota(jnp.int32, (count, count), 1)
    return jnp.sum(jnp.where(down == across, row, 0.0), axis=1, keepdims=True)


def live_row(count_ref, slots):
    return lax.broadcasted_iota(jnp.int32, (1, slots), 1) < count_ref[0]


def stacked_heads(field):
    heads = field.shape[1] // HD
    return jnp.concatenate([field[:, h * HD : (h + 1) * HD].astype(F32) for h in range(heads)], axis=0)


def payload_kernel(place_ref, count_ref, pair_ref, frequency_ref, pay_ref, copies_ref, cos_ref, sin_ref, stage, sems):
    slots = cos_ref.shape[0]
    index = pair_ref[2 * slots : 2 * slots + 8, 0:slots].astype(F32)
    position = 2.0 * index[0:1] + index[1:2] + (place_ref[0] * TOK_DEV).astype(F32)
    angles = as_column(position) * frequency_ref[...]
    col_ids = lax.broadcasted_iota(jnp.int32, (slots, HD), 1)
    row_ids = lax.broadcasted_iota(jnp.int32, (slots, HD), 0)
    cos_full = jnp.cos(angles)
    sin_signed = jnp.where(col_ids < HD // 2, -1.0, 1.0) * jnp.sin(angles)
    cos_ref[...] = cos_full
    sin_ref[...] = sin_signed
    turned = turn(pair_ref[0:slots, :].astype(F32), cos_full, sin_signed).astype(BF16)
    marked = (row_ids >= count_ref[0]) & (col_ids == 0)
    value = jnp.where(marked, DEAD_MARK, pair_ref[slots : 2 * slots, :].astype(F32)).astype(BF16)
    pay_ref[0:slots, :] = turned
    pay_ref[slots : 2 * slots, :] = value
    chunk = stage.shape[0]
    for i in range(chunk):
        stage[i, 0:slots, :] = turned
        stage[i, slots : 2 * slots, :] = value
    copies = [
        pltpu.make_async_copy(stage, copies_ref.at[pl.ds(i * chunk, chunk)], sems.at[i])
        for i in range(copies_ref.shape[0] // chunk)
    ]
    for copy in copies:
        copy.start()
    for copy in copies:
        copy.wait()


def column_block(place_ref, shift, parts, width):
    way = 1 - 2 * lax.rem(place_ref[0], 2)
    owner = lax.rem(place_ref[1] - shift * way + 2 * parts, parts)
    return pl.ds(pl.multiple_of(owner * width, width), width)


def query_kernel(count_ref, query_ref, cos_ref, sin_ref, logit_ref, out_ref, gate_ref):
    cos_full, sin_signed = cos_ref[...], sin_ref[...]
    for h in range(query_ref.shape[1] // HD):
        part = query_ref[:, h * HD : (h + 1) * HD].astype(F32)
        out_ref[:, h * HD : (h + 1) * HD] = turn(part, cos_full, sin_signed).astype(BF16)
    slots = query_ref.shape[0]
    gate = jnp.where(live_row(count_ref, slots), 1.0 / (1.0 + jnp.exp(-logit_ref[...])), 0.0)
    gate_ref[...] = jnp.broadcast_to(as_column(gate), gate_ref.shape)


def weight_copies(place_ref, weight_ref, held, sems):
    parts, _, width = held.shape
    copies = []
    for at, shift in enumerate(tp_order(parts)):
        columns = column_block(place_ref, shift, parts, width)
        copies.append(pltpu.make_async_copy(weight_ref.at[:, columns], held.at[at], sems.at[at]))
    for copy in copies:
        copy.start()
    return copies


def cotangent_kernel(place_ref, weight_ref, gate_ref, pair_ref, *refs):
    pieces, (grad_ref, held, sems) = (pair_ref,) + refs[:-3], refs[-3:]
    copies = weight_copies(place_ref, weight_ref, held, sems)
    total = None
    for at, copy in enumerate(copies):
        copy.wait()
        part = matmul(pieces[at // 2][at % 2], held[at], ((1,), (1,)))
        total = part if total is None else total + part
    grad_ref[...] = (total * gate_ref[:, 0:1]).astype(BF16)


def forward_kernel(place_ref, index_ref, own_ref, sibling_ref, grad_ref, pay_ref, piece_ref, part_ref, weight_ref, score_ref):
    slots = own_ref.shape[0]
    groups, keys, rows = score_ref.shape
    chunk = keys // slots
    me = place_ref[0]
    my_core = lax.rem(me, 2)
    my_chip = lax.div(me, 2)

    query = jnp.concatenate([stacked_heads(own_ref[...]), stacked_heads(sibling_ref[...])], axis=0)
    query_t = query.T.astype(BF16)
    index_row = index_ref[...].astype(F32)
    index_col = as_column(index_row)
    beyond = jnp.where(my_core == 0, 2.0 * TOK_DEV, -1.0)
    sibling_row = jnp.full((1, rows // 2), 1.0, F32) * beyond
    own_rows = rows // 2 // slots
    limit_row = jnp.concatenate([index_row] * own_rows + [sibling_row], axis=1)

    peak = jnp.full((1, rows), LOWEST, F32)
    for group in range(groups):
        blocks = pl.ds(group * chunk, chunk)
        scores = matmul(piece_ref[blocks, 0:slots, :].reshape(keys, HD), query_t, ((1,), (0,)))
        for i in range(chunk):
            chip = group * chunk + i
            reach = jnp.where(chip < my_chip, 0.0, LOWEST)
            first = piece_ref[chip, slots : 2 * slots, 0:1].astype(F32)
            bias = jnp.where(first > DEAD_LIMIT, LOWEST, reach)
            block = scores[i * slots : (i + 1) * slots, :] + bias
            score_ref[group, i * slots : (i + 1) * slots, :] = block
            peak = jnp.maximum(peak, jnp.max(block, axis=0, keepdims=True))

    own_keys, own_values = pay_ref[0:slots, :], pay_ref[slots : 2 * slots, :]
    own_scores = matmul(own_keys, query_t, ((1,), (0,)))
    own_scores = jnp.where(index_col <= limit_row, own_scores, LOWEST)
    own_scores = own_scores + jnp.where(own_values[:, 0:1].astype(F32) > DEAD_LIMIT, LOWEST, 0.0)
    own_at = pl.ds(pl.multiple_of(lax.rem(my_chip, chunk) * slots, slots), slots)
    score_ref[pl.ds(lax.div(my_chip, chunk), 1), own_at, :] = own_scores[None]
    peak = jnp.maximum(peak, jnp.max(own_scores, axis=0, keepdims=True))

    total = jnp.zeros((1, rows), F32)
    summed = jnp.zeros((HD, rows), F32)
    for group in range(groups):
        weights = jnp.exp2((score_ref[group] - peak) * FACTOR)
        total = total + jnp.sum(weights, axis=0, keepdims=True)
        weights = weights.astype(BF16)
        weight_ref[group] = weights
        values = piece_ref[pl.ds(group * chunk, chunk), slots : 2 * slots, :].reshape(keys, HD)
        summed = summed + matmul(values, weights, ((0,), (0,)))
    part_ref[0:HD, :] = summed
    row_ids = lax.broadcasted_iota(jnp.int32, (8, rows), 0)
    part_ref[HD : HD + 8, :] = jnp.where(row_ids == 0, peak, total)
    part_ref[HD + 8 : HD + 8 + slots, :] = grad_ref[...].astype(F32)


def backward_kernel(
    own_part, sibling_part, own_ref, sibling_ref, grad_ref, weight_ref, piece_ref, att_ref, delta_ref, dq_ref, dq_sibling_ref, out_ref, stage, sems
):
    slots = own_ref.shape[0]
    groups, keys, rows = weight_ref.shape
    chunk = keys // slots
    half = rows // 2
    heads = half // slots

    def swapped(at):
        return jnp.concatenate([sibling_part[at, half:rows], sibling_part[at, 0:half]], axis=1)

    stats = pl.ds(HD, 8)
    mine, theirs = own_part[stats, :], swapped(stats)
    peak = jnp.maximum(mine[0:1], theirs[0:1])
    mine_factor = jnp.exp2((mine[0:1] - peak) * FACTOR)
    their_factor = jnp.exp2((theirs[0:1] - peak) * FACTOR)
    inverse = 1.0 / (mine[1:2] * mine_factor + theirs[1:2] * their_factor)
    body = pl.ds(0, HD)
    mine_factor, their_factor = mine_factor * inverse, their_factor * inverse
    att_t = own_part[body, :] * mine_factor + swapped(body) * their_factor
    att_t = att_t.astype(BF16).astype(F32)
    att = att_t[:, 0:half].T.astype(BF16)
    for h in range(heads):
        att_ref[:, h * HD : (h + 1) * HD] = att[h * slots : (h + 1) * slots, :]

    query_t = jnp.concatenate([stacked_heads(own_ref[...]), stacked_heads(sibling_ref[...])], axis=0).T
    sibling_grad = sibling_part[HD + 8 : HD + 8 + slots, :]
    grad_t = jnp.concatenate([stacked_heads(grad_ref[...]), stacked_heads(sibling_grad)], axis=0).T
    grad_tb = grad_t.astype(BF16)
    delta = jnp.sum(att_t * grad_t, axis=0, keepdims=True)
    delta_ref[...] = jnp.broadcast_to(delta[:, 0:half], delta_ref.shape)

    query_scaled = (query_t * (mine_factor * SCALE)).astype(BF16)
    grad_scaled = (grad_t * mine_factor).astype(BF16)
    dq_t = jnp.zeros((HD, rows), F32)
    copies = []
    for group in range(groups):
        blocks = pl.ds(group * chunk, chunk)
        weights = weight_ref[group]
        values = piece_ref[blocks, slots : 2 * slots, :].reshape(keys, HD)
        grad_probs = matmul(values, grad_tb, ((1,), (0,)))
        grad_score = (weights.astype(F32) * (grad_probs - delta)).astype(BF16)
        key_part = matmul(grad_score, query_scaled, ((1,), (1,)))
        value_part = matmul(weights, grad_scaled, ((1,), (1,)))
        stage[blocks, 0:slots, :] = key_part.astype(BF16).reshape(chunk, slots, HD)
        stage[blocks, slots : 2 * slots, :] = value_part.astype(BF16).reshape(chunk, slots, HD)
        copies.append(pltpu.make_async_copy(stage.at[blocks], out_ref.at[blocks], sems.at[group]))
        copies[-1].start()
        dq_t = dq_t + matmul(piece_ref[blocks, 0:slots, :].reshape(keys, HD), grad_score, ((0,), (0,)))
    dq = (dq_t * (mine_factor * SCALE)).T
    dq_ref[...] = dq[0:half, :]
    dq_sibling_ref[...] = dq[half:rows, :].astype(BF16)
    for copy in copies:
        copy.wait()


def projection_kernel(place_ref, weight_ref, att_ref, delta_ref, *refs):
    part_refs, (held, sems) = refs[:-2], refs[-2:]
    copies = weight_copies(place_ref, weight_ref, held, sems)
    slots = att_ref.shape[0]
    pair, _, width = part_refs[0].shape
    rows = delta_ref.shape[1]
    delta = delta_ref[...]
    row_sum = delta[:, 0:slots]
    for h in range(1, rows // slots):
        row_sum = row_sum + delta[:, h * slots : (h + 1) * slots]
    extra = jnp.concatenate([row_sum, jnp.zeros((8, width - slots), F32)], axis=1)
    extra = jnp.concatenate([extra, extra], axis=0).astype(BF16)
    att = att_ref[...]
    for at, copy in enumerate(copies):
        copy.wait()
        part_ref = part_refs[at // pair]
        part_ref[at % pair, 0:slots, :] = matmul(att, held[at], ((1,), (0,))).astype(BF16)
        part_ref[at % pair, slots : slots + 16, :] = extra


def added_up(stack_ref):
    total = stack_ref[0].astype(F32)
    for step in range(1, stack_ref.shape[0]):
        total = total + stack_ref[step].astype(F32)
    return total


def update_kernel(count_ref, own_ref, landed_ref, logit_ref, index_ref, hidden_ref, update_ref, after_ref, grad_ref):
    slots = update_ref.shape[0]
    tokens = hidden_ref.shape[0]
    live = live_row(count_ref, slots)
    gate = 1.0 / (1.0 + jnp.exp(-logit_ref[...]))
    total = own_ref[0].astype(F32) + landed_ref[0].astype(F32)
    update = (total[0:slots, :] * as_column(jnp.where(live, gate, 0.0))).astype(BF16)
    update_ref[...] = update
    token_ids = lax.broadcasted_iota(jnp.int32, (tokens, slots), 0)
    chosen = jnp.where(token_ids == index_ref[...], 1.0, 0.0).astype(BF16)
    added = matmul(chosen, update, ((1,), (0,)))
    after_ref[...] = (hidden_ref[...].astype(F32) + added).astype(BF16)
    grad_ref[...] = jnp.where(live, total[slots : slots + 1, 0:slots] * (1.0 - gate), 0.0)


def query_grad_kernel(cos_ref, sin_ref, own_ref, arrived_ref, dq_ref):
    slots = dq_ref.shape[0]
    total = own_ref[...] + arrived_ref[...].astype(F32)
    for h in range(dq_ref.shape[1] // HD):
        back = turn(total[h * slots : (h + 1) * slots, :], cos_ref[...], -sin_ref[...])
        dq_ref[:, h * HD : (h + 1) * HD] = back.astype(BF16)


def finish_kernel(cos_ref, sin_ref, landed_ref, dk_ref, dv_ref):
    slots = dk_ref.shape[0]
    total = added_up(landed_ref)
    dk_ref[...] = turn(total[0:slots, :], cos_ref[...], -sin_ref[...]).astype(BF16)
    dv_ref[...] = total[slots : 2 * slots, :].astype(BF16)


def tp_shifts(parts):
    half = parts // 2
    return [shift if 2 * shift <= half else shift - half for shift in range(1, half)]


def tp_order(parts):
    return [shift + step for shift in [0] + tp_shifts(parts) for step in (0, parts // 2)]


def on_device(
    dims,
    tp_count,
    queries,
    key_vectors,
    value_vectors,
    out_weight,
    router_logit,
    chosen_index,
    chosen_count,
    out_cotangent,
    hidden_state,
):
    ny, nx, nc = dims
    slots, width = queries.shape
    heads = width // HD
    rows = nc * heads * slots
    blocks = ny * nx
    chunk = min(8, blocks)

    def exchange(array):
        groups = [[chip * nc + core for chip in range(blocks)] for core in range(nc)]
        return lax.all_to_all(array, "ctx", 0, 0, axis_index_groups=groups, tiled=True)

    def to_sibling(array):
        return lax.ppermute(array, "ctx", [(i, i ^ 1) for i in range(ny * nx * nc)])

    def tp_send(array, shift):
        pairs = []
        for shard in range(ny * nx * nc):
            for part in range(tp_count):
                to = (part + shift * (1 - 2 * (shard % nc))) % tp_count
                pairs.append((shard * tp_count + part, shard * tp_count + to))
        return lax.ppermute(array, ("ctx", "tp"), pairs)

    def summed(first, second):
        return (first.astype(F32) + second.astype(F32)).astype(BF16)

    my_shard = lax.axis_index("ctx").astype(jnp.int32)
    place = jnp.stack([my_shard, lax.axis_index("tp").astype(jnp.int32)])
    index_row = chosen_index[None, :]
    index_rows = jnp.stack([chosen_index // 2, chosen_index % 2]).astype(BF16)
    index_rows = jnp.pad(index_rows, ((0, 14), (0, HD - slots)))
    logit_row = router_logit[None, :]
    half = jnp.arange(HD // 2, dtype=F32)
    frequency = ROTARY_BASE ** (-(half * 2.0 / HD))
    frequency = jnp.concatenate([frequency, frequency])[None, :]

    payload, payloads, cos_full, sin_signed = call(
        payload_kernel,
        [
            jax.ShapeDtypeStruct((2 * slots, HD), BF16),
            jax.ShapeDtypeStruct((blocks, 2 * slots, HD), BF16),
            jax.ShapeDtypeStruct((slots, HD), F32),
            jax.ShapeDtypeStruct((slots, HD), F32),
        ],
        [SMEM] * 2 + [VMEM] * 2,
        [pltpu.VMEM((chunk, 2 * slots, HD), BF16), pltpu.SemaphoreType.DMA((blocks // chunk,))],
        out_specs=[VMEM, HBM, VMEM, VMEM],
    )(
        place,
        chosen_count,
        jnp.concatenate([key_vectors, value_vectors, index_rows], axis=0),
        frequency,
    )
    first_arrival = tp_send(out_cotangent[None], tp_count // 2)
    payloads, first_arrival = lax.optimization_barrier((payloads, first_arrival))
    pieces = exchange(payloads)

    own_queries, gate = call(
        query_kernel,
        [jax.ShapeDtypeStruct((slots, width), BF16), jax.ShapeDtypeStruct((slots, HD), F32)],
        [SMEM] + [VMEM] * 4,
    )(chosen_count, queries, cos_full, sin_signed, logit_row)
    sibling_queries = to_sibling(own_queries)

    held = [
        pltpu.VMEM((tp_count, width, width), BF16),
        pltpu.SemaphoreType.DMA((tp_count,)),
    ]
    pair = jnp.concatenate([out_cotangent[None], first_arrival], axis=0)
    cot = [pair] + [tp_send(pair, shift) for shift in tp_shifts(tp_count)]
    grad_attention = call(
        cotangent_kernel,
        jax.ShapeDtypeStruct((slots, width), BF16),
        [SMEM, HBM] + [VMEM] * (1 + len(cot)),
        held,
        limit=50,
    )(place, out_weight, gate, *cot)

    scored = (blocks // chunk, chunk * slots, rows)
    part, weights = call(
        forward_kernel,
        [
            jax.ShapeDtypeStruct((HD + 8 + slots, rows), F32),
            jax.ShapeDtypeStruct(scored, BF16),
        ],
        [SMEM] + [VMEM] * 6,
        [pltpu.VMEM(scored, F32)],
    )(place, index_row, own_queries, sibling_queries, grad_attention, payload, pieces)
    sibling_part = to_sibling(part)
    attention, delta, dq_own, dq_sibling, outs = call(
        backward_kernel,
        [
            jax.ShapeDtypeStruct((slots, width), BF16),
            jax.ShapeDtypeStruct((8, rows // 2), F32),
            jax.ShapeDtypeStruct((rows // 2, HD), F32),
            jax.ShapeDtypeStruct((rows // 2, HD), BF16),
            jax.ShapeDtypeStruct((blocks, 2 * slots, HD), BF16),
        ],
        [VMEM] * 7,
        [pltpu.VMEM((blocks, 2 * slots, HD), BF16), pltpu.SemaphoreType.DMA((blocks // chunk,))],
        out_specs=[VMEM] * 4 + [HBM],
    )(part, sibling_part, own_queries, sibling_queries, grad_attention, weights, pieces)
    landed = exchange(outs)

    shares = call(
        projection_kernel,
        [jax.ShapeDtypeStruct((2, slots + 16, width), BF16)] * (tp_count // 2),
        [SMEM, HBM] + [VMEM] * 2,
        held,
        limit=50,
    )(place, out_weight, attention, delta)
    dq_arrived = to_sibling(dq_sibling)
    grad_queries = call(
        query_grad_kernel, jax.ShapeDtypeStruct((slots, width), BF16), [VMEM] * 4
    )(cos_full, sin_signed, dq_own, dq_arrived)
    arrived = [tp_send(share, -shift) for share, shift in zip(shares[1:], tp_shifts(tp_count))]
    arrived, grad_queries = lax.optimization_barrier((arrived, grad_queries))
    shares = functools.reduce(jnp.add, [part.astype(F32) for part in [shares[0]] + arrived]).astype(BF16)
    near = shares[:1]
    arrived = tp_send(shares[1:], -(tp_count // 2))

    grad_keys, grad_values = call(
        finish_kernel, [jax.ShapeDtypeStruct((slots, HD), BF16)] * 2, [VMEM] * 3
    )(cos_full, sin_signed, landed)

    update, hidden_after, grad_row = call(
        update_kernel,
        [
            jax.ShapeDtypeStruct((slots, width), BF16),
            jax.ShapeDtypeStruct(hidden_state.shape, BF16),
            jax.ShapeDtypeStruct((1, slots), F32),
        ],
        [SMEM] + [VMEM] * 5,
    )(chosen_count, near, arrived, logit_row, index_row, hidden_state)
    return (update, grad_queries, grad_keys, grad_values, grad_row[0], hidden_after)


def layout(shards):
    nx = 4 if shards >= 16 else 2
    return (shards // (nx * 2), nx, 2)


def solution(mesh):
    shards, tp_count = mesh.shape["ctx"], mesh.shape["tp"]
    placed = (
        P("ctx", "tp"),
        P("ctx", "tp"),
        P("ctx", "tp"),
        P("tp", None),
        P("ctx"),
        P("ctx"),
        P("ctx"),
        P("ctx", "tp"),
        P("ctx", "tp"),
    )
    return jax.shard_map(
        functools.partial(on_device, layout(shards), tp_count),
        mesh=mesh,
        in_specs=placed,
        out_specs=(
            P("ctx", "tp"),
            P("ctx", "tp"),
            P("ctx", "tp"),
            P("ctx", "tp"),
            P("ctx"),
            P("ctx", "tp"),
        ),
        check_vma=False,
    )
```

```python
import functools
import math

import jax
import jax.numpy as jnp
from jax import lax
from jax.experimental import pallas as pl
from jax.experimental.pallas import tpu as pltpu
from jax.sharding import PartitionSpec as P

HD = 128
TOK_DEV = 512
ROTARY_BASE = 500000.0
LOWEST = -1e30
DEAD_MARK = 1024.0
DEAD_LIMIT = 512.0
SCALE = 1.0 / math.sqrt(HD)
FACTOR = SCALE * math.log2(math.e)
F32 = jnp.float32
BF16 = jnp.bfloat16

VMEM = pl.BlockSpec(memory_space=pltpu.VMEM)
SMEM = pl.BlockSpec(memory_space=pltpu.SMEM)
HBM = pl.BlockSpec(memory_space=pltpu.HBM)


def call(kernel, out_shape, in_specs, scratch=(), limit=32, out_specs=None):
    return pl.pallas_call(
        kernel,
        out_shape=out_shape,
        in_specs=in_specs,
        out_specs=out_specs or jax.tree.map(lambda _: VMEM, out_shape),
        scratch_shapes=list(scratch),
        compiler_params=pltpu.CompilerParams(vmem_limit_bytes=limit * 1024 * 1024),
    )


def turn(rows, cos_full, sin_signed):
    return rows * cos_full + pltpu.roll(rows, HD // 2, 1) * sin_signed


def matmul(a, b, dims):
    return lax.dot_general(a, b, (dims, ((), ())), preferred_element_type=F32)


def as_column(row):
    count = row.shape[1]
    down = lax.broadcasted_iota(jnp.int32, (count, count), 0)
    across = lax.broadcasted_iota(jnp.int32, (count, count), 1)
    return jnp.sum(jnp.where(down == across, row, 0.0), axis=1, keepdims=True)


def live_row(count_ref, slots):
    return lax.broadcasted_iota(jnp.int32, (1, slots), 1) < count_ref[0]


def stacked_heads(field):
    heads = field.shape[1] // HD
    return jnp.concatenate([field[:, h * HD : (h + 1) * HD].astype(F32) for h in range(heads)], axis=0)


def payload_kernel(count_ref, pair_ref, position_ref, frequency_ref, pay_ref, copies_ref, cos_ref, sin_ref, stage, sems):
    slots = cos_ref.shape[0]
    angles = as_column(position_ref[...]) * frequency_ref[...]
    col_ids = lax.broadcasted_iota(jnp.int32, (slots, HD), 1)
    row_ids = lax.broadcasted_iota(jnp.int32, (slots, HD), 0)
    cos_full = jnp.cos(angles)
    sin_signed = jnp.where(col_ids < HD // 2, -1.0, 1.0) * jnp.sin(angles)
    cos_ref[...] = cos_full
    sin_ref[...] = sin_signed
    turned = turn(pair_ref[0:slots, :].astype(F32), cos_full, sin_signed).astype(BF16)
    marked = (row_ids >= count_ref[0]) & (col_ids == 0)
    value = jnp.where(marked, DEAD_MARK, pair_ref[slots : 2 * slots, :].astype(F32)).astype(BF16)
    pay_ref[0:slots, :] = turned
    pay_ref[slots : 2 * slots, :] = value
    chunk = stage.shape[0]
    for i in range(chunk):
        stage[i, 0:slots, :] = turned
        stage[i, slots : 2 * slots, :] = value
    copies = [
        pltpu.make_async_copy(stage, copies_ref.at[pl.ds(i * chunk, chunk)], sems.at[i])
        for i in range(copies_ref.shape[0] // chunk)
    ]
    for copy in copies:
        copy.start()
    for copy in copies:
        copy.wait()


def column_block(place_ref, shift, parts, width):
    way = 1 - 2 * lax.rem(place_ref[0], 2)
    owner = lax.rem(place_ref[1] - shift * way + 2 * parts, parts)
    return pl.ds(pl.multiple_of(owner * width, width), width)


def query_kernel(count_ref, query_ref, cos_ref, sin_ref, logit_ref, out_ref, gate_ref):
    cos_full, sin_signed = cos_ref[...], sin_ref[...]
    for h in range(query_ref.shape[1] // HD):
        part = query_ref[:, h * HD : (h + 1) * HD].astype(F32)
        out_ref[:, h * HD : (h + 1) * HD] = turn(part, cos_full, sin_signed).astype(BF16)
    slots = query_ref.shape[0]
    gate = jnp.where(live_row(count_ref, slots), 1.0 / (1.0 + jnp.exp(-logit_ref[...])), 0.0)
    gate_ref[...] = jnp.broadcast_to(as_column(gate), gate_ref.shape)


def weight_copies(place_ref, weight_ref, held, sems):
    parts, _, width = held.shape
    copies = []
    for at, shift in enumerate(tp_order(parts)):
        columns = column_block(place_ref, shift, parts, width)
        copies.append(pltpu.make_async_copy(weight_ref.at[:, columns], held.at[at], sems.at[at]))
    for copy in copies:
        copy.start()
    return copies


def cotangent_kernel(place_ref, weight_ref, gate_ref, pair_ref, *refs):
    pieces, (grad_ref, held, sems) = (pair_ref,) + refs[:-3], refs[-3:]
    copies = weight_copies(place_ref, weight_ref, held, sems)
    total = None
    for at, copy in enumerate(copies):
        copy.wait()
        part = matmul(pieces[at // 2][at % 2], held[at], ((1,), (1,)))
        total = part if total is None else total + part
    grad_ref[...] = (total * gate_ref[:, 0:1]).astype(BF16)


def forward_kernel(place_ref, index_ref, own_ref, sibling_ref, grad_ref, pay_ref, piece_ref, part_ref, weight_ref, score_ref):
    slots = own_ref.shape[0]
    groups, keys, rows = score_ref.shape
    chunk = keys // slots
    me = place_ref[0]
    my_core = lax.rem(me, 2)
    my_chip = lax.div(me, 2)

    query = jnp.concatenate([stacked_heads(own_ref[...]), stacked_heads(sibling_ref[...])], axis=0)
    query_t = query.T.astype(BF16)
    index_row = index_ref[...].astype(F32)
    index_col = as_column(index_row)
    beyond = jnp.where(my_core == 0, 2.0 * TOK_DEV, -1.0)
    sibling_row = jnp.full((1, rows // 2), 1.0, F32) * beyond
    own_rows = rows // 2 // slots
    limit_row = jnp.concatenate([index_row] * own_rows + [sibling_row], axis=1)

    peak = jnp.full((1, rows), LOWEST, F32)
    for group in range(groups):
        blocks = pl.ds(group * chunk, chunk)
        scores = matmul(piece_ref[blocks, 0:slots, :].reshape(keys, HD), query_t, ((1,), (0,)))
        for i in range(chunk):
            chip = i * groups + group
            reach = jnp.where(chip < my_chip, 0.0, LOWEST)
            first = piece_ref[group * chunk + i, slots : 2 * slots, 0:1].astype(F32)
            bias = jnp.where(first > DEAD_LIMIT, LOWEST, reach)
            block = scores[i * slots : (i + 1) * slots, :] + bias
            score_ref[group, i * slots : (i + 1) * slots, :] = block
            peak = jnp.maximum(peak, jnp.max(block, axis=0, keepdims=True))

    own_keys, own_values = pay_ref[0:slots, :], pay_ref[slots : 2 * slots, :]
    own_scores = matmul(own_keys, query_t, ((1,), (0,)))
    own_scores = jnp.where(index_col <= limit_row, own_scores, LOWEST)
    own_scores = own_scores + jnp.where(own_values[:, 0:1].astype(F32) > DEAD_LIMIT, LOWEST, 0.0)
    own_at = pl.ds(pl.multiple_of(lax.div(my_chip, groups) * slots, slots), slots)
    score_ref[pl.ds(lax.rem(my_chip, groups), 1), own_at, :] = own_scores[None]
    peak = jnp.maximum(peak, jnp.max(own_scores, axis=0, keepdims=True))

    total = jnp.zeros((1, rows), F32)
    summed = jnp.zeros((HD, rows), F32)
    for group in range(groups):
        weights = jnp.exp2((score_ref[group] - peak) * FACTOR)
        total = total + jnp.sum(weights, axis=0, keepdims=True)
        weights = weights.astype(BF16)
        weight_ref[group] = weights
        values = piece_ref[pl.ds(group * chunk, chunk), slots : 2 * slots, :].reshape(keys, HD)
        summed = summed + matmul(values, weights, ((0,), (0,)))
    part_ref[0:HD, :] = summed
    row_ids = lax.broadcasted_iota(jnp.int32, (8, rows), 0)
    part_ref[HD : HD + 8, :] = jnp.where(row_ids == 0, peak, total)
    part_ref[HD + 8 : HD + 8 + slots, :] = grad_ref[...].astype(F32)


def backward_kernel(
    own_part, sibling_part, own_ref, sibling_ref, grad_ref, weight_ref, piece_ref, att_ref, delta_ref, dq_ref, dq_sibling_ref, out_ref, stage, sems
):
    slots = own_ref.shape[0]
    groups, keys, rows = weight_ref.shape
    chunk = keys // slots
    half = rows // 2
    heads = half // slots

    def swapped(at):
        return jnp.concatenate([sibling_part[at, half:rows], sibling_part[at, 0:half]], axis=1)

    stats = pl.ds(HD, 8)
    mine, theirs = own_part[stats, :], swapped(stats)
    peak = jnp.maximum(mine[0:1], theirs[0:1])
    mine_factor = jnp.exp2((mine[0:1] - peak) * FACTOR)
    their_factor = jnp.exp2((theirs[0:1] - peak) * FACTOR)
    inverse = 1.0 / (mine[1:2] * mine_factor + theirs[1:2] * their_factor)
    body = pl.ds(0, HD)
    mine_factor, their_factor = mine_factor * inverse, their_factor * inverse
    att_t = own_part[body, :] * mine_factor + swapped(body) * their_factor
    att_t = att_t.astype(BF16).astype(F32)
    att = att_t[:, 0:half].T.astype(BF16)
    for h in range(heads):
        att_ref[:, h * HD : (h + 1) * HD] = att[h * slots : (h + 1) * slots, :]

    query_t = jnp.concatenate([stacked_heads(own_ref[...]), stacked_heads(sibling_ref[...])], axis=0).T
    sibling_grad = sibling_part[HD + 8 : HD + 8 + slots, :]
    grad_t = jnp.concatenate([stacked_heads(grad_ref[...]), stacked_heads(sibling_grad)], axis=0).T
    grad_tb = grad_t.astype(BF16)
    delta = jnp.sum(att_t * grad_t, axis=0, keepdims=True)
    delta_ref[...] = jnp.broadcast_to(delta[:, 0:half], delta_ref.shape)

    query_scaled = (query_t * (mine_factor * SCALE)).astype(BF16)
    grad_scaled = (grad_t * mine_factor).astype(BF16)
    dq_t = jnp.zeros((HD, rows), F32)
    copies = []
    for group in range(groups):
        blocks = pl.ds(group * chunk, chunk)
        weights = weight_ref[group]
        values = piece_ref[blocks, slots : 2 * slots, :].reshape(keys, HD)
        grad_probs = matmul(values, grad_tb, ((1,), (0,)))
        grad_score = (weights.astype(F32) * (grad_probs - delta)).astype(BF16)
        key_part = matmul(grad_score, query_scaled, ((1,), (1,)))
        value_part = matmul(weights, grad_scaled, ((1,), (1,)))
        stage[blocks, 0:slots, :] = key_part.astype(BF16).reshape(chunk, slots, HD)
        stage[blocks, slots : 2 * slots, :] = value_part.astype(BF16).reshape(chunk, slots, HD)
        copies.append(pltpu.make_async_copy(stage.at[blocks], out_ref.at[blocks], sems.at[group]))
        copies[-1].start()
        dq_t = dq_t + matmul(piece_ref[blocks, 0:slots, :].reshape(keys, HD), grad_score, ((0,), (0,)))
    dq = (dq_t * (mine_factor * SCALE)).T
    dq_ref[...] = dq[0:half, :]
    dq_sibling_ref[...] = dq[half:rows, :].astype(BF16)
    for copy in copies:
        copy.wait()


def projection_kernel(place_ref, weight_ref, att_ref, delta_ref, *refs):
    part_refs, (held, sems) = refs[:-2], refs[-2:]
    copies = weight_copies(place_ref, weight_ref, held, sems)
    slots = att_ref.shape[0]
    pair, _, width = part_refs[0].shape
    rows = delta_ref.shape[1]
    delta = delta_ref[...]
    row_sum = delta[:, 0:slots]
    for h in range(1, rows // slots):
        row_sum = row_sum + delta[:, h * slots : (h + 1) * slots]
    extra = jnp.concatenate([row_sum, jnp.zeros((8, width - slots), F32)], axis=1)
    extra = jnp.concatenate([extra, extra], axis=0).astype(BF16)
    att = att_ref[...]
    for at, copy in enumerate(copies):
        copy.wait()
        part_ref = part_refs[at // pair]
        part_ref[at % pair, 0:slots, :] = matmul(att, held[at], ((1,), (0,))).astype(BF16)
        part_ref[at % pair, slots : slots + 16, :] = extra


def added_up(stack_ref):
    total = stack_ref[0].astype(F32)
    for step in range(1, stack_ref.shape[0]):
        total = total + stack_ref[step].astype(F32)
    return total


def sum_kernel(stack_ref, out_ref):
    out_ref[...] = added_up(stack_ref).astype(BF16)


def update_kernel(count_ref, own_ref, landed_ref, logit_ref, index_ref, hidden_ref, update_ref, after_ref, grad_ref):
    slots = update_ref.shape[0]
    tokens = hidden_ref.shape[0]
    live = live_row(count_ref, slots)
    gate = 1.0 / (1.0 + jnp.exp(-logit_ref[...]))
    total = own_ref[0].astype(F32) + landed_ref[0].astype(F32)
    update = (total[0:slots, :] * as_column(jnp.where(live, gate, 0.0))).astype(BF16)
    update_ref[...] = update
    token_ids = lax.broadcasted_iota(jnp.int32, (tokens, slots), 0)
    chosen = jnp.where(token_ids == index_ref[...], 1.0, 0.0).astype(BF16)
    added = matmul(chosen, update, ((1,), (0,)))
    after_ref[...] = (hidden_ref[...].astype(F32) + added).astype(BF16)
    grad_ref[...] = jnp.where(live, total[slots : slots + 1, 0:slots] * (1.0 - gate), 0.0)


def query_grad_kernel(cos_ref, sin_ref, own_ref, arrived_ref, dq_ref):
    slots = dq_ref.shape[0]
    total = own_ref[...] + arrived_ref[...].astype(F32)
    for h in range(dq_ref.shape[1] // HD):
        back = turn(total[h * slots : (h + 1) * slots, :], cos_ref[...], -sin_ref[...])
        dq_ref[:, h * HD : (h + 1) * HD] = back.astype(BF16)


def finish_kernel(cos_ref, sin_ref, landed_ref, dk_ref, dv_ref):
    slots = dk_ref.shape[0]
    total = added_up(landed_ref)
    dk_ref[...] = turn(total[0:slots, :], cos_ref[...], -sin_ref[...]).astype(BF16)
    dv_ref[...] = total[slots : 2 * slots, :].astype(BF16)


def tp_shifts(parts):
    half = parts // 2
    return [shift if 2 * shift <= half else shift - half for shift in range(1, half)]


def tp_order(parts):
    return [shift + step for shift in [0] + tp_shifts(parts) for step in (0, parts // 2)]


def on_device(
    dims,
    tp_count,
    queries,
    key_vectors,
    value_vectors,
    out_weight,
    router_logit,
    chosen_index,
    chosen_count,
    out_cotangent,
    hidden_state,
):
    ny, nx, nc = dims
    slots, width = queries.shape
    heads = width // HD
    rows = nc * heads * slots
    blocks = ny * nx

    def at(y, x, c):
        return (y * nx + x) * nc + c

    y_groups = [[at(y, x, c) for y in range(ny)] for x in range(nx) for c in range(nc)]
    all_groups = [[at(y, x, c) for x in range(nx) for y in range(ny)] for c in range(nc)]
    x_groups = [[at(y, x, c) for x in range(nx)] for y in range(ny) for c in range(nc)]

    def exchange(array, groups):
        return lax.all_to_all(array, "ctx", 0, 0, axis_index_groups=groups, tiled=True)

    def to_sibling(array):
        return lax.ppermute(array, "ctx", [(i, i ^ 1) for i in range(ny * nx * nc)])

    def tp_send(array, shift):
        pairs = []
        for shard in range(ny * nx * nc):
            for part in range(tp_count):
                to = (part + shift * (1 - 2 * (shard % nc))) % tp_count
                pairs.append((shard * tp_count + part, shard * tp_count + to))
        return lax.ppermute(array, ("ctx", "tp"), pairs)

    def summed(first, second):
        return (first.astype(F32) + second.astype(F32)).astype(BF16)

    my_shard = lax.axis_index("ctx").astype(jnp.int32)
    place = jnp.stack([my_shard, lax.axis_index("tp").astype(jnp.int32)])
    index_row = chosen_index[None, :]
    logit_row = router_logit[None, :]
    half = jnp.arange(HD // 2, dtype=F32)
    frequency = ROTARY_BASE ** (-(half * 2.0 / HD))
    frequency = jnp.concatenate([frequency, frequency])[None, :]

    payload, payloads, cos_full, sin_signed = call(
        payload_kernel,
        [
            jax.ShapeDtypeStruct((2 * slots, HD), BF16),
            jax.ShapeDtypeStruct((blocks, 2 * slots, HD), BF16),
            jax.ShapeDtypeStruct((slots, HD), F32),
            jax.ShapeDtypeStruct((slots, HD), F32),
        ],
        [SMEM] + [VMEM] * 3,
        [pltpu.VMEM((ny, 2 * slots, HD), BF16), pltpu.SemaphoreType.DMA((nx,))],
        out_specs=[VMEM, HBM, VMEM, VMEM],
    )(
        chosen_count,
        jnp.concatenate([key_vectors, value_vectors], axis=0),
        (my_shard * TOK_DEV + chosen_index).astype(F32)[None, :],
        frequency,
    )
    first_arrival = tp_send(out_cotangent[None], tp_count // 2)
    pieces = exchange(payloads, all_groups)

    own_queries, gate = call(
        query_kernel,
        [jax.ShapeDtypeStruct((slots, width), BF16), jax.ShapeDtypeStruct((slots, HD), F32)],
        [SMEM] + [VMEM] * 4,
    )(chosen_count, queries, cos_full, sin_signed, logit_row)
    sibling_queries = to_sibling(own_queries)

    held = [
        pltpu.VMEM((tp_count, width, width), BF16),
        pltpu.SemaphoreType.DMA((tp_count,)),
    ]
    pair = jnp.concatenate([out_cotangent[None], first_arrival], axis=0)
    cot = [pair] + [tp_send(pair, shift) for shift in tp_shifts(tp_count)]
    grad_attention = call(
        cotangent_kernel,
        jax.ShapeDtypeStruct((slots, width), BF16),
        [SMEM, HBM] + [VMEM] * (1 + len(cot)),
        held,
        limit=50,
    )(place, out_weight, gate, *cot)

    scored = (nx, ny * slots, rows)
    part, weights = call(
        forward_kernel,
        [
            jax.ShapeDtypeStruct((HD + 8 + slots, rows), F32),
            jax.ShapeDtypeStruct(scored, BF16),
        ],
        [SMEM] + [VMEM] * 6,
        [pltpu.VMEM(scored, F32)],
    )(place, index_row, own_queries, sibling_queries, grad_attention, payload, pieces)
    sibling_part = to_sibling(part)
    attention, delta, dq_own, dq_sibling, outs = call(
        backward_kernel,
        [
            jax.ShapeDtypeStruct((slots, width), BF16),
            jax.ShapeDtypeStruct((8, rows // 2), F32),
            jax.ShapeDtypeStruct((rows // 2, HD), F32),
            jax.ShapeDtypeStruct((rows // 2, HD), BF16),
            jax.ShapeDtypeStruct((blocks, 2 * slots, HD), BF16),
        ],
        [VMEM] * 7,
        [pltpu.VMEM((blocks, 2 * slots, HD), BF16), pltpu.SemaphoreType.DMA((nx,))],
        out_specs=[VMEM] * 4 + [HBM],
    )(part, sibling_part, own_queries, sibling_queries, grad_attention, weights, pieces)
    crossed = exchange(outs.reshape(nx, ny, 2 * slots, HD), x_groups)
    stacked = call(sum_kernel, jax.ShapeDtypeStruct((ny, 2 * slots, HD), BF16), [VMEM])(crossed)
    landed = exchange(stacked, y_groups)

    shares = call(
        projection_kernel,
        [jax.ShapeDtypeStruct((2, slots + 16, width), BF16)] * (tp_count // 2),
        [SMEM, HBM] + [VMEM] * 2,
        held,
        limit=50,
    )(place, out_weight, attention, delta)
    dq_arrived = to_sibling(dq_sibling)
    grad_queries = call(
        query_grad_kernel, jax.ShapeDtypeStruct((slots, width), BF16), [VMEM] * 4
    )(cos_full, sin_signed, dq_own, dq_arrived)
    arrived = [tp_send(share, -shift) for share, shift in zip(shares[1:], tp_shifts(tp_count))]
    shares = functools.reduce(jnp.add, [part.astype(F32) for part in [shares[0]] + arrived]).astype(BF16)
    near, far = shares[:1], shares[1:]
    far, _ = lax.optimization_barrier((far, stacked))
    arrived = tp_send(far, -(tp_count // 2))

    grad_keys, grad_values = call(
        finish_kernel, [jax.ShapeDtypeStruct((slots, HD), BF16)] * 2, [VMEM] * 3
    )(cos_full, sin_signed, landed)

    update, hidden_after, grad_row = call(
        update_kernel,
        [
            jax.ShapeDtypeStruct((slots, width), BF16),
            jax.ShapeDtypeStruct(hidden_state.shape, BF16),
            jax.ShapeDtypeStruct((1, slots), F32),
        ],
        [SMEM] + [VMEM] * 5,
    )(chosen_count, near, arrived, logit_row, index_row, hidden_state)
    return (update, grad_queries, grad_keys, grad_values, grad_row[0], hidden_after)


def layout(shards):
    nx = 4 if shards >= 16 else 2
    return (shards // (nx * 2), nx, 2)


def solution(mesh):
    shards, tp_count = mesh.shape["ctx"], mesh.shape["tp"]
    placed = (
        P("ctx", "tp"),
        P("ctx", "tp"),
        P("ctx", "tp"),
        P("tp", None),
        P("ctx"),
        P("ctx"),
        P("ctx"),
        P("ctx", "tp"),
        P("ctx", "tp"),
    )
    return jax.shard_map(
        functools.partial(on_device, layout(shards), tp_count),
        mesh=mesh,
        in_specs=placed,
        out_specs=(
            P("ctx", "tp"),
            P("ctx", "tp"),
            P("ctx", "tp"),
            P("ctx", "tp"),
            P("ctx"),
            P("ctx", "tp"),
        ),
        check_vma=False,
    )
```

```python
import functools
import math

import jax
import jax.numpy as jnp
from jax import lax
from jax.experimental import pallas as pl
from jax.experimental.pallas import tpu as pltpu
from jax.sharding import PartitionSpec as P

HD = 128
TOK_DEV = 512
ROTARY_BASE = 500000.0
LOWEST = -1e30
DEAD_MARK = 1024.0
DEAD_LIMIT = 512.0
SCALE = 1.0 / math.sqrt(HD)
FACTOR = SCALE * math.log2(math.e)
F32 = jnp.float32
BF16 = jnp.bfloat16

VMEM = pl.BlockSpec(memory_space=pltpu.VMEM)
SMEM = pl.BlockSpec(memory_space=pltpu.SMEM)
HBM = pl.BlockSpec(memory_space=pltpu.HBM)


def call(kernel, out_shape, in_specs, scratch=(), limit=32, out_specs=None):
    return pl.pallas_call(
        kernel,
        out_shape=out_shape,
        in_specs=in_specs,
        out_specs=out_specs or jax.tree.map(lambda _: VMEM, out_shape),
        scratch_shapes=list(scratch),
        compiler_params=pltpu.CompilerParams(vmem_limit_bytes=limit * 1024 * 1024),
    )


def turn(rows, cos_full, sin_signed):
    return rows * cos_full + pltpu.roll(rows, HD // 2, 1) * sin_signed


def matmul(a, b, dims):
    return lax.dot_general(a, b, (dims, ((), ())), preferred_element_type=F32)


def as_column(row):
    count = row.shape[1]
    down = lax.broadcasted_iota(jnp.int32, (count, count), 0)
    across = lax.broadcasted_iota(jnp.int32, (count, count), 1)
    return jnp.sum(jnp.where(down == across, row, 0.0), axis=1, keepdims=True)


def live_row(count_ref, slots):
    return lax.broadcasted_iota(jnp.int32, (1, slots), 1) < count_ref[0]


def stacked_heads(field):
    heads = field.shape[1] // HD
    return jnp.concatenate([field[:, h * HD : (h + 1) * HD].astype(F32) for h in range(heads)], axis=0)


def payload_kernel(count_ref, pair_ref, position_ref, frequency_ref, pay_ref, copies_ref, cos_ref, sin_ref, stage, sems):
    slots = cos_ref.shape[0]
    angles = as_column(position_ref[...]) * frequency_ref[...]
    col_ids = lax.broadcasted_iota(jnp.int32, (slots, HD), 1)
    row_ids = lax.broadcasted_iota(jnp.int32, (slots, HD), 0)
    cos_full = jnp.cos(angles)
    sin_signed = jnp.where(col_ids < HD // 2, -1.0, 1.0) * jnp.sin(angles)
    cos_ref[...] = cos_full
    sin_ref[...] = sin_signed
    turned = turn(pair_ref[0:slots, :].astype(F32), cos_full, sin_signed).astype(BF16)
    marked = (row_ids >= count_ref[0]) & (col_ids == 0)
    value = jnp.where(marked, DEAD_MARK, pair_ref[slots : 2 * slots, :].astype(F32)).astype(BF16)
    pay_ref[0:slots, :] = turned
    pay_ref[slots : 2 * slots, :] = value
    chunk = stage.shape[0]
    for i in range(chunk):
        stage[i, 0:slots, :] = turned
        stage[i, slots : 2 * slots, :] = value
    copies = [
        pltpu.make_async_copy(stage, copies_ref.at[pl.ds(i * chunk, chunk)], sems.at[i])
        for i in range(copies_ref.shape[0] // chunk)
    ]
    for copy in copies:
        copy.start()
    for copy in copies:
        copy.wait()


def column_block(place_ref, step, parts, width):
    owner = lax.bitwise_xor(place_ref[1], jnp.int32(step))
    return pl.ds(pl.multiple_of(owner * width, width), width)


def query_kernel(count_ref, query_ref, cos_ref, sin_ref, logit_ref, out_ref, gate_ref):
    cos_full, sin_signed = cos_ref[...], sin_ref[...]
    for h in range(query_ref.shape[1] // HD):
        part = query_ref[:, h * HD : (h + 1) * HD].astype(F32)
        out_ref[:, h * HD : (h + 1) * HD] = turn(part, cos_full, sin_signed).astype(BF16)
    slots = query_ref.shape[0]
    gate = jnp.where(live_row(count_ref, slots), 1.0 / (1.0 + jnp.exp(-logit_ref[...])), 0.0)
    gate_ref[...] = jnp.broadcast_to(as_column(gate), gate_ref.shape)


def weight_copies(place_ref, weight_ref, held, sems):
    parts, _, width = held.shape
    copies = []
    for at, step in enumerate(tp_order(parts)):
        columns = column_block(place_ref, step, parts, width)
        copies.append(pltpu.make_async_copy(weight_ref.at[:, columns], held.at[at], sems.at[at]))
    for copy in copies:
        copy.start()
    return copies


def cotangent_kernel(place_ref, weight_ref, gate_ref, pair_ref, *refs):
    pieces, (grad_ref, held, sems) = (pair_ref,) + refs[:-3], refs[-3:]
    copies = weight_copies(place_ref, weight_ref, held, sems)
    total = None
    for at, copy in enumerate(copies):
        copy.wait()
        part = matmul(pieces[at // 2][at % 2], held[at], ((1,), (1,)))
        total = part if total is None else total + part
    grad_ref[...] = (total * gate_ref[:, 0:1]).astype(BF16)


def forward_kernel(place_ref, index_ref, own_ref, sibling_ref, grad_ref, pay_ref, piece_ref, part_ref, weight_ref, score_ref):
    slots = own_ref.shape[0]
    groups, keys, rows = score_ref.shape
    chunk = keys // slots
    me = place_ref[0]
    my_core = lax.rem(me, 2)
    my_chip = lax.div(me, 2)

    query = jnp.concatenate([stacked_heads(own_ref[...]), stacked_heads(sibling_ref[...])], axis=0)
    query_t = query.T.astype(BF16)
    index_row = index_ref[...].astype(F32)
    index_col = as_column(index_row)
    beyond = jnp.where(my_core == 0, 2.0 * TOK_DEV, -1.0)
    sibling_row = jnp.full((1, rows // 2), 1.0, F32) * beyond
    own_rows = rows // 2 // slots
    limit_row = jnp.concatenate([index_row] * own_rows + [sibling_row], axis=1)

    peak = jnp.full((1, rows), LOWEST, F32)
    for group in range(groups):
        blocks = pl.ds(group * chunk, chunk)
        scores = matmul(piece_ref[blocks, 0:slots, :].reshape(keys, HD), query_t, ((1,), (0,)))
        for i in range(chunk):
            chip = i * groups + group
            reach = jnp.where(chip < my_chip, 0.0, LOWEST)
            first = piece_ref[group * chunk + i, slots : 2 * slots, 0:1].astype(F32)
            bias = jnp.where(first > DEAD_LIMIT, LOWEST, reach)
            block = scores[i * slots : (i + 1) * slots, :] + bias
            score_ref[group, i * slots : (i + 1) * slots, :] = block
            peak = jnp.maximum(peak, jnp.max(block, axis=0, keepdims=True))

    own_keys, own_values = pay_ref[0:slots, :], pay_ref[slots : 2 * slots, :]
    own_scores = matmul(own_keys, query_t, ((1,), (0,)))
    own_scores = jnp.where(index_col <= limit_row, own_scores, LOWEST)
    own_scores = own_scores + jnp.where(own_values[:, 0:1].astype(F32) > DEAD_LIMIT, LOWEST, 0.0)
    own_at = pl.ds(pl.multiple_of(lax.div(my_chip, groups) * slots, slots), slots)
    score_ref[pl.ds(lax.rem(my_chip, groups), 1), own_at, :] = own_scores[None]
    peak = jnp.maximum(peak, jnp.max(own_scores, axis=0, keepdims=True))

    total = jnp.zeros((1, rows), F32)
    summed = jnp.zeros((HD, rows), F32)
    for group in range(groups):
        weights = jnp.exp2((score_ref[group] - peak) * FACTOR)
        total = total + jnp.sum(weights, axis=0, keepdims=True)
        weights = weights.astype(BF16)
        weight_ref[group] = weights
        values = piece_ref[pl.ds(group * chunk, chunk), slots : 2 * slots, :].reshape(keys, HD)
        summed = summed + matmul(values, weights, ((0,), (0,)))
    part_ref[0:HD, :] = summed
    row_ids = lax.broadcasted_iota(jnp.int32, (8, rows), 0)
    part_ref[HD : HD + 8, :] = jnp.where(row_ids == 0, peak, total)
    part_ref[HD + 8 : HD + 8 + slots, :] = grad_ref[...].astype(F32)


def backward_kernel(
    own_part, sibling_part, own_ref, sibling_ref, grad_ref, weight_ref, piece_ref, att_ref, delta_ref, dq_ref, dq_sibling_ref, out_ref, stage, sems
):
    slots = own_ref.shape[0]
    groups, keys, rows = weight_ref.shape
    chunk = keys // slots
    half = rows // 2
    heads = half // slots

    def swapped(at):
        return jnp.concatenate([sibling_part[at, half:rows], sibling_part[at, 0:half]], axis=1)

    stats = pl.ds(HD, 8)
    mine, theirs = own_part[stats, :], swapped(stats)
    peak = jnp.maximum(mine[0:1], theirs[0:1])
    mine_factor = jnp.exp2((mine[0:1] - peak) * FACTOR)
    their_factor = jnp.exp2((theirs[0:1] - peak) * FACTOR)
    inverse = 1.0 / (mine[1:2] * mine_factor + theirs[1:2] * their_factor)
    body = pl.ds(0, HD)
    mine_factor, their_factor = mine_factor * inverse, their_factor * inverse
    att_t = own_part[body, :] * mine_factor + swapped(body) * their_factor
    att_t = att_t.astype(BF16).astype(F32)
    att = att_t[:, 0:half].T.astype(BF16)
    for h in range(heads):
        att_ref[:, h * HD : (h + 1) * HD] = att[h * slots : (h + 1) * slots, :]

    query_t = jnp.concatenate([stacked_heads(own_ref[...]), stacked_heads(sibling_ref[...])], axis=0).T
    sibling_grad = sibling_part[HD + 8 : HD + 8 + slots, :]
    grad_t = jnp.concatenate([stacked_heads(grad_ref[...]), stacked_heads(sibling_grad)], axis=0).T
    grad_tb = grad_t.astype(BF16)
    delta = jnp.sum(att_t * grad_t, axis=0, keepdims=True)
    delta_ref[...] = jnp.broadcast_to(delta[:, 0:half], delta_ref.shape)

    query_scaled = (query_t * (mine_factor * SCALE)).astype(BF16)
    grad_scaled = (grad_t * mine_factor).astype(BF16)
    dq_t = jnp.zeros((HD, rows), F32)
    copies = []
    for group in range(groups):
        blocks = pl.ds(group * chunk, chunk)
        weights = weight_ref[group]
        values = piece_ref[blocks, slots : 2 * slots, :].reshape(keys, HD)
        grad_probs = matmul(values, grad_tb, ((1,), (0,)))
        grad_score = (weights.astype(F32) * (grad_probs - delta)).astype(BF16)
        key_part = matmul(grad_score, query_scaled, ((1,), (1,)))
        value_part = matmul(weights, grad_scaled, ((1,), (1,)))
        stage[blocks, 0:slots, :] = key_part.astype(BF16).reshape(chunk, slots, HD)
        stage[blocks, slots : 2 * slots, :] = value_part.astype(BF16).reshape(chunk, slots, HD)
        copies.append(pltpu.make_async_copy(stage.at[blocks], out_ref.at[blocks], sems.at[group]))
        copies[-1].start()
        dq_t = dq_t + matmul(piece_ref[blocks, 0:slots, :].reshape(keys, HD), grad_score, ((0,), (0,)))
    dq = (dq_t * (mine_factor * SCALE)).T
    dq_ref[...] = dq[0:half, :]
    dq_sibling_ref[...] = dq[half:rows, :].astype(BF16)
    for copy in copies:
        copy.wait()


def projection_kernel(place_ref, weight_ref, att_ref, delta_ref, *refs):
    part_refs, (held, sems) = refs[:-2], refs[-2:]
    copies = weight_copies(place_ref, weight_ref, held, sems)
    slots = att_ref.shape[0]
    pair, _, width = part_refs[0].shape
    rows = delta_ref.shape[1]
    delta = delta_ref[...]
    row_sum = delta[:, 0:slots]
    for h in range(1, rows // slots):
        row_sum = row_sum + delta[:, h * slots : (h + 1) * slots]
    extra = jnp.concatenate([row_sum, jnp.zeros((8, width - slots), F32)], axis=1)
    extra = jnp.concatenate([extra, extra], axis=0).astype(BF16)
    att = att_ref[...]
    for at, copy in enumerate(copies):
        copy.wait()
        part_ref = part_refs[at // pair]
        part_ref[at % pair, 0:slots, :] = matmul(att, held[at], ((1,), (0,))).astype(BF16)
        part_ref[at % pair, slots : slots + 16, :] = extra


def added_up(stack_ref):
    total = stack_ref[0].astype(F32)
    for step in range(1, stack_ref.shape[0]):
        total = total + stack_ref[step].astype(F32)
    return total


def sum_kernel(stack_ref, out_ref):
    out_ref[...] = added_up(stack_ref).astype(BF16)


def update_kernel(count_ref, own_ref, landed_ref, logit_ref, index_ref, hidden_ref, update_ref, after_ref, grad_ref):
    slots = update_ref.shape[0]
    tokens = hidden_ref.shape[0]
    live = live_row(count_ref, slots)
    gate = 1.0 / (1.0 + jnp.exp(-logit_ref[...]))
    total = own_ref[0].astype(F32) + landed_ref[0].astype(F32)
    update = (total[0:slots, :] * as_column(jnp.where(live, gate, 0.0))).astype(BF16)
    update_ref[...] = update
    token_ids = lax.broadcasted_iota(jnp.int32, (tokens, slots), 0)
    chosen = jnp.where(token_ids == index_ref[...], 1.0, 0.0).astype(BF16)
    added = matmul(chosen, update, ((1,), (0,)))
    after_ref[...] = (hidden_ref[...].astype(F32) + added).astype(BF16)
    grad_ref[...] = jnp.where(live, total[slots : slots + 1, 0:slots] * (1.0 - gate), 0.0)


def query_grad_kernel(cos_ref, sin_ref, own_ref, arrived_ref, dq_ref):
    slots = dq_ref.shape[0]
    total = own_ref[...] + arrived_ref[...].astype(F32)
    for h in range(dq_ref.shape[1] // HD):
        back = turn(total[h * slots : (h + 1) * slots, :], cos_ref[...], -sin_ref[...])
        dq_ref[:, h * HD : (h + 1) * HD] = back.astype(BF16)


def finish_kernel(cos_ref, sin_ref, landed_ref, dk_ref, dv_ref):
    slots = dk_ref.shape[0]
    total = added_up(landed_ref)
    dk_ref[...] = turn(total[0:slots, :], cos_ref[...], -sin_ref[...]).astype(BF16)
    dv_ref[...] = total[slots : 2 * slots, :].astype(BF16)


def tp_steps(parts):
    return list(range(parts // 2 - 1, 0, -1))


def tp_order(parts):
    return [step ^ far for step in [0] + tp_steps(parts) for far in (0, parts // 2)]


def on_device(
    dims,
    tp_count,
    queries,
    key_vectors,
    value_vectors,
    out_weight,
    router_logit,
    chosen_index,
    chosen_count,
    out_cotangent,
    hidden_state,
):
    ny, nx, nc = dims
    slots, width = queries.shape
    heads = width // HD
    rows = nc * heads * slots
    blocks = ny * nx

    def at(y, x, c):
        return (y * nx + x) * nc + c

    y_groups = [[at(y, x, c) for y in range(ny)] for x in range(nx) for c in range(nc)]
    all_groups = [[at(y, x, c) for x in range(nx) for y in range(ny)] for c in range(nc)]
    x_groups = [[at(y, x, c) for x in range(nx)] for y in range(ny) for c in range(nc)]

    def exchange(array, groups):
        return lax.all_to_all(array, "ctx", 0, 0, axis_index_groups=groups, tiled=True)

    def to_sibling(array):
        return lax.ppermute(array, "ctx", [(i, i ^ 1) for i in range(ny * nx * nc)])

    def tp_swap(array, step):
        return lax.ppermute(array, "tp", [(part, part ^ step) for part in range(tp_count)])

    def summed(first, second):
        return (first.astype(F32) + second.astype(F32)).astype(BF16)

    my_shard = lax.axis_index("ctx").astype(jnp.int32)
    place = jnp.stack([my_shard, lax.axis_index("tp").astype(jnp.int32)])
    index_row = chosen_index[None, :]
    logit_row = router_logit[None, :]
    half = jnp.arange(HD // 2, dtype=F32)
    frequency = ROTARY_BASE ** (-(half * 2.0 / HD))
    frequency = jnp.concatenate([frequency, frequency])[None, :]

    payload, payloads, cos_full, sin_signed = call(
        payload_kernel,
        [
            jax.ShapeDtypeStruct((2 * slots, HD), BF16),
            jax.ShapeDtypeStruct((blocks, 2 * slots, HD), BF16),
            jax.ShapeDtypeStruct((slots, HD), F32),
            jax.ShapeDtypeStruct((slots, HD), F32),
        ],
        [SMEM] + [VMEM] * 3,
        [pltpu.VMEM((ny, 2 * slots, HD), BF16), pltpu.SemaphoreType.DMA((nx,))],
        out_specs=[VMEM, HBM, VMEM, VMEM],
    )(
        chosen_count,
        jnp.concatenate([key_vectors, value_vectors], axis=0),
        (my_shard * TOK_DEV + chosen_index).astype(F32)[None, :],
        frequency,
    )
    first_arrival = tp_swap(out_cotangent[None], tp_count // 2)
    pieces = exchange(payloads, all_groups)

    own_queries, gate = call(
        query_kernel,
        [jax.ShapeDtypeStruct((slots, width), BF16), jax.ShapeDtypeStruct((slots, HD), F32)],
        [SMEM] + [VMEM] * 4,
    )(chosen_count, queries, cos_full, sin_signed, logit_row)
    sibling_queries = to_sibling(own_queries)

    held = [
        pltpu.VMEM((tp_count, width, width), BF16),
        pltpu.SemaphoreType.DMA((tp_count,)),
    ]
    pair = jnp.concatenate([out_cotangent[None], first_arrival], axis=0)
    cot = [pair] + [tp_swap(pair, step) for step in tp_steps(tp_count)]
    grad_attention = call(
        cotangent_kernel,
        jax.ShapeDtypeStruct((slots, width), BF16),
        [SMEM, HBM] + [VMEM] * (1 + len(cot)),
        held,
        limit=50,
    )(place, out_weight, gate, *cot)

    scored = (nx, ny * slots, rows)
    part, weights = call(
        forward_kernel,
        [
            jax.ShapeDtypeStruct((HD + 8 + slots, rows), F32),
            jax.ShapeDtypeStruct(scored, BF16),
        ],
        [SMEM] + [VMEM] * 6,
        [pltpu.VMEM(scored, F32)],
    )(place, index_row, own_queries, sibling_queries, grad_attention, payload, pieces)
    sibling_part = to_sibling(part)
    attention, delta, dq_own, dq_sibling, outs = call(
        backward_kernel,
        [
            jax.ShapeDtypeStruct((slots, width), BF16),
            jax.ShapeDtypeStruct((8, rows // 2), F32),
            jax.ShapeDtypeStruct((rows // 2, HD), F32),
            jax.ShapeDtypeStruct((rows // 2, HD), BF16),
            jax.ShapeDtypeStruct((blocks, 2 * slots, HD), BF16),
        ],
        [VMEM] * 7,
        [pltpu.VMEM((blocks, 2 * slots, HD), BF16), pltpu.SemaphoreType.DMA((nx,))],
        out_specs=[VMEM] * 4 + [HBM],
    )(part, sibling_part, own_queries, sibling_queries, grad_attention, weights, pieces)
    crossed = exchange(outs.reshape(nx, ny, 2 * slots, HD), x_groups)
    stacked = call(sum_kernel, jax.ShapeDtypeStruct((ny, 2 * slots, HD), BF16), [VMEM])(crossed)
    landed = exchange(stacked, y_groups)

    shares = call(
        projection_kernel,
        [jax.ShapeDtypeStruct((2, slots + 16, width), BF16)] * (tp_count // 2),
        [SMEM, HBM] + [VMEM] * 2,
        held,
        limit=50,
    )(place, out_weight, attention, delta)
    dq_arrived = to_sibling(dq_sibling)
    grad_queries = call(
        query_grad_kernel, jax.ShapeDtypeStruct((slots, width), BF16), [VMEM] * 4
    )(cos_full, sin_signed, dq_own, dq_arrived)
    arrived = [tp_swap(share, step) for share, step in zip(shares[1:], tp_steps(tp_count))]
    shares = functools.reduce(jnp.add, [part.astype(F32) for part in [shares[0]] + arrived]).astype(BF16)
    near, far = shares[:1], shares[1:]
    far, _ = lax.optimization_barrier((far, stacked))
    arrived = tp_swap(far, tp_count // 2)

    grad_keys, grad_values = call(
        finish_kernel, [jax.ShapeDtypeStruct((slots, HD), BF16)] * 2, [VMEM] * 3
    )(cos_full, sin_signed, landed)

    arrived, grad_keys, grad_values = lax.optimization_barrier((arrived, grad_keys, grad_values))
    update, hidden_after, grad_row = call(
        update_kernel,
        [
            jax.ShapeDtypeStruct((slots, width), BF16),
            jax.ShapeDtypeStruct(hidden_state.shape, BF16),
            jax.ShapeDtypeStruct((1, slots), F32),
        ],
        [SMEM] + [VMEM] * 5,
    )(chosen_count, near, arrived, logit_row, index_row, hidden_state)
    return (update, grad_queries, grad_keys, grad_values, grad_row[0], hidden_after)


def layout(shards):
    nx = 4 if shards >= 16 else 2
    return (shards // (nx * 2), nx, 2)


def solution(mesh):
    shards, tp_count = mesh.shape["ctx"], mesh.shape["tp"]
    placed = (
        P("ctx", "tp"),
        P("ctx", "tp"),
        P("ctx", "tp"),
        P("tp", None),
        P("ctx"),
        P("ctx"),
        P("ctx"),
        P("ctx", "tp"),
        P("ctx", "tp"),
    )
    return jax.shard_map(
        functools.partial(on_device, layout(shards), tp_count),
        mesh=mesh,
        in_specs=placed,
        out_specs=(
            P("ctx", "tp"),
            P("ctx", "tp"),
            P("ctx", "tp"),
            P("ctx", "tp"),
            P("ctx"),
            P("ctx", "tp"),
        ),
        check_vma=False,
    )
```

```python
import functools
import math

import jax
import jax.numpy as jnp
from jax import lax
from jax.experimental import pallas as pl
from jax.experimental.pallas import tpu as pltpu
from jax.sharding import PartitionSpec as P

HD = 128
TOK_DEV = 512
ROTARY_BASE = 500000.0
LOWEST = -1e30
DEAD_MARK = 1024.0
DEAD_LIMIT = 512.0
SCALE = 1.0 / math.sqrt(HD)
FACTOR = SCALE * math.log2(math.e)
F32 = jnp.float32
BF16 = jnp.bfloat16

VMEM = pl.BlockSpec(memory_space=pltpu.VMEM)
SMEM = pl.BlockSpec(memory_space=pltpu.SMEM)
HBM = pl.BlockSpec(memory_space=pltpu.HBM)


def call(kernel, out_shape, in_specs, scratch=(), limit=32, out_specs=None):
    return pl.pallas_call(
        kernel,
        out_shape=out_shape,
        in_specs=in_specs,
        out_specs=out_specs or jax.tree.map(lambda _: VMEM, out_shape),
        scratch_shapes=list(scratch),
        compiler_params=pltpu.CompilerParams(vmem_limit_bytes=limit * 1024 * 1024),
    )


def turn(rows, cos_full, sin_signed):
    return rows * cos_full + pltpu.roll(rows, HD // 2, 1) * sin_signed


def matmul(a, b, dims):
    return lax.dot_general(a, b, (dims, ((), ())), preferred_element_type=F32)


def as_column(row):
    count = row.shape[1]
    down = lax.broadcasted_iota(jnp.int32, (count, count), 0)
    across = lax.broadcasted_iota(jnp.int32, (count, count), 1)
    return jnp.sum(jnp.where(down == across, row, 0.0), axis=1, keepdims=True)


def live_row(count_ref, slots):
    return lax.broadcasted_iota(jnp.int32, (1, slots), 1) < count_ref[0]


def stacked_heads(field):
    heads = field.shape[1] // HD
    return jnp.concatenate([field[:, h * HD : (h + 1) * HD].astype(F32) for h in range(heads)], axis=0)


def payload_kernel(count_ref, pair_ref, position_ref, frequency_ref, pay_ref, copies_ref, cos_ref, sin_ref, stage, sems):
    slots = cos_ref.shape[0]
    angles = as_column(position_ref[...]) * frequency_ref[...]
    col_ids = lax.broadcasted_iota(jnp.int32, (slots, HD), 1)
    row_ids = lax.broadcasted_iota(jnp.int32, (slots, HD), 0)
    cos_full = jnp.cos(angles)
    sin_signed = jnp.where(col_ids < HD // 2, -1.0, 1.0) * jnp.sin(angles)
    cos_ref[...] = cos_full
    sin_ref[...] = sin_signed
    turned = turn(pair_ref[0:slots, :].astype(F32), cos_full, sin_signed).astype(BF16)
    marked = (row_ids >= count_ref[0]) & (col_ids == 0)
    value = jnp.where(marked, DEAD_MARK, pair_ref[slots : 2 * slots, :].astype(F32)).astype(BF16)
    pay_ref[0:slots, :] = turned
    pay_ref[slots : 2 * slots, :] = value
    chunk = stage.shape[0]
    for i in range(chunk):
        stage[i, 0:slots, :] = turned
        stage[i, slots : 2 * slots, :] = value
    copies = [
        pltpu.make_async_copy(stage, copies_ref.at[pl.ds(i * chunk, chunk)], sems.at[i])
        for i in range(copies_ref.shape[0] // chunk)
    ]
    for copy in copies:
        copy.start()
    for copy in copies:
        copy.wait()


def column_block(place_ref, shift, parts, width):
    way = 1 - 2 * lax.rem(place_ref[0], 2)
    owner = lax.rem(place_ref[1] - shift * way + 2 * parts, parts)
    return pl.ds(pl.multiple_of(owner * width, width), width)


def query_kernel(count_ref, query_ref, cos_ref, sin_ref, logit_ref, out_ref, gate_ref):
    cos_full, sin_signed = cos_ref[...], sin_ref[...]
    for h in range(query_ref.shape[1] // HD):
        part = query_ref[:, h * HD : (h + 1) * HD].astype(F32)
        out_ref[:, h * HD : (h + 1) * HD] = turn(part, cos_full, sin_signed).astype(BF16)
    slots = query_ref.shape[0]
    gate = jnp.where(live_row(count_ref, slots), 1.0 / (1.0 + jnp.exp(-logit_ref[...])), 0.0)
    gate_ref[...] = jnp.broadcast_to(as_column(gate), gate_ref.shape)


def weight_copies(place_ref, weight_ref, held, sems):
    parts, _, width = held.shape
    copies = []
    for at, shift in enumerate(tp_order(parts)):
        columns = column_block(place_ref, shift, parts, width)
        copies.append(pltpu.make_async_copy(weight_ref.at[:, columns], held.at[at], sems.at[at]))
    for copy in copies:
        copy.start()
    return copies


def cotangent_kernel(place_ref, weight_ref, gate_ref, pair_ref, *refs):
    pieces, (grad_ref, held, sems) = (pair_ref,) + refs[:-3], refs[-3:]
    copies = weight_copies(place_ref, weight_ref, held, sems)
    total = None
    for at, copy in enumerate(copies):
        copy.wait()
        part = matmul(pieces[at // 2][at % 2], held[at], ((1,), (1,)))
        total = part if total is None else total + part
    grad_ref[...] = (total * gate_ref[:, 0:1]).astype(BF16)


def forward_kernel(place_ref, index_ref, own_ref, sibling_ref, grad_ref, pay_ref, piece_ref, part_ref, weight_ref, score_ref):
    slots = own_ref.shape[0]
    groups, keys, rows = score_ref.shape
    chunk = keys // slots
    me = place_ref[0]
    my_core = lax.rem(me, 2)
    my_chip = lax.div(me, 2)

    query = jnp.concatenate([stacked_heads(own_ref[...]), stacked_heads(sibling_ref[...])], axis=0)
    query_t = query.T.astype(BF16)
    index_row = index_ref[...].astype(F32)
    index_col = as_column(index_row)
    beyond = jnp.where(my_core == 0, 2.0 * TOK_DEV, -1.0)
    sibling_row = jnp.full((1, rows // 2), 1.0, F32) * beyond
    own_rows = rows // 2 // slots
    limit_row = jnp.concatenate([index_row] * own_rows + [sibling_row], axis=1)

    peak = jnp.full((1, rows), LOWEST, F32)
    for group in range(groups):
        blocks = pl.ds(group * chunk, chunk)
        scores = matmul(piece_ref[blocks, 0:slots, :].reshape(keys, HD), query_t, ((1,), (0,)))
        for i in range(chunk):
            chip = i * groups + group
            reach = jnp.where(chip < my_chip, 0.0, LOWEST)
            first = piece_ref[group * chunk + i, slots : 2 * slots, 0:1].astype(F32)
            bias = jnp.where(first > DEAD_LIMIT, LOWEST, reach)
            block = scores[i * slots : (i + 1) * slots, :] + bias
            score_ref[group, i * slots : (i + 1) * slots, :] = block
            peak = jnp.maximum(peak, jnp.max(block, axis=0, keepdims=True))

    own_keys, own_values = pay_ref[0:slots, :], pay_ref[slots : 2 * slots, :]
    own_scores = matmul(own_keys, query_t, ((1,), (0,)))
    own_scores = jnp.where(index_col <= limit_row, own_scores, LOWEST)
    own_scores = own_scores + jnp.where(own_values[:, 0:1].astype(F32) > DEAD_LIMIT, LOWEST, 0.0)
    own_at = pl.ds(pl.multiple_of(lax.div(my_chip, groups) * slots, slots), slots)
    score_ref[pl.ds(lax.rem(my_chip, groups), 1), own_at, :] = own_scores[None]
    peak = jnp.maximum(peak, jnp.max(own_scores, axis=0, keepdims=True))

    total = jnp.zeros((1, rows), F32)
    summed = jnp.zeros((HD, rows), F32)
    for group in range(groups):
        weights = jnp.exp2((score_ref[group] - peak) * FACTOR)
        total = total + jnp.sum(weights, axis=0, keepdims=True)
        weights = weights.astype(BF16)
        weight_ref[group] = weights
        values = piece_ref[pl.ds(group * chunk, chunk), slots : 2 * slots, :].reshape(keys, HD)
        summed = summed + matmul(values, weights, ((0,), (0,)))
    part_ref[0:HD, :] = summed
    row_ids = lax.broadcasted_iota(jnp.int32, (8, rows), 0)
    part_ref[HD : HD + 8, :] = jnp.where(row_ids == 0, peak, total)
    part_ref[HD + 8 : HD + 8 + slots, :] = grad_ref[...].astype(F32)


def backward_kernel(
    own_part, sibling_part, own_ref, sibling_ref, grad_ref, weight_ref, piece_ref, att_ref, delta_ref, dq_ref, dq_sibling_ref, out_ref, stage, sems
):
    slots = own_ref.shape[0]
    groups, keys, rows = weight_ref.shape
    chunk = keys // slots
    half = rows // 2
    heads = half // slots

    def swapped(at):
        return jnp.concatenate([sibling_part[at, half:rows], sibling_part[at, 0:half]], axis=1)

    stats = pl.ds(HD, 8)
    mine, theirs = own_part[stats, :], swapped(stats)
    peak = jnp.maximum(mine[0:1], theirs[0:1])
    mine_factor = jnp.exp2((mine[0:1] - peak) * FACTOR)
    their_factor = jnp.exp2((theirs[0:1] - peak) * FACTOR)
    inverse = 1.0 / (mine[1:2] * mine_factor + theirs[1:2] * their_factor)
    body = pl.ds(0, HD)
    mine_factor, their_factor = mine_factor * inverse, their_factor * inverse
    att_t = own_part[body, :] * mine_factor + swapped(body) * their_factor
    att_t = att_t.astype(BF16).astype(F32)
    att = att_t[:, 0:half].T.astype(BF16)
    for h in range(heads):
        att_ref[:, h * HD : (h + 1) * HD] = att[h * slots : (h + 1) * slots, :]

    query_t = jnp.concatenate([stacked_heads(own_ref[...]), stacked_heads(sibling_ref[...])], axis=0).T
    sibling_grad = sibling_part[HD + 8 : HD + 8 + slots, :]
    grad_t = jnp.concatenate([stacked_heads(grad_ref[...]), stacked_heads(sibling_grad)], axis=0).T
    grad_tb = grad_t.astype(BF16)
    delta = jnp.sum(att_t * grad_t, axis=0, keepdims=True)
    delta_ref[...] = jnp.broadcast_to(delta[:, 0:half], delta_ref.shape)

    query_scaled = (query_t * (mine_factor * SCALE)).astype(BF16)
    grad_scaled = (grad_t * mine_factor).astype(BF16)
    dq_t = jnp.zeros((HD, rows), F32)
    copies = []
    for group in range(groups):
        blocks = pl.ds(group * chunk, chunk)
        weights = weight_ref[group]
        values = piece_ref[blocks, slots : 2 * slots, :].reshape(keys, HD)
        grad_probs = matmul(values, grad_tb, ((1,), (0,)))
        grad_score = (weights.astype(F32) * (grad_probs - delta)).astype(BF16)
        key_part = matmul(grad_score, query_scaled, ((1,), (1,)))
        value_part = matmul(weights, grad_scaled, ((1,), (1,)))
        stage[blocks, 0:slots, :] = key_part.astype(BF16).reshape(chunk, slots, HD)
        stage[blocks, slots : 2 * slots, :] = value_part.astype(BF16).reshape(chunk, slots, HD)
        copies.append(pltpu.make_async_copy(stage.at[blocks], out_ref.at[blocks], sems.at[group]))
        copies[-1].start()
        dq_t = dq_t + matmul(piece_ref[blocks, 0:slots, :].reshape(keys, HD), grad_score, ((0,), (0,)))
    dq = (dq_t * (mine_factor * SCALE)).T
    dq_ref[...] = dq[0:half, :]
    dq_sibling_ref[...] = dq[half:rows, :].astype(BF16)
    for copy in copies:
        copy.wait()


def projection_kernel(place_ref, weight_ref, att_ref, delta_ref, *refs):
    part_refs, (held, sems) = refs[:-2], refs[-2:]
    copies = weight_copies(place_ref, weight_ref, held, sems)
    slots = att_ref.shape[0]
    pair, _, width = part_refs[0].shape
    rows = delta_ref.shape[1]
    delta = delta_ref[...]
    row_sum = delta[:, 0:slots]
    for h in range(1, rows // slots):
        row_sum = row_sum + delta[:, h * slots : (h + 1) * slots]
    extra = jnp.concatenate([row_sum, jnp.zeros((8, width - slots), F32)], axis=1)
    extra = jnp.concatenate([extra, extra], axis=0).astype(BF16)
    att = att_ref[...]
    for at, copy in enumerate(copies):
        copy.wait()
        part_ref = part_refs[at // pair]
        part_ref[at % pair, 0:slots, :] = matmul(att, held[at], ((1,), (0,))).astype(BF16)
        part_ref[at % pair, slots : slots + 16, :] = extra


def added_up(stack_ref):
    total = stack_ref[0].astype(F32)
    for step in range(1, stack_ref.shape[0]):
        total = total + stack_ref[step].astype(F32)
    return total


def sum_kernel(stack_ref, out_ref):
    out_ref[...] = added_up(stack_ref).astype(BF16)


def update_kernel(count_ref, own_ref, landed_ref, logit_ref, index_ref, hidden_ref, update_ref, after_ref, grad_ref):
    slots = update_ref.shape[0]
    tokens = hidden_ref.shape[0]
    live = live_row(count_ref, slots)
    gate = 1.0 / (1.0 + jnp.exp(-logit_ref[...]))
    total = own_ref[0].astype(F32) + landed_ref[0].astype(F32)
    update = (total[0:slots, :] * as_column(jnp.where(live, gate, 0.0))).astype(BF16)
    update_ref[...] = update
    token_ids = lax.broadcasted_iota(jnp.int32, (tokens, slots), 0)
    chosen = jnp.where(token_ids == index_ref[...], 1.0, 0.0).astype(BF16)
    added = matmul(chosen, update, ((1,), (0,)))
    after_ref[...] = (hidden_ref[...].astype(F32) + added).astype(BF16)
    grad_ref[...] = jnp.where(live, total[slots : slots + 1, 0:slots] * (1.0 - gate), 0.0)


def query_grad_kernel(cos_ref, sin_ref, own_ref, arrived_ref, dq_ref):
    slots = dq_ref.shape[0]
    total = own_ref[...] + arrived_ref[...].astype(F32)
    for h in range(dq_ref.shape[1] // HD):
        back = turn(total[h * slots : (h + 1) * slots, :], cos_ref[...], -sin_ref[...])
        dq_ref[:, h * HD : (h + 1) * HD] = back.astype(BF16)


def finish_kernel(cos_ref, sin_ref, landed_ref, dk_ref, dv_ref):
    slots = dk_ref.shape[0]
    total = added_up(landed_ref)
    dk_ref[...] = turn(total[0:slots, :], cos_ref[...], -sin_ref[...]).astype(BF16)
    dv_ref[...] = total[slots : 2 * slots, :].astype(BF16)


def tp_shifts(parts):
    half = parts // 2
    return [shift if 2 * shift <= half else shift - half for shift in range(1, half)]


def tp_order(parts):
    return [shift + step for shift in [0] + tp_shifts(parts) for step in (0, parts // 2)]


def on_device(
    dims,
    tp_count,
    queries,
    key_vectors,
    value_vectors,
    out_weight,
    router_logit,
    chosen_index,
    chosen_count,
    out_cotangent,
    hidden_state,
):
    ny, nx, nc = dims
    slots, width = queries.shape
    heads = width // HD
    rows = nc * heads * slots
    blocks = ny * nx

    def at(y, x, c):
        return (y * nx + x) * nc + c

    y_groups = [[at(y, x, c) for y in range(ny)] for x in range(nx) for c in range(nc)]
    all_groups = [[at(y, x, c) for x in range(nx) for y in range(ny)] for c in range(nc)]
    x_groups = [[at(y, x, c) for x in range(nx)] for y in range(ny) for c in range(nc)]

    def exchange(array, groups):
        return lax.all_to_all(array, "ctx", 0, 0, axis_index_groups=groups, tiled=True)

    def to_sibling(array):
        return lax.ppermute(array, "ctx", [(i, i ^ 1) for i in range(ny * nx * nc)])

    def tp_send(array, shift):
        pairs = []
        for shard in range(ny * nx * nc):
            for part in range(tp_count):
                to = (part + shift * (1 - 2 * (shard % nc))) % tp_count
                pairs.append((shard * tp_count + part, shard * tp_count + to))
        return lax.ppermute(array, ("ctx", "tp"), pairs)

    def summed(first, second):
        return (first.astype(F32) + second.astype(F32)).astype(BF16)

    my_shard = lax.axis_index("ctx").astype(jnp.int32)
    place = jnp.stack([my_shard, lax.axis_index("tp").astype(jnp.int32)])
    index_row = chosen_index[None, :]
    logit_row = router_logit[None, :]
    half = jnp.arange(HD // 2, dtype=F32)
    frequency = ROTARY_BASE ** (-(half * 2.0 / HD))
    frequency = jnp.concatenate([frequency, frequency])[None, :]

    payload, payloads, cos_full, sin_signed = call(
        payload_kernel,
        [
            jax.ShapeDtypeStruct((2 * slots, HD), BF16),
            jax.ShapeDtypeStruct((blocks, 2 * slots, HD), BF16),
            jax.ShapeDtypeStruct((slots, HD), F32),
            jax.ShapeDtypeStruct((slots, HD), F32),
        ],
        [SMEM] + [VMEM] * 3,
        [pltpu.VMEM((ny, 2 * slots, HD), BF16), pltpu.SemaphoreType.DMA((nx,))],
        out_specs=[VMEM, HBM, VMEM, VMEM],
    )(
        chosen_count,
        jnp.concatenate([key_vectors, value_vectors], axis=0),
        (my_shard * TOK_DEV + chosen_index).astype(F32)[None, :],
        frequency,
    )
    first_arrival = tp_send(out_cotangent[None], tp_count // 2)
    pieces = exchange(payloads, all_groups)

    own_queries, gate = call(
        query_kernel,
        [jax.ShapeDtypeStruct((slots, width), BF16), jax.ShapeDtypeStruct((slots, HD), F32)],
        [SMEM] + [VMEM] * 4,
    )(chosen_count, queries, cos_full, sin_signed, logit_row)
    sibling_queries = to_sibling(own_queries)

    held = [
        pltpu.VMEM((tp_count, width, width), BF16),
        pltpu.SemaphoreType.DMA((tp_count,)),
    ]
    pair = jnp.concatenate([out_cotangent[None], first_arrival], axis=0)
    cot = [pair] + [tp_send(pair, shift) for shift in tp_shifts(tp_count)]
    grad_attention = call(
        cotangent_kernel,
        jax.ShapeDtypeStruct((slots, width), BF16),
        [SMEM, HBM] + [VMEM] * (1 + len(cot)),
        held,
        limit=50,
    )(place, out_weight, gate, *cot)

    scored = (nx, ny * slots, rows)
    part, weights = call(
        forward_kernel,
        [
            jax.ShapeDtypeStruct((HD + 8 + slots, rows), F32),
            jax.ShapeDtypeStruct(scored, BF16),
        ],
        [SMEM] + [VMEM] * 6,
        [pltpu.VMEM(scored, F32)],
    )(place, index_row, own_queries, sibling_queries, grad_attention, payload, pieces)
    sibling_part = to_sibling(part)
    attention, delta, dq_own, dq_sibling, outs = call(
        backward_kernel,
        [
            jax.ShapeDtypeStruct((slots, width), BF16),
            jax.ShapeDtypeStruct((8, rows // 2), F32),
            jax.ShapeDtypeStruct((rows // 2, HD), F32),
            jax.ShapeDtypeStruct((rows // 2, HD), BF16),
            jax.ShapeDtypeStruct((blocks, 2 * slots, HD), BF16),
        ],
        [VMEM] * 7,
        [pltpu.VMEM((blocks, 2 * slots, HD), BF16), pltpu.SemaphoreType.DMA((nx,))],
        out_specs=[VMEM] * 4 + [HBM],
    )(part, sibling_part, own_queries, sibling_queries, grad_attention, weights, pieces)
    crossed = exchange(outs.reshape(nx, ny, 2 * slots, HD), x_groups)
    stacked = call(sum_kernel, jax.ShapeDtypeStruct((ny, 2 * slots, HD), BF16), [VMEM])(crossed)
    landed = exchange(stacked, y_groups)

    shares = call(
        projection_kernel,
        [jax.ShapeDtypeStruct((2, slots + 16, width), BF16)] * (tp_count // 2),
        [SMEM, HBM] + [VMEM] * 2,
        held,
        limit=50,
    )(place, out_weight, attention, delta)
    dq_arrived = to_sibling(dq_sibling)
    grad_queries = call(
        query_grad_kernel, jax.ShapeDtypeStruct((slots, width), BF16), [VMEM] * 4
    )(cos_full, sin_signed, dq_own, dq_arrived)
    arrived = [tp_send(share, -shift) for share, shift in zip(shares[1:], tp_shifts(tp_count))]
    shares = functools.reduce(jnp.add, [part.astype(F32) for part in [shares[0]] + arrived]).astype(BF16)
    near, far = shares[:1], shares[1:]
    far, _ = lax.optimization_barrier((far, stacked))
    arrived = tp_send(far, -(tp_count // 2))

    grad_keys, grad_values = call(
        finish_kernel, [jax.ShapeDtypeStruct((slots, HD), BF16)] * 2, [VMEM] * 3
    )(cos_full, sin_signed, landed)

    arrived, grad_keys, grad_values = lax.optimization_barrier((arrived, grad_keys, grad_values))
    update, hidden_after, grad_row = call(
        update_kernel,
        [
            jax.ShapeDtypeStruct((slots, width), BF16),
            jax.ShapeDtypeStruct(hidden_state.shape, BF16),
            jax.ShapeDtypeStruct((1, slots), F32),
        ],
        [SMEM] + [VMEM] * 5,
    )(chosen_count, near, arrived, logit_row, index_row, hidden_state)
    return (update, grad_queries, grad_keys, grad_values, grad_row[0], hidden_after)


def layout(shards):
    nx = 4 if shards >= 16 else 2
    return (shards // (nx * 2), nx, 2)


def solution(mesh):
    shards, tp_count = mesh.shape["ctx"], mesh.shape["tp"]
    placed = (
        P("ctx", "tp"),
        P("ctx", "tp"),
        P("ctx", "tp"),
        P("tp", None),
        P("ctx"),
        P("ctx"),
        P("ctx"),
        P("ctx", "tp"),
        P("ctx", "tp"),
    )
    return jax.shard_map(
        functools.partial(on_device, layout(shards), tp_count),
        mesh=mesh,
        in_specs=placed,
        out_specs=(
            P("ctx", "tp"),
            P("ctx", "tp"),
            P("ctx", "tp"),
            P("ctx", "tp"),
            P("ctx"),
            P("ctx", "tp"),
        ),
        check_vma=False,
    )
```

```python
import functools
import math

import jax
import jax.numpy as jnp
from jax import lax
from jax.experimental import pallas as pl
from jax.experimental.pallas import tpu as pltpu
from jax.sharding import PartitionSpec as P

HD = 128
TOK_DEV = 512
ROTARY_BASE = 500000.0
LOWEST = -1e30
DEAD_MARK = 1024.0
DEAD_LIMIT = 512.0
SCALE = 1.0 / math.sqrt(HD)
FACTOR = SCALE * math.log2(math.e)
F32 = jnp.float32
BF16 = jnp.bfloat16

VMEM = pl.BlockSpec(memory_space=pltpu.VMEM)
SMEM = pl.BlockSpec(memory_space=pltpu.SMEM)
HBM = pl.BlockSpec(memory_space=pltpu.HBM)


def call(kernel, out_shape, in_specs, scratch=(), limit=32, out_specs=None):
    return pl.pallas_call(
        kernel,
        out_shape=out_shape,
        in_specs=in_specs,
        out_specs=out_specs or jax.tree.map(lambda _: VMEM, out_shape),
        scratch_shapes=list(scratch),
        compiler_params=pltpu.CompilerParams(vmem_limit_bytes=limit * 1024 * 1024),
    )


def turn(rows, cos_full, sin_signed):
    return rows * cos_full + pltpu.roll(rows, HD // 2, 1) * sin_signed


def matmul(a, b, dims):
    return lax.dot_general(a, b, (dims, ((), ())), preferred_element_type=F32)


def as_column(row):
    count = row.shape[1]
    down = lax.broadcasted_iota(jnp.int32, (count, count), 0)
    across = lax.broadcasted_iota(jnp.int32, (count, count), 1)
    return jnp.sum(jnp.where(down == across, row, 0.0), axis=1, keepdims=True)


def live_row(count_ref, slots):
    return lax.broadcasted_iota(jnp.int32, (1, slots), 1) < count_ref[0]


def stacked_heads(field):
    heads = field.shape[1] // HD
    return jnp.concatenate([field[:, h * HD : (h + 1) * HD].astype(F32) for h in range(heads)], axis=0)


def payload_kernel(count_ref, pair_ref, position_ref, frequency_ref, pay_ref, copies_ref, cos_ref, sin_ref, stage, sems):
    slots = cos_ref.shape[0]
    angles = as_column(position_ref[...]) * frequency_ref[...]
    col_ids = lax.broadcasted_iota(jnp.int32, (slots, HD), 1)
    row_ids = lax.broadcasted_iota(jnp.int32, (slots, HD), 0)
    cos_full = jnp.cos(angles)
    sin_signed = jnp.where(col_ids < HD // 2, -1.0, 1.0) * jnp.sin(angles)
    cos_ref[...] = cos_full
    sin_ref[...] = sin_signed
    turned = turn(pair_ref[0:slots, :].astype(F32), cos_full, sin_signed).astype(BF16)
    marked = (row_ids >= count_ref[0]) & (col_ids == 0)
    value = jnp.where(marked, DEAD_MARK, pair_ref[slots : 2 * slots, :].astype(F32)).astype(BF16)
    pay_ref[0:slots, :] = turned
    pay_ref[slots : 2 * slots, :] = value
    chunk = stage.shape[0]
    for i in range(chunk):
        stage[i, 0:slots, :] = turned
        stage[i, slots : 2 * slots, :] = value
    copies = [
        pltpu.make_async_copy(stage, copies_ref.at[pl.ds(i * chunk, chunk)], sems.at[i])
        for i in range(copies_ref.shape[0] // chunk)
    ]
    for copy in copies:
        copy.start()
    for copy in copies:
        copy.wait()


def column_block(place_ref, shift, parts, width):
    way = 1 - 2 * lax.rem(place_ref[0], 2)
    owner = lax.rem(place_ref[1] - shift * way + 2 * parts, parts)
    return pl.ds(pl.multiple_of(owner * width, width), width)


def query_kernel(count_ref, query_ref, cos_ref, sin_ref, logit_ref, out_ref, gate_ref):
    cos_full, sin_signed = cos_ref[...], sin_ref[...]
    for h in range(query_ref.shape[1] // HD):
        part = query_ref[:, h * HD : (h + 1) * HD].astype(F32)
        out_ref[:, h * HD : (h + 1) * HD] = turn(part, cos_full, sin_signed).astype(BF16)
    slots = query_ref.shape[0]
    gate = jnp.where(live_row(count_ref, slots), 1.0 / (1.0 + jnp.exp(-logit_ref[...])), 0.0)
    gate_ref[...] = jnp.broadcast_to(as_column(gate), gate_ref.shape)


def weight_copies(place_ref, weight_ref, held, sems):
    parts, _, width = held.shape
    copies = []
    for at, shift in enumerate(tp_order(parts)):
        columns = column_block(place_ref, shift, parts, width)
        copies.append(pltpu.make_async_copy(weight_ref.at[:, columns], held.at[at], sems.at[at]))
    for copy in copies:
        copy.start()
    return copies


def cotangent_kernel(place_ref, weight_ref, gate_ref, pair_ref, *refs):
    pieces, (grad_ref, held, sems) = (pair_ref,) + refs[:-3], refs[-3:]
    copies = weight_copies(place_ref, weight_ref, held, sems)
    total = None
    for at, copy in enumerate(copies):
        copy.wait()
        part = matmul(pieces[at // 2][at % 2], held[at], ((1,), (1,)))
        total = part if total is None else total + part
    grad_ref[...] = (total * gate_ref[:, 0:1]).astype(BF16)


def forward_kernel(place_ref, index_ref, own_ref, sibling_ref, grad_ref, pay_ref, piece_ref, part_ref, weight_ref, score_ref):
    slots = own_ref.shape[0]
    groups, keys, rows = score_ref.shape
    chunk = keys // slots
    me = place_ref[0]
    my_core = lax.rem(me, 2)
    my_chip = lax.div(me, 2)

    query = jnp.concatenate([stacked_heads(own_ref[...]), stacked_heads(sibling_ref[...])], axis=0)
    query_t = query.T.astype(BF16)
    index_row = index_ref[...].astype(F32)
    index_col = as_column(index_row)
    beyond = jnp.where(my_core == 0, 2.0 * TOK_DEV, -1.0)
    sibling_row = jnp.full((1, rows // 2), 1.0, F32) * beyond
    own_rows = rows // 2 // slots
    limit_row = jnp.concatenate([index_row] * own_rows + [sibling_row], axis=1)

    peak = jnp.full((1, rows), LOWEST, F32)
    for group in range(groups):
        blocks = pl.ds(group * chunk, chunk)
        scores = matmul(piece_ref[blocks, 0:slots, :].reshape(keys, HD), query_t, ((1,), (0,)))
        for i in range(chunk):
            chip = i * groups + group
            reach = jnp.where(chip < my_chip, 0.0, LOWEST)
            first = piece_ref[group * chunk + i, slots : 2 * slots, 0:1].astype(F32)
            bias = jnp.where(first > DEAD_LIMIT, LOWEST, reach)
            block = scores[i * slots : (i + 1) * slots, :] + bias
            score_ref[group, i * slots : (i + 1) * slots, :] = block
            peak = jnp.maximum(peak, jnp.max(block, axis=0, keepdims=True))

    own_keys, own_values = pay_ref[0:slots, :], pay_ref[slots : 2 * slots, :]
    own_scores = matmul(own_keys, query_t, ((1,), (0,)))
    own_scores = jnp.where(index_col <= limit_row, own_scores, LOWEST)
    own_scores = own_scores + jnp.where(own_values[:, 0:1].astype(F32) > DEAD_LIMIT, LOWEST, 0.0)
    own_at = pl.ds(pl.multiple_of(lax.div(my_chip, groups) * slots, slots), slots)
    score_ref[pl.ds(lax.rem(my_chip, groups), 1), own_at, :] = own_scores[None]
    peak = jnp.maximum(peak, jnp.max(own_scores, axis=0, keepdims=True))

    total = jnp.zeros((1, rows), F32)
    summed = jnp.zeros((HD, rows), F32)
    for group in range(groups):
        weights = jnp.exp2((score_ref[group] - peak) * FACTOR)
        total = total + jnp.sum(weights, axis=0, keepdims=True)
        weights = weights.astype(BF16)
        weight_ref[group] = weights
        values = piece_ref[pl.ds(group * chunk, chunk), slots : 2 * slots, :].reshape(keys, HD)
        summed = summed + matmul(values, weights, ((0,), (0,)))
    part_ref[0:HD, :] = summed
    row_ids = lax.broadcasted_iota(jnp.int32, (8, rows), 0)
    part_ref[HD : HD + 8, :] = jnp.where(row_ids == 0, peak, total)
    part_ref[HD + 8 : HD + 8 + slots, :] = grad_ref[...].astype(F32)


def backward_kernel(
    own_part, sibling_part, own_ref, sibling_ref, grad_ref, weight_ref, piece_ref, att_ref, delta_ref, dq_ref, dq_sibling_ref, out_ref, stage, sems
):
    slots = own_ref.shape[0]
    groups, keys, rows = weight_ref.shape
    chunk = keys // slots
    half = rows // 2
    heads = half // slots

    def swapped(at):
        return jnp.concatenate([sibling_part[at, half:rows], sibling_part[at, 0:half]], axis=1)

    stats = pl.ds(HD, 8)
    mine, theirs = own_part[stats, :], swapped(stats)
    peak = jnp.maximum(mine[0:1], theirs[0:1])
    mine_factor = jnp.exp2((mine[0:1] - peak) * FACTOR)
    their_factor = jnp.exp2((theirs[0:1] - peak) * FACTOR)
    inverse = 1.0 / (mine[1:2] * mine_factor + theirs[1:2] * their_factor)
    body = pl.ds(0, HD)
    mine_factor, their_factor = mine_factor * inverse, their_factor * inverse
    att_t = own_part[body, :] * mine_factor + swapped(body) * their_factor
    att_t = att_t.astype(BF16).astype(F32)
    att = att_t[:, 0:half].T.astype(BF16)
    for h in range(heads):
        att_ref[:, h * HD : (h + 1) * HD] = att[h * slots : (h + 1) * slots, :]

    query_t = jnp.concatenate([stacked_heads(own_ref[...]), stacked_heads(sibling_ref[...])], axis=0).T
    sibling_grad = sibling_part[HD + 8 : HD + 8 + slots, :]
    grad_t = jnp.concatenate([stacked_heads(grad_ref[...]), stacked_heads(sibling_grad)], axis=0).T
    grad_tb = grad_t.astype(BF16)
    delta = jnp.sum(att_t * grad_t, axis=0, keepdims=True)
    delta_ref[...] = jnp.broadcast_to(delta[:, 0:half], delta_ref.shape)

    query_scaled = (query_t * (mine_factor * SCALE)).astype(BF16)
    grad_scaled = (grad_t * mine_factor).astype(BF16)
    dq_t = jnp.zeros((HD, rows), F32)
    copies = []
    for group in range(groups):
        blocks = pl.ds(group * chunk, chunk)
        weights = weight_ref[group]
        values = piece_ref[blocks, slots : 2 * slots, :].reshape(keys, HD)
        grad_probs = matmul(values, grad_tb, ((1,), (0,)))
        grad_score = (weights.astype(F32) * (grad_probs - delta)).astype(BF16)
        key_part = matmul(grad_score, query_scaled, ((1,), (1,)))
        value_part = matmul(weights, grad_scaled, ((1,), (1,)))
        stage[blocks, 0:slots, :] = key_part.astype(BF16).reshape(chunk, slots, HD)
        stage[blocks, slots : 2 * slots, :] = value_part.astype(BF16).reshape(chunk, slots, HD)
        copies.append(pltpu.make_async_copy(stage.at[blocks], out_ref.at[blocks], sems.at[group]))
        copies[-1].start()
        dq_t = dq_t + matmul(piece_ref[blocks, 0:slots, :].reshape(keys, HD), grad_score, ((0,), (0,)))
    dq = (dq_t * (mine_factor * SCALE)).T
    dq_ref[...] = dq[0:half, :]
    dq_sibling_ref[...] = dq[half:rows, :].astype(BF16)
    for copy in copies:
        copy.wait()


def projection_kernel(place_ref, weight_ref, att_ref, delta_ref, *refs):
    part_refs, (held, sems) = refs[:-2], refs[-2:]
    copies = weight_copies(place_ref, weight_ref, held, sems)
    slots = att_ref.shape[0]
    pair, _, width = part_refs[0].shape
    rows = delta_ref.shape[1]
    delta = delta_ref[...]
    row_sum = delta[:, 0:slots]
    for h in range(1, rows // slots):
        row_sum = row_sum + delta[:, h * slots : (h + 1) * slots]
    extra = jnp.concatenate([row_sum, jnp.zeros((8, width - slots), F32)], axis=1)
    extra = jnp.concatenate([extra, extra], axis=0).astype(BF16)
    att = att_ref[...]
    for at, copy in enumerate(copies):
        copy.wait()
        part_ref = part_refs[at // pair]
        part_ref[at % pair, 0:slots, :] = matmul(att, held[at], ((1,), (0,))).astype(BF16)
        part_ref[at % pair, slots : slots + 16, :] = extra


def added_up(stack_ref):
    total = stack_ref[0].astype(F32)
    for step in range(1, stack_ref.shape[0]):
        total = total + stack_ref[step].astype(F32)
    return total


def sum_kernel(stack_ref, out_ref):
    out_ref[...] = added_up(stack_ref).astype(BF16)


def update_kernel(count_ref, own_ref, landed_ref, logit_ref, index_ref, hidden_ref, update_ref, after_ref, grad_ref):
    slots = update_ref.shape[0]
    tokens = hidden_ref.shape[0]
    live = live_row(count_ref, slots)
    gate = 1.0 / (1.0 + jnp.exp(-logit_ref[...]))
    total = own_ref[0].astype(F32) + landed_ref[0].astype(F32)
    update = (total[0:slots, :] * as_column(jnp.where(live, gate, 0.0))).astype(BF16)
    update_ref[...] = update
    token_ids = lax.broadcasted_iota(jnp.int32, (tokens, slots), 0)
    chosen = jnp.where(token_ids == index_ref[...], 1.0, 0.0).astype(BF16)
    added = matmul(chosen, update, ((1,), (0,)))
    after_ref[...] = (hidden_ref[...].astype(F32) + added).astype(BF16)
    grad_ref[...] = jnp.where(live, total[slots : slots + 1, 0:slots] * (1.0 - gate), 0.0)


def query_grad_kernel(cos_ref, sin_ref, own_ref, arrived_ref, dq_ref):
    slots = dq_ref.shape[0]
    total = own_ref[...] + arrived_ref[...].astype(F32)
    for h in range(dq_ref.shape[1] // HD):
        back = turn(total[h * slots : (h + 1) * slots, :], cos_ref[...], -sin_ref[...])
        dq_ref[:, h * HD : (h + 1) * HD] = back.astype(BF16)


def finish_kernel(cos_ref, sin_ref, landed_ref, dk_ref, dv_ref):
    slots = dk_ref.shape[0]
    total = added_up(landed_ref)
    dk_ref[...] = turn(total[0:slots, :], cos_ref[...], -sin_ref[...]).astype(BF16)
    dv_ref[...] = total[slots : 2 * slots, :].astype(BF16)


def tp_shifts(parts):
    half = parts // 2
    return sorted((shift if 2 * shift <= half else shift - half for shift in range(1, half)), key=abs)


def tp_order(parts):
    return [shift + step for shift in [0] + tp_shifts(parts) for step in (0, parts // 2)]


def on_device(
    dims,
    tp_count,
    queries,
    key_vectors,
    value_vectors,
    out_weight,
    router_logit,
    chosen_index,
    chosen_count,
    out_cotangent,
    hidden_state,
):
    ny, nx, nc = dims
    slots, width = queries.shape
    heads = width // HD
    rows = nc * heads * slots
    blocks = ny * nx

    def at(y, x, c):
        return (y * nx + x) * nc + c

    y_groups = [[at(y, x, c) for y in range(ny)] for x in range(nx) for c in range(nc)]
    all_groups = [[at(y, x, c) for x in range(nx) for y in range(ny)] for c in range(nc)]
    x_groups = [[at(y, x, c) for x in range(nx)] for y in range(ny) for c in range(nc)]

    def exchange(array, groups):
        return lax.all_to_all(array, "ctx", 0, 0, axis_index_groups=groups, tiled=True)

    def to_sibling(array):
        return lax.ppermute(array, "ctx", [(i, i ^ 1) for i in range(ny * nx * nc)])

    def tp_send(array, shift):
        pairs = []
        for shard in range(ny * nx * nc):
            for part in range(tp_count):
                to = (part + shift * (1 - 2 * (shard % nc))) % tp_count
                pairs.append((shard * tp_count + part, shard * tp_count + to))
        return lax.ppermute(array, ("ctx", "tp"), pairs)

    def summed(first, second):
        return (first.astype(F32) + second.astype(F32)).astype(BF16)

    my_shard = lax.axis_index("ctx").astype(jnp.int32)
    place = jnp.stack([my_shard, lax.axis_index("tp").astype(jnp.int32)])
    index_row = chosen_index[None, :]
    logit_row = router_logit[None, :]
    half = jnp.arange(HD // 2, dtype=F32)
    frequency = ROTARY_BASE ** (-(half * 2.0 / HD))
    frequency = jnp.concatenate([frequency, frequency])[None, :]

    payload, payloads, cos_full, sin_signed = call(
        payload_kernel,
        [
            jax.ShapeDtypeStruct((2 * slots, HD), BF16),
            jax.ShapeDtypeStruct((blocks, 2 * slots, HD), BF16),
            jax.ShapeDtypeStruct((slots, HD), F32),
            jax.ShapeDtypeStruct((slots, HD), F32),
        ],
        [SMEM] + [VMEM] * 3,
        [pltpu.VMEM((ny, 2 * slots, HD), BF16), pltpu.SemaphoreType.DMA((nx,))],
        out_specs=[VMEM, HBM, VMEM, VMEM],
    )(
        chosen_count,
        jnp.concatenate([key_vectors, value_vectors], axis=0),
        (my_shard * TOK_DEV + chosen_index).astype(F32)[None, :],
        frequency,
    )
    first_arrival = tp_send(out_cotangent[None], tp_count // 2)
    pieces = exchange(payloads, all_groups)

    own_queries, gate = call(
        query_kernel,
        [jax.ShapeDtypeStruct((slots, width), BF16), jax.ShapeDtypeStruct((slots, HD), F32)],
        [SMEM] + [VMEM] * 4,
    )(chosen_count, queries, cos_full, sin_signed, logit_row)
    sibling_queries = to_sibling(own_queries)

    held = [
        pltpu.VMEM((tp_count, width, width), BF16),
        pltpu.SemaphoreType.DMA((tp_count,)),
    ]
    pair = jnp.concatenate([out_cotangent[None], first_arrival], axis=0)
    cot = [pair] + [tp_send(pair, shift) for shift in tp_shifts(tp_count)]
    grad_attention = call(
        cotangent_kernel,
        jax.ShapeDtypeStruct((slots, width), BF16),
        [SMEM, HBM] + [VMEM] * (1 + len(cot)),
        held,
        limit=50,
    )(place, out_weight, gate, *cot)

    scored = (nx, ny * slots, rows)
    part, weights = call(
        forward_kernel,
        [
            jax.ShapeDtypeStruct((HD + 8 + slots, rows), F32),
            jax.ShapeDtypeStruct(scored, BF16),
        ],
        [SMEM] + [VMEM] * 6,
        [pltpu.VMEM(scored, F32)],
    )(place, index_row, own_queries, sibling_queries, grad_attention, payload, pieces)
    sibling_part = to_sibling(part)
    attention, delta, dq_own, dq_sibling, outs = call(
        backward_kernel,
        [
            jax.ShapeDtypeStruct((slots, width), BF16),
            jax.ShapeDtypeStruct((8, rows // 2), F32),
            jax.ShapeDtypeStruct((rows // 2, HD), F32),
            jax.ShapeDtypeStruct((rows // 2, HD), BF16),
            jax.ShapeDtypeStruct((blocks, 2 * slots, HD), BF16),
        ],
        [VMEM] * 7,
        [pltpu.VMEM((blocks, 2 * slots, HD), BF16), pltpu.SemaphoreType.DMA((nx,))],
        out_specs=[VMEM] * 4 + [HBM],
    )(part, sibling_part, own_queries, sibling_queries, grad_attention, weights, pieces)
    crossed = exchange(outs.reshape(nx, ny, 2 * slots, HD), x_groups)
    stacked = call(sum_kernel, jax.ShapeDtypeStruct((ny, 2 * slots, HD), BF16), [VMEM])(crossed)
    landed = exchange(stacked, y_groups)

    shares = call(
        projection_kernel,
        [jax.ShapeDtypeStruct((2, slots + 16, width), BF16)] * (tp_count // 2),
        [SMEM, HBM] + [VMEM] * 2,
        held,
        limit=50,
    )(place, out_weight, attention, delta)
    dq_arrived = to_sibling(dq_sibling)
    grad_queries = call(
        query_grad_kernel, jax.ShapeDtypeStruct((slots, width), BF16), [VMEM] * 4
    )(cos_full, sin_signed, dq_own, dq_arrived)
    arrived = [tp_send(share, -shift) for share, shift in zip(shares[1:], tp_shifts(tp_count))]
    shares = functools.reduce(jnp.add, [part.astype(F32) for part in [shares[0]] + arrived]).astype(BF16)
    near, far = shares[:1], shares[1:]
    far, _ = lax.optimization_barrier((far, stacked))
    arrived = tp_send(far, -(tp_count // 2))

    grad_keys, grad_values = call(
        finish_kernel, [jax.ShapeDtypeStruct((slots, HD), BF16)] * 2, [VMEM] * 3
    )(cos_full, sin_signed, landed)

    arrived, grad_keys, grad_values = lax.optimization_barrier((arrived, grad_keys, grad_values))
    update, hidden_after, grad_row = call(
        update_kernel,
        [
            jax.ShapeDtypeStruct((slots, width), BF16),
            jax.ShapeDtypeStruct(hidden_state.shape, BF16),
            jax.ShapeDtypeStruct((1, slots), F32),
        ],
        [SMEM] + [VMEM] * 5,
    )(chosen_count, near, arrived, logit_row, index_row, hidden_state)
    return (update, grad_queries, grad_keys, grad_values, grad_row[0], hidden_after)


def layout(shards):
    nx = 4 if shards >= 16 else 2
    return (shards // (nx * 2), nx, 2)


def solution(mesh):
    shards, tp_count = mesh.shape["ctx"], mesh.shape["tp"]
    placed = (
        P("ctx", "tp"),
        P("ctx", "tp"),
        P("ctx", "tp"),
        P("tp", None),
        P("ctx"),
        P("ctx"),
        P("ctx"),
        P("ctx", "tp"),
        P("ctx", "tp"),
    )
    return jax.shard_map(
        functools.partial(on_device, layout(shards), tp_count),
        mesh=mesh,
        in_specs=placed,
        out_specs=(
            P("ctx", "tp"),
            P("ctx", "tp"),
            P("ctx", "tp"),
            P("ctx", "tp"),
            P("ctx"),
            P("ctx", "tp"),
        ),
        check_vma=False,
    )
```
